128 devices in a mesh: exp: 32 (over z, x, core), hid: 4 (over y).
Axes of the slice: x: 4, y: 4, z: 4, core: 2. Of those that a mesh axis runs over, the one named last changes fastest.
Arguments:
- block_input: bfloat16 [32768, 1024], P(('exp', 'hid')), may hold values from -6 to 6
- norm1_gain: float32 [1024], replicated, may hold values from 0.1 to 1.9
- norm1_bias: float32 [1024], replicated, may hold values from -1.5 to 1.5
- w_qkv: bfloat16 [3, 1024, 1024], P(None, None, 'hid'), may hold values from -0.1875 to 0.1875
- w_out: bfloat16 [1024, 1024], P('hid'), may hold values from -1 to 1
- norm2_gain: float32 [1024], replicated, may hold values from 0.1 to 1.9
- norm2_bias: float32 [1024], replicated, may hold values from -1.5 to 1.5
- w_in: bfloat16 [64, 1024, 4096], P('exp', None, 'hid'), may hold values from -0.1875 to 0.1875
- w_down: bfloat16 [64, 4096, 1024], P('exp', 'hid'), may hold values from -0.09375 to 0.09375
- expert_ids: int32 [32768, 1], P(('exp', 'hid')), may hold values from 0 to 63; in each aligned block of 256 rows (0 to 255, 256 to 511, ...) at most 8 rows name the same one
- out_grad: bfloat16 [32768, 1024], P(('exp', 'hid')), may hold values from -6 to 6
Outputs:
- output: bfloat16 [32768, 1024], P(('exp', 'hid'))
- grad_input: float32 [32768, 1024], P(('exp', 'hid'))
- d_norm1_gain: float32 [1024], replicated
- d_norm1_bias: float32 [1024], replicated
- d_w_qkv: float32 [3, 1024, 1024], P(None, None, 'hid')
- d_w_out: float32 [1024, 1024], P('hid')
- d_norm2_gain: float32 [1024], replicated
- d_norm2_bias: float32 [1024], replicated
- d_w_in: float32 [64, 1024, 4096], P('exp', None, 'hid')
- d_w_down: float32 [64, 4096, 1024], P('exp', 'hid')
The draws below stay inside these ranges and needn't reach their ends.
Inputs may be any that keep to these rules, and one draw needn't show every extreme that they name: `expert_ids`: among the 256 rows of one device, at most 8 name the same expert, and in every draw some expert is named by exactly 8 rows of some device.
All inputs are finite; a program needn't handle non-finite values.
Results may differ from the reference program's by a relative error of at most 0.02.
Values may be sent and summed in bfloat16 or wider, within the bound.
A program may use at most 192 MiB of HBM per device.

```python
import math
import jax
import jax.numpy as jnp
import numpy as np
from jax import lax

D = 1024
H = 16
HD = 64
FF = 4096
TOK_DEV = 256
E = 64
CAP = 8
LEN = 1024
TOKENS = 32768
N_EXP = 32
N_HID = 4


def steps_of(rng, dims, pieces, least, largest):
    def one(axis_at, blocks):
        draws = jax.random.uniform(jax.random.fold_in(jax.random.fold_in(rng, 6), axis_at), (blocks,), jnp.float32, least / len(pieces), largest / len(pieces))
        return jnp.repeat(jnp.exp(draws), dims[axis_at] // blocks).reshape((-1,) + (1,) * (len(dims) - axis_at - 1))

    factor_of = one(*pieces[0])
    for cut in pieces[1:]:
        factor_of = factor_of * one(*cut)
    return factor_of


def routed_block(stream_key, own, number, rows, number_of, top, limit, slope):
    order = jax.random.permutation(stream_key, number_of)
    crowded, usual = portions_of(number_of, rows * top, limit, slope, True), portions_of(number_of, rows * top, limit, slope, False)
    places = jnp.arange(number_of)

    def named(sizes, turn):
        used = int((sizes > 0).sum())
        fixed = max(1, used // 4)
        passed = fixed + (places - fixed + turn * (used - fixed)) % max(1, number_of - fixed)
        return jnp.zeros((number_of,), jnp.int32).at[order[jnp.where(places < fixed, places, passed)]].set(jnp.asarray(sizes, jnp.int32))

    sizes = jnp.where(number % 4 == 0, named(crowded, number // 4), named(usual, number - number // 4 - 1))
    mixed = jax.random.permutation(jax.random.fold_in(own, 3), number_of)
    source_of, taker = mixed[0:number_of // 2 * 2:2], mixed[1:number_of // 2 * 2:2]
    room = jnp.minimum(sizes[source_of] - 1, limit - sizes[taker]) // 2
    room = jnp.where((source_of == order[0]) | (taker == order[0]) | (sizes[taker] == 0), 0, jnp.maximum(room, 0))
    passed = jax.random.randint(jax.random.fold_in(own, 4), (number_of // 2,), 0, 1 << 20) % (room + 1)
    sizes = sizes.at[source_of].add(-passed).at[taker].add(passed)
    items = jnp.searchsorted(jnp.cumsum(sizes), jnp.arange(rows * top), side="right").astype(jnp.int32)
    listing = items.reshape(top, rows).T
    listing = listing[jax.random.permutation(jax.random.fold_in(own, 1), rows)]
    turn = jax.random.randint(jax.random.fold_in(own, 2), (rows, 1), 0, top)
    return jnp.take_along_axis(listing, (jnp.arange(top)[None, :] + turn) % top, axis=1)


def portions_of(number_of, total, reach, skew, full):
    portions = [(1 << 20) // math.isqrt(grade ** skew) + 1 for grade in range(1, number_of + 1)]
    largest = reach if full else min(reach, max(-(-total // number_of), total * portions[0] // sum(portions)))
    least = 1 if total - largest >= number_of - 1 else 0
    counts, spare = [largest] + [least] * (number_of - 1), total - largest - least * (number_of - 1)
    while spare > 0:
        free = [i for i in range(1, number_of) if counts[i] < largest] or [i for i in range(1, number_of) if counts[i] < reach]
        pool, remaining = sum([portions[i] for i in free]), spare
        for i in free:
            addition = min(reach - counts[i], max(1, remaining * portions[i] // pool), spare)
            counts[i] = counts[i] + addition
            spare = spare - addition
    return np.array(counts)


def gaussian(rng, extent, spread, limit, pieces=(), held_as=jnp.bfloat16):
    values = spread * jax.random.normal(rng, extent, jnp.float32)
    if pieces:
        values = values * steps_of(rng, extent, pieces, -0.22, 0.18)
    return jnp.clip(values, -limit, limit).astype(held_as)


def setup_inputs(seed: int = 0) -> dict:
    seeds = jax.random.split(jax.random.key(seed), 12)
    block_input = gaussian(seeds[0], (TOKENS, D), 1.0, 6.0, ((0, 128),))
    norm1_gain = jnp.clip(1.0 + 0.18 * jax.random.normal(seeds[1], (D,), jnp.float32), 0.1, 1.9)
    norm1_bias = gaussian(seeds[2], (D,), 0.3, 1.5, (), jnp.float32)
    w_qkv = gaussian(seeds[3], (3, D, H * HD), D ** -0.5, 0.1875, ((2, 4),))
    w_out = gaussian(seeds[4], (H * HD, D), (H * HD // 32) ** -0.5, 1.0, ((0, 4),))
    norm2_gain = jnp.clip(1.0 + 0.18 * jax.random.normal(seeds[5], (D,), jnp.float32), 0.1, 1.9)
    norm2_bias = gaussian(seeds[6], (D,), 0.3, 1.5, (), jnp.float32)
    w_in = gaussian(seeds[7], (E, D, FF), D ** -0.5, 0.1875, ((0, 32), (2, 4)))
    w_down = gaussian(seeds[8], (E, FF, D), FF ** -0.5, 0.09375, ((0, 32), (1, 4)))
    expert_ids_keys = jax.random.split(jax.random.fold_in(seeds[9], 1), TOKENS // TOK_DEV)
    expert_ids_turns = jax.random.permutation(jax.random.fold_in(seeds[9], 3), TOKENS // TOK_DEV)
    expert_ids = jax.vmap(lambda own, number: routed_block(jax.random.fold_in(seeds[9], 2), own, number, TOK_DEV, E, 1, CAP, 2))(expert_ids_keys, expert_ids_turns).reshape((TOKENS, 1))
    out_grad = gaussian(seeds[10], (TOKENS, D), 1.0, 6.0, ((0, 128),))
    return {"block_input": block_input, "norm1_gain": norm1_gain, "norm1_bias": norm1_bias, "w_qkv": w_qkv, "w_out": w_out, "norm2_gain": norm2_gain, "norm2_bias": norm2_bias, "w_in": w_in, "w_down": w_down, "expert_ids": expert_ids, "out_grad": out_grad}


EPSILON = 1e-05
NEG_LARGE = -1e+30
HIGHEST = lax.Precision.HIGHEST

@jax.custom_vjp
def low(v):
    return lax.optimization_barrier(v.astype(jnp.bfloat16)).astype(jnp.float32)

@jax.custom_vjp
def low_back(v):
    return v

def low_keep(v):
    return (low(v), None)

def low_pass(kept, grad):
    return (grad,)

def back_keep(v):
    return (v, None)

def back_low(kept, grad):
    return (low(grad),)
low.defvjp(low_keep, low_pass)
low_back.defvjp(back_keep, back_low)

def layer_norm(vectors, norm_gain, norm_bias):
    row_mean = lax.optimization_barrier(jnp.mean(vectors, -1, keepdims=True))
    centered = vectors - row_mean
    variance = lax.optimization_barrier(jnp.mean(centered * centered, -1, keepdims=True))
    return centered * lax.rsqrt(variance + EPSILON) * norm_gain + norm_bias

def smooth_act(pre_act):
    return jax.nn.gelu(pre_act, approximate=True)

def attend_sequence(query_seq, key_seq, value_seq):
    length_here = query_seq.shape[0]
    scores = low_back(jnp.einsum('qhd,khd->hqk', query_seq, key_seq, precision=HIGHEST) * HD ** (-0.5))
    positions = jnp.arange(length_here, dtype=jnp.int32)
    allowed = positions[None, :] <= positions[:, None]
    scores = jnp.where(allowed[None], scores, NEG_LARGE)
    attn_probs = low(jax.nn.softmax(scores, axis=-1))
    return jnp.einsum('hqk,khd->qhd', attn_probs, value_seq, precision=HIGHEST)

def seq_step(triple):
    return attend_sequence(triple[0], triple[1], triple[2])

def expert_step(triple):
    hidden_pre = low_back(jnp.dot(triple[0], triple[1], precision=HIGHEST))
    activated = low(smooth_act(hidden_pre))
    return low_back(low(jnp.dot(activated, triple[2], precision=HIGHEST)))

def routing(expert_ids):
    picked = expert_ids[:, 0].astype(jnp.int32)
    one_hot = (picked[:, None] == jnp.arange(E, dtype=jnp.int32)[None, :]).astype(jnp.int32)
    position = lax.optimization_barrier(jnp.sum(jnp.cumsum(one_hot, 0) * one_hot, 1)) - 1
    expert_room = N_EXP * N_HID * CAP
    slot_index = (picked * expert_room + position).astype(jnp.int32)
    slot_table = jnp.full((E * expert_room,), TOKENS, jnp.int32)
    slot_table = slot_table.at[slot_index].set(jnp.arange(TOKENS, dtype=jnp.int32))
    return (slot_table.reshape(E, expert_room), slot_index)

def reference(block_input, norm1_gain, norm1_bias, w_qkv, w_out, norm2_gain, norm2_bias, w_in, w_down, expert_ids, out_grad):
    slot_table, slot_index = routing(expert_ids)

    def forward(inputs, gain_one, bias_one, qkv_weight, out_weight, gain_two, bias_two, first_weight, second_weight):
        normed = low(layer_norm(inputs, gain_one, bias_one))
        projected = low_back(low(jnp.einsum('td,idh->ith', normed, qkv_weight, precision=HIGHEST)))
        seq_total = TOKENS // LEN
        stacked = projected.reshape(3, seq_total, LEN, H, HD)
        attn_heads = lax.map(jax.checkpoint(seq_step), (stacked[0], stacked[1], stacked[2]))
        attn_heads = low_back(low(attn_heads.reshape(TOKENS, H * HD)))
        attn_sum = low_back(jnp.dot(attn_heads, out_weight, precision=HIGHEST))
        residual = inputs + attn_sum
        routed = low_back(low(layer_norm(residual, gain_two, bias_two)))
        padded = jnp.concatenate([routed, jnp.zeros((1, D), routed.dtype)], 0)
        expert_rows = jnp.take(padded, slot_table, axis=0)
        results = lax.map(jax.checkpoint(expert_step), (expert_rows, first_weight, second_weight))
        mixed_rows = jnp.take(results.reshape(-1, D), slot_index, axis=0)
        return residual + mixed_rows
    primals = (block_input.astype(jnp.float32), norm1_gain.astype(jnp.float32), norm1_bias.astype(jnp.float32), w_qkv.astype(jnp.float32), w_out.astype(jnp.float32), norm2_gain.astype(jnp.float32), norm2_bias.astype(jnp.float32), w_in.astype(jnp.float32), w_down.astype(jnp.float32))
    result, pullback = jax.vjp(forward, *primals)
    gradients = pullback(out_grad.astype(jnp.float32))
    return (result.astype(jnp.bfloat16), gradients[0], gradients[1], gradients[2], gradients[3], gradients[4], gradients[5], gradients[6], gradients[7], gradients[8])
```

```python
import jax
import jax.numpy as jnp
from jax import lax
from jax.experimental import pallas as pl
from jax.experimental.pallas import tpu as pltpu
from jax.sharding import PartitionSpec as P

HD = 64
EPSILON = 1e-05
NEG_LARGE = -1e30
BF = jnp.bfloat16
F32 = jnp.float32
MESH = pl.DeviceIdType.MESH
ANY = pl.BlockSpec(memory_space=pl.ANY)
VMEM = pl.BlockSpec(memory_space=pltpu.VMEM)
N_HID = 4
N_EXP = 32
ROWS = 256
WIDTH = 1024
SLOTS = 512
MIB = 1 << 20


def dot(a, b):
    return jnp.dot(a, b, preferred_element_type=F32)


def dot_nt(a, b):
    return lax.dot_general(a, b, (((1,), (1,)), ((), ())), preferred_element_type=F32)


def dot_tn(a, b):
    return lax.dot_general(a, b, (((0,), (0,)), ((), ())), preferred_element_type=F32)


def place():
    return lax.axis_index("exp"), lax.axis_index("hid")


def hid_of(h, step):
    return lax.rem(h + step + N_HID, N_HID)


def exp_of(e, dz, dx, dc):
    z, x, c = e // 8, lax.rem(e // 2, 4), lax.rem(e, 2)
    return (lax.rem(z + dz, 4) * 4 + lax.rem(x + dx, 4)) * 2 + lax.rem(c + dc, 2)


def plane_steps(order):
    return [
        (dz, dx, dc)
        for dz in order
        for dx in (0, 1, 3, 2)
        for dc in (0, 1)
        if (dz, dx, dc) != (0, 0, 0)
    ]


def greet(peers):
    barrier = pltpu.get_barrier_semaphore()
    for peer in peers:
        pl.semaphore_signal(barrier, inc=1, device_id=peer, device_id_type=MESH)
    pl.semaphore_wait(barrier, len(peers))


class Links:
    def __init__(self, send_sem, recv_sem):
        self.send_sem, self.recv_sem, self.used = send_sem, recv_sem, 0

    def remote(self, src, dst, peer):
        i = self.used
        self.used += 1
        copy = pltpu.make_async_remote_copy(
            src_ref=src,
            dst_ref=dst,
            send_sem=self.send_sem.at[i],
            recv_sem=self.recv_sem.at[i],
            device_id=peer,
            device_id_type=MESH,
        )
        copy.start()
        return copy

    def local(self, src, dst):
        i = self.used
        self.used += 1
        copy = pltpu.make_async_copy(src, dst, self.send_sem.at[i])
        copy.start()
        return copy


def rows_at(start, size, unit=16):
    return pl.ds(pl.multiple_of(start, unit), size)


def split_experts(block):
    n = block.shape[0] // 16
    wide = block.astype(F32).reshape(n, 2, 8, block.shape[1])
    return [wide[:, i].reshape(n * 8, block.shape[1]).astype(BF) for i in (0, 1)]


def merge_experts(first, second):
    n, width = first.shape[0] // 8, first.shape[1]
    pair = jnp.concatenate(
        [first.reshape(n, 1, 8, width), second.reshape(n, 1, 8, width)], axis=1
    )
    return pair.reshape(n * 16, width).astype(BF)


def norm_parts(rows):
    centered = rows - jnp.mean(rows, -1, keepdims=True)
    scale = lax.rsqrt(jnp.mean(centered * centered, -1, keepdims=True) + EPSILON)
    return centered * scale, scale


def norm_back(grad, hat, scale, gain):
    gh = grad * gain
    inner = jnp.mean(gh * hat, -1, keepdims=True)
    return scale * (gh - jnp.mean(gh, -1, keepdims=True) - hat * inner)


def start_kernel(x_ref, gain_ref, bias_ref, ids_ref, grad_ref, normed_ref, pick_ref, send_ref):
    hat, _ = norm_parts(x_ref[...].astype(F32))
    normed_ref[...] = (hat * gain_ref[...] + bias_ref[...]).astype(BF)
    ids = ids_ref[...]
    named = jnp.where(ids == lax.broadcasted_iota(jnp.int32, (ROWS, 128), 1), 1.0, 0.0)
    earlier = jnp.where(
        lax.broadcasted_iota(jnp.int32, (ROWS, ROWS), 1)
        < lax.broadcasted_iota(jnp.int32, (ROWS, ROWS), 0),
        1.0,
        0.0,
    )
    running = dot(earlier.astype(BF), named.astype(BF))
    position = jnp.sum(running * named, axis=1, keepdims=True).astype(jnp.int32)
    slot = ids * 8 + position
    pick = jnp.where(slot == lax.broadcasted_iota(jnp.int32, (ROWS, SLOTS), 1), 1.0, 0.0).astype(BF)
    pick_ref[...] = pick
    send_ref[...] = dot_tn(pick, grad_ref[...]).astype(BF)


def start_call(block_input, gain, bias, ids, out_grad):
    return pl.pallas_call(
        start_kernel,
        out_shape=(
            jax.ShapeDtypeStruct((ROWS, WIDTH), BF),
            jax.ShapeDtypeStruct((ROWS, SLOTS), BF),
            jax.ShapeDtypeStruct((SLOTS, WIDTH), BF),
        ),
        in_specs=[VMEM] * 5,
        out_specs=[VMEM] * 3,
        compiler_params=pltpu.CompilerParams(vmem_limit_bytes=32 * MIB),
        cost_estimate=pl.CostEstimate(flops=4 * 10**8, bytes_accessed=4 * MIB, transcendentals=0),
        name="start",
    )(block_input, gain, bias, ids, out_grad)


def gather_begin(links, src, out, e, h):
    up, down = (e, hid_of(h, 1)), (e, hid_of(h, -1))
    mine = out.at[rows_at(h * ROWS, ROWS)]
    first = links.remote(src, mine, up)
    second = links.remote(src, mine, down)
    return first, second, links.local(src, mine)


def gather_relay(links, begun, out, e, h):
    up, down = (e, hid_of(h, 1)), (e, hid_of(h, -1))
    half = ROWS // 2
    first, second, own = begun
    first.wait_recv()
    piece = out.at[rows_at(hid_of(h, -1) * ROWS, half)]
    third = links.remote(piece, piece, up)
    second.wait_recv()
    piece = out.at[rows_at(hid_of(h, 1) * ROWS + half, half)]
    fourth = links.remote(piece, piece, down)
    return first, second, third, fourth, own


def gather_end(copies):
    first, second, third, fourth, own = copies
    own.wait()
    third.wait()
    fourth.wait()
    first.wait_send()
    second.wait_send()


def reduce_begin(links, term, got, half_up, half_down, e, h):
    up, down = (e, hid_of(h, 1)), (e, hid_of(h, -1))
    half = ROWS // 2
    far, above, below = hid_of(h, 2) * ROWS, hid_of(h, 1) * ROWS, hid_of(h, -1) * ROWS
    one = links.remote(term.at[rows_at(far, half)], half_up, up)
    two = links.remote(term.at[rows_at(far + half, half)], half_down, down)
    three = links.remote(term.at[rows_at(above + half, half)], got.at[0, pl.ds(half, half)], up)
    four = links.remote(term.at[rows_at(below, half)], got.at[1, pl.ds(0, half)], down)
    return one, two, three, four


def reduce_middle(links, begun, term, got, half_up, half_down, pass_up, pass_down, e, h):
    up, down = (e, hid_of(h, 1)), (e, hid_of(h, -1))
    half = ROWS // 2
    above, below = hid_of(h, 1) * ROWS, hid_of(h, -1) * ROWS
    one, two, three, four = begun
    one.wait_recv()
    pass_up[...] = (
        term[rows_at(above, half), :].astype(F32) + half_up[...].astype(F32)
    ).astype(BF)
    five = links.remote(pass_up, got.at[0, pl.ds(0, half)], up)
    two.wait_recv()
    pass_down[...] = (
        term[rows_at(below + half, half), :].astype(F32) + half_down[...].astype(F32)
    ).astype(BF)
    six = links.remote(pass_down, got.at[1, pl.ds(half, half)], down)
    return one, two, three, four, five, six


def reduce_end(copies, term, got, h):
    for copy in copies[2:]:
        copy.wait_recv()
    return (
        term[rows_at(h * ROWS, ROWS), :].astype(F32)
        + got[0].astype(F32)
        + got[1].astype(F32)
    )


def reduce_scratch():
    half = ROWS // 2
    return [pltpu.VMEM((2, ROWS, WIDTH), BF)] + [pltpu.VMEM((half, WIDTH), BF)] * 4


def sems(count):
    return [pltpu.SemaphoreType.DMA((count,)), pltpu.SemaphoreType.DMA((count,))]


def hid_peers(e, h):
    return [(e, hid_of(h, 1)), (e, hid_of(h, -1))]


def plane_peers(e, h):
    return [(exp_of(e, *step), h) for step in plane_steps((0, 1, 3, 2))]


def first_kernel(normed_ref, send_ref, joined_ref, rows_ref, landed, send_sem, recv_sem):
    e, h = place()
    greet(hid_peers(e, h) + plane_peers(e, h))
    links = Links(send_sem, recv_sem)
    begun = gather_begin(links, normed_ref, joined_ref, e, h)
    own = landed.at[rows_at(e * 16, 16)]
    copies = []
    for step in plane_steps((0, 1, 3, 2)):
        t = exp_of(e, *step)
        copies.append(links.remote(send_ref.at[rows_at(t * 16, 16)], own, (t, h)))
    kept = links.local(send_ref.at[rows_at(e * 16, 16)], own)
    relayed = gather_relay(links, begun, joined_ref, e, h)
    kept.wait()
    for copy in copies:
        copy.wait_recv()
    for i in range(4):
        pair = split_experts(landed[pl.ds(i * 128, 128), :])
        for j in (0, 1):
            rows_ref[j, pl.ds(i * 64, 64), :] = pair[j]
    gather_end(relayed)
    for copy in copies:
        copy.wait_send()


def first_call(normed, send):
    return pl.pallas_call(
        first_kernel,
        out_shape=(
            jax.ShapeDtypeStruct((N_HID * ROWS, WIDTH), BF),
            jax.ShapeDtypeStruct((2, ROWS, WIDTH), BF),
        ),
        in_specs=[VMEM] * 2,
        out_specs=[VMEM] * 2,
        scratch_shapes=[pltpu.VMEM((SLOTS, WIDTH), BF)] + sems(37),
        compiler_params=pltpu.CompilerParams(
            collective_id=1, has_side_effects=True, vmem_limit_bytes=32 * MIB
        ),
        cost_estimate=pl.CostEstimate(flops=0, bytes_accessed=40 * MIB, transcendentals=0),
        name="gather_and_send",
    )(normed, send)


def head_lanes(shape, head):
    return lax.broadcasted_iota(jnp.int32, shape, 1) // HD == head


def causal_tail(scores_t):
    keys, queries = scores_t.shape
    tail = scores_t[keys - queries :]
    allowed = lax.broadcasted_iota(jnp.int32, tail.shape, 0) <= lax.broadcasted_iota(
        jnp.int32, tail.shape, 1
    )
    tail = jnp.where(allowed, tail, NEG_LARGE)
    if keys == queries:
        return tail
    return jnp.concatenate([scores_t[: keys - queries], tail], axis=0)


def forward_kernel(joined_ref, wqkv_ref, wout_ref, q_ref, k_ref, v_ref, heads_ref, logs_ref, term_ref, total):
    rows = joined_ref[...]
    q_ref[...] = dot(rows, wqkv_ref[0]).astype(BF)
    k_ref[...] = dot(rows, wqkv_ref[1]).astype(BF)
    v_ref[...] = dot(rows, wqkv_ref[2]).astype(BF)
    width = q_ref.shape[1]
    logs_ref[...] = jnp.zeros_like(logs_ref)
    for block in range(rows.shape[0] // ROWS):
        keys = (block + 1) * ROWS
        here = pl.ds(block * ROWS, ROWS)
        total[...] = jnp.zeros_like(total)

        def head_step(head, carry, keys=keys, here=here):
            lanes = head_lanes((ROWS, width), head)
            query = jnp.where(lanes, q_ref[here, :] * BF(HD**-0.5), BF(0))
            scores = causal_tail(dot_nt(k_ref[pl.ds(0, keys), :], query))
            top = jnp.max(scores, axis=0, keepdims=True)
            exps = jnp.exp(scores - top)
            summed = jnp.sum(exps, axis=0, keepdims=True)
            logs_ref[pl.ds(head, 1), here] = top + jnp.log(summed)
            probs = (exps * (1.0 / summed)).astype(BF)
            mixed = dot_tn(probs, v_ref[pl.ds(0, keys), :])
            total[...] = jnp.where(lanes, mixed, total[...])
            return carry

        lax.fori_loop(0, width // HD, head_step, 0)
        heads_ref[here, :] = total[...].astype(BF)
    term_ref[...] = dot(heads_ref[...], wout_ref[...]).astype(BF)


def forward_call(joined, w_qkv, w_out):
    rows, width = joined.shape[0], w_qkv.shape[2]
    part = jax.ShapeDtypeStruct((rows, width), BF)
    return pl.pallas_call(
        forward_kernel,
        out_shape=(part, part, part, part, jax.ShapeDtypeStruct((8, rows), F32), jax.ShapeDtypeStruct((rows, WIDTH), BF)),
        in_specs=[VMEM] * 3,
        out_specs=[VMEM] * 6,
        scratch_shapes=[pltpu.VMEM((ROWS, width), F32)],
        compiler_params=pltpu.CompilerParams(vmem_limit_bytes=48 * MIB),
        cost_estimate=pl.CostEstimate(flops=6 * 10**9, bytes_accessed=8 * MIB, transcendentals=4 * 10**6),
        name="attention_forward",
    )(joined, w_qkv, w_out)


def second_kernel(
    term_ref, x_ref, gain_ref, bias_ref, pick_ref,
    residual_ref, rows_ref,
    got, half_up, half_down, pass_up, pass_down, outgoing, landed, staged, send_sem, recv_sem,
):
    e, h = place()
    up, down = (e, hid_of(h, 1)), (e, hid_of(h, -1))
    z = e // 8
    greet(hid_peers(e, h) + plane_peers(e, h))
    links = Links(send_sem, recv_sem)
    begun = reduce_begin(links, term_ref, got, half_up, half_down, e, h)
    reduced = reduce_middle(links, begun, term_ref, got, half_up, half_down, pass_up, pass_down, e, h)
    residual = x_ref[...].astype(F32) + reduce_end(reduced, term_ref, got, h)
    residual_ref[...] = residual
    hat, _ = norm_parts(residual)
    routed = (hat * gain_ref[...] + bias_ref[...]).astype(BF)
    outgoing[...] = dot_tn(pick_ref[...], routed).astype(BF)
    mine = landed.at[rows_at(e * 16, 16)]
    order = (0, 1, 3, 2)
    sent = {}
    for dz in order:
        sent[dz] = []
        for step in plane_steps((dz,)):
            t = exp_of(e, *step)
            sent[dz].append(links.remote(outgoing.at[rows_at(t * 16, 16)], mine, (t, h)))
    kept = links.local(outgoing.at[rows_at(e * 16, 16)], mine)
    waits = []
    pending = None

    def relay(chunk):
        at, first, second = chunk
        first.wait_recv()
        third = links.remote(
            rows_ref.at[0, rows_at(ROWS + at, 64)], rows_ref.at[0, rows_at(3 * ROWS + at, 64)], up
        )
        second.wait_recv()
        fourth = links.remote(
            rows_ref.at[1, rows_at(2 * ROWS + at, 64)], rows_ref.at[1, rows_at(3 * ROWS + at, 64)], down
        )
        waits.extend((third, fourth))

    for dz in order:
        if dz == 0:
            kept.wait()
        for copy in sent[dz]:
            copy.wait_recv()
        from_z = lax.rem(z - dz + 4, 4)
        at = from_z * 64
        pair = split_experts(landed[rows_at(from_z * 128, 128), :])
        for j in (0, 1):
            staged[j, rows_at(at, 64), :] = pair[j]
        piece = staged.at[:, rows_at(at, 64)]
        first = links.remote(piece, rows_ref.at[:, rows_at(ROWS + at, 64)], up)
        second = links.remote(piece, rows_ref.at[:, rows_at(2 * ROWS + at, 64)], down)
        own = links.local(piece, rows_ref.at[:, rows_at(at, 64)])
        if pending is not None:
            relay(pending)
        pending = (at, first, second)
        waits.append(own)
        sent[dz].extend((first, second))
    relay(pending)
    for copy in waits:
        copy.wait()
    for dz in order:
        for copy in sent[dz]:
            copy.wait_send()
    for copy in reduced:
        copy.wait_send()


def second_call(term, block_input, gain, bias, pick):
    return pl.pallas_call(
        second_kernel,
        out_shape=(
            jax.ShapeDtypeStruct((ROWS, WIDTH), F32),
            jax.ShapeDtypeStruct((2, N_HID * ROWS, WIDTH), BF),
        ),
        in_specs=[VMEM] * 5,
        out_specs=[VMEM, ANY],
        scratch_shapes=reduce_scratch()
        + [pltpu.VMEM((SLOTS, WIDTH), BF)] * 2
        + [pltpu.VMEM((2, ROWS, WIDTH), BF)]
        + sems(6 + 32 + 20),
        compiler_params=pltpu.CompilerParams(
            collective_id=2, has_side_effects=True, vmem_limit_bytes=32 * MIB
        ),
        cost_estimate=pl.CostEstimate(flops=0, bytes_accessed=100 * MIB, transcendentals=0),
        name="reduce_norm_send",
    )(term, block_input, gain, bias, pick)


def expert_kernel(x_ref, g0_ref, g1_ref, g2_ref, g3a_ref, g3b_ref, win_ref, wdown_ref, act_ref, gpre_ref, up_ref, grad_ref):
    expert, block = pl.program_id(0), pl.program_id(1)
    for i, ref in enumerate((g0_ref, g1_ref, g2_ref)):

        @pl.when(block == i)
        def _(ref=ref):
            grad_ref[...] = ref[...]

    for i, ref in enumerate((g3a_ref, g3b_ref)):

        @pl.when((block == 3) & (expert == i))
        def _(ref=ref):
            grad_ref[0] = ref[...]

    pre = dot(x_ref[0], win_ref[0])
    grad_act = dot_nt(grad_ref[0], wdown_ref[0])
    root = 0.7978845608028654
    square = pre * pre
    curve = jnp.tanh(root * (pre + 0.044715 * (square * pre)))
    half = 0.5 * (1.0 + curve)
    act_ref[0] = (pre * half).astype(BF)
    slope = half + 0.5 * pre * (1.0 - curve * curve) * (root * (1.0 + 3 * 0.044715 * square))
    grad_pre = (grad_act * slope).astype(BF)
    gpre_ref[0] = grad_pre
    up_ref[0] = dot_nt(grad_pre, win_ref[0]).astype(BF)


def expert_call(rows, grads, w_in, w_down):
    whole = jax.ShapeDtypeStruct(rows.shape, BF)
    part = pl.BlockSpec((1, ROWS, WIDTH), lambda i, j: (i, j, 0))
    fixed = pl.BlockSpec((1, ROWS, WIDTH), lambda i, j: (i, 0, 0))
    weight = pl.BlockSpec((1, WIDTH, WIDTH), lambda i, j: (i, 0, 0))
    flat = pl.BlockSpec((ROWS, WIDTH), lambda i, j: (0, 0))
    return pl.pallas_call(
        expert_kernel,
        grid=(2, N_HID),
        out_shape=(whole,) * 4,
        in_specs=[part, fixed, fixed, fixed, flat, flat, weight, weight],
        out_specs=[part] * 4,
        compiler_params=pltpu.CompilerParams(vmem_limit_bytes=48 * MIB),
        cost_estimate=pl.CostEstimate(flops=13 * 10**9, bytes_accessed=32 * MIB, transcendentals=2 * 10**6),
        name="experts",
    )(rows, *grads, w_in, w_down)


def third_kernel(
    up_ref, pick_ref, residual_ref, grad_ref, gain_ref,
    gres_ref, joined_ref, vec_ref,
    ub, half_up, half_down, pass_up, pass_down, got, outgoing, landed, gradient, send_sem, recv_sem,
):
    e, h = place()
    up, down = (e, hid_of(h, 1)), (e, hid_of(h, -1))
    z = e // 8
    greet(hid_peers(e, h) + plane_peers(e, h))
    links = Links(send_sem, recv_sem)
    order = (2, 1, 3, 0)
    begun = []
    for dz in order:
        at = lax.rem(z + dz, 4) * 64
        piece = rows_at(at, 64)
        far, above, below = (rows_at(k * ROWS + at, 64) for k in (3, 2, 1))
        begun.append((
            at,
            links.remote(up_ref.at[0, far], half_up.at[piece], up),
            links.remote(up_ref.at[1, far], half_down.at[piece], down),
            links.remote(up_ref.at[1, above], got.at[0, 1, piece], up),
            links.remote(up_ref.at[0, below], got.at[1, 0, piece], down),
        ))
    held = links.local(up_ref.at[:, pl.ds(0, 3 * ROWS)], ub)
    held.wait()
    passed = []
    for at, one, two, three, four in begun:
        piece = rows_at(at, 64)
        one.wait_recv()
        pass_up[piece, :] = (
            ub[0, rows_at(2 * ROWS + at, 64), :].astype(F32) + half_up[piece, :].astype(F32)
        ).astype(BF)
        five = links.remote(pass_up.at[piece], got.at[0, 0, piece], up)
        two.wait_recv()
        pass_down[piece, :] = (
            ub[1, rows_at(ROWS + at, 64), :].astype(F32) + half_down[piece, :].astype(F32)
        ).astype(BF)
        six = links.remote(pass_down.at[piece], got.at[1, 1, piece], down)
        passed.append((five, six))
    mine = landed.at[rows_at(e * 16, 16)]
    back = []
    for dz, (at, one, two, three, four), (five, six) in zip(order, begun, passed):
        for copy in (three, four, five, six):
            copy.wait_recv()
        piece = rows_at(at, 64)
        pair = [
            ub[j, piece, :].astype(F32) + got[0, j, piece, :].astype(F32) + got[1, j, piece, :].astype(F32)
            for j in (0, 1)
        ]
        outgoing[rows_at(at * 2, 128), :] = merge_experts(*pair)
        for step in plane_steps((dz,)):
            t = exp_of(e, *step)
            back.append(links.remote(outgoing.at[rows_at(t * 16, 16)], mine, (t, h)))
    kept = links.local(outgoing.at[rows_at(e * 16, 16)], mine)
    kept.wait()
    for copy in back:
        copy.wait_recv()
    routed = dot(pick_ref[...], landed[...])
    hat, scale = norm_parts(residual_ref[...])
    vec_ref[...] = jnp.zeros_like(vec_ref)
    vec_ref[2:3, :] = jnp.sum(routed * hat, axis=0, keepdims=True)
    vec_ref[3:4, :] = jnp.sum(routed, axis=0, keepdims=True)
    gres = grad_ref[...].astype(F32) + norm_back(routed, hat, scale, gain_ref[...])
    gres_ref[...] = gres
    gradient[...] = gres.astype(BF)
    gathered = gather_relay(links, gather_begin(links, gradient, joined_ref, e, h), joined_ref, e, h)
    gather_end(gathered)
    for copy in back:
        copy.wait_send()
    for _, *copies in begun:
        for copy in copies:
            copy.wait_send()
    for pair in passed:
        for copy in pair:
            copy.wait_send()


def third_call(up, pick, residual, out_grad, gain):
    full = pltpu.VMEM((ROWS, WIDTH), BF)
    return pl.pallas_call(
        third_kernel,
        out_shape=(
            jax.ShapeDtypeStruct((ROWS, WIDTH), F32),
            jax.ShapeDtypeStruct((N_HID * ROWS, WIDTH), BF),
            jax.ShapeDtypeStruct((8, WIDTH), F32),
        ),
        in_specs=[ANY] + [VMEM] * 4,
        out_specs=[VMEM] * 3,
        scratch_shapes=[pltpu.VMEM((2, 3 * ROWS, WIDTH), BF)]
        + [full] * 4
        + [pltpu.VMEM((2, 2, ROWS, WIDTH), BF)]
        + [pltpu.VMEM((SLOTS, WIDTH), BF)] * 2
        + [full]
        + sems(16 + 8 + 1 + 32 + 5),
        compiler_params=pltpu.CompilerParams(
            collective_id=3, has_side_effects=True, vmem_limit_bytes=40 * MIB
        ),
        cost_estimate=pl.CostEstimate(flops=0, bytes_accessed=100 * MIB, transcendentals=0),
        name="reduce_back_gather",
    )(up, pick, residual, out_grad, gain)


def backward_kernel(
    grad_ref, wout_ref, wqkv_ref, joined_ref, q_ref, k_ref, v_ref, heads_ref, logs_ref,
    term_ref, dw_ref,
    gheads, gq, gk, gv, dq,
):
    rows, width = q_ref.shape
    gheads[...] = dot_nt(grad_ref[...], wout_ref[...]).astype(BF)
    for i in range(4):
        block = dot_tn(heads_ref[...], grad_ref[:, pl.ds(i * width, width)])
        dw_ref[pl.ds(3 * WIDTH + i * width, width), :] = block.astype(BF)
    gk[...] = jnp.zeros_like(gk)
    gv[...] = jnp.zeros_like(gv)
    for block in range(rows // ROWS):
        keys = (block + 1) * ROWS
        here = pl.ds(block * ROWS, ROWS)
        dq[...] = jnp.zeros_like(dq)

        def head_step(head, carry, keys=keys, here=here):
            lanes = head_lanes((ROWS, width), head)
            query = jnp.where(lanes, q_ref[here, :] * BF(HD**-0.5), BF(0))
            grad = jnp.where(lanes, gheads[here, :], BF(0))
            scores = causal_tail(dot_nt(k_ref[pl.ds(0, keys), :], query))
            probs = jnp.exp(scores - logs_ref[pl.ds(head, 1), here])
            weighted = probs * dot_nt(v_ref[pl.ds(0, keys), :], grad)
            inner = jnp.sum(weighted, axis=0, keepdims=True)
            grad_scores = (weighted - probs * inner).astype(BF)
            gv[pl.ds(0, keys), :] += dot(probs.astype(BF), grad)
            gk[pl.ds(0, keys), :] += dot(grad_scores, query)
            dq[...] = jnp.where(lanes, dot_tn(grad_scores, k_ref[pl.ds(0, keys), :]), dq[...])
            return carry

        lax.fori_loop(0, width // HD, head_step, 0)
        gq[here, :] = (dq[...] * HD**-0.5).astype(BF)
    parts = (gq[...], gk[...].astype(BF), gv[...].astype(BF))
    term_ref[...] = sum(dot_nt(part, wqkv_ref[i]) for i, part in enumerate(parts)).astype(BF)
    for i, part in enumerate(parts):
        dw_ref[pl.ds(i * WIDTH, WIDTH), :] = dot_tn(joined_ref[...], part).astype(BF)


def backward_call(grad, w_out, w_qkv, joined, q, k, v, heads, logs):
    rows, width = q.shape
    return pl.pallas_call(
        backward_kernel,
        out_shape=(
            jax.ShapeDtypeStruct((rows, WIDTH), BF),
            jax.ShapeDtypeStruct((4 * WIDTH, width), BF),
        ),
        in_specs=[VMEM] * 9,
        out_specs=[VMEM] * 2,
        scratch_shapes=[
            pltpu.VMEM((rows, width), BF),
            pltpu.VMEM((rows, width), BF),
            pltpu.VMEM((rows, width), F32),
            pltpu.VMEM((rows, width), F32),
            pltpu.VMEM((ROWS, width), F32),
        ],
        compiler_params=pltpu.CompilerParams(vmem_limit_bytes=52 * MIB),
        cost_estimate=pl.CostEstimate(flops=12 * 10**9, bytes_accessed=12 * MIB, transcendentals=4 * 10**6),
        name="attention_backward",
    )(grad, w_out, w_qkv, joined, q, k, v, heads, logs)


CHIPS = [(dz, dx, 0) for dz in (0, 1, 3, 2) for dx in (0, 1, 3, 2) if (dz, dx) != (0, 0)]


def last_kernel(
    term_ref, gres_ref, x_ref, gain_ref, mixed_ref, pick_ref, residual_ref, dw_ref, vec_ref,
    out_ref, ginput_ref, dwsum_ref, vecsum_ref,
    got, half_up, half_down, pass_up, pass_down, outgoing, landed,
    core_got, halves, pieces, summed, vec, vec_got, send_sem, recv_sem,
):
    e, h = place()
    z, x, c = e // 8, lax.rem(e // 2, 4), lax.rem(e, 2)
    chip = z * 4 + x
    twin = (exp_of(e, 0, 0, 1), h)
    across = [(exp_of(e, *step), h) for step in CHIPS]
    greet(hid_peers(e, h) + [(e, hid_of(h, 2))] + plane_peers(e, h))
    links = Links(send_sem, recv_sem)
    half = 2 * WIDTH
    swap = links.remote(dw_ref.at[rows_at((1 - c) * half, half)], core_got, twin)
    begun = reduce_begin(links, term_ref, got, half_up, half_down, e, h)
    mine = landed.at[rows_at(e * 16, 16)]
    back = []
    for i in range(4):
        pair = [mixed_ref[j, pl.ds(i * 64, 64), :].astype(F32) for j in (0, 1)]
        outgoing[pl.ds(i * 128, 128), :] = merge_experts(*pair)
    for step in plane_steps((2, 1, 3, 0)):
        t = exp_of(e, *step)
        back.append(links.remote(outgoing.at[rows_at(t * 16, 16)], mine, (t, h)))
    kept = links.local(outgoing.at[rows_at(e * 16, 16)], mine)
    swap.wait_recv()
    halves[...] = (
        dw_ref[rows_at(c * half, half), :].astype(F32) + core_got[...].astype(F32)
    ).astype(BF)
    spread = []
    for i, peer in enumerate(across):
        t = peer[0] // 2
        spread.append(links.remote(halves.at[rows_at(t * 128, 128)], pieces.at[i], peer))
    reduced = reduce_middle(links, begun, term_ref, got, half_up, half_down, pass_up, pass_down, e, h)
    grad = reduce_end(reduced, term_ref, got, h)
    hat, scale = norm_parts(x_ref[...].astype(F32))
    ginput_ref[...] = gres_ref[...] + norm_back(grad, hat, scale, gain_ref[...])
    vec[0] = vec_ref[...]
    vec[0, 0:1, :] = jnp.sum(grad * hat, axis=0, keepdims=True)
    vec[0, 1:2, :] = jnp.sum(grad, axis=0, keepdims=True)
    rounds = (
        [(e, hid_of(h, k)) for k in (1, 2, 3)],
        [(exp_of(e, 0, dx, dc), h) for dx in range(4) for dc in (0, 1) if (dx, dc) != (0, 0)],
        [(exp_of(e, dz, 0, 0), h) for dz in (1, 2, 3)],
    )
    small = []
    slot = 0
    copies = [links.remote(vec.at[0], vec_got.at[slot + i], peer) for i, peer in enumerate(rounds[0])]
    for copy in spread:
        copy.wait_recv()
    total = halves[rows_at(chip * 128, 128), :].astype(F32)
    for i in range(len(across)):
        total = total + pieces[i].astype(F32)
    summed[...] = total.astype(BF)
    place_of = dwsum_ref.at[rows_at(c * half + chip * 128, 128)]
    share = [links.remote(summed, place_of, peer) for peer in across]
    share_own = links.local(summed, place_of)
    for number in range(3):
        for copy in copies:
            copy.wait_recv()
        whole = vec[number]
        for i in range(len(rounds[number])):
            whole = whole + vec_got[slot + i]
        slot += len(rounds[number])
        small.extend(copies)
        if number < 2:
            vec[number + 1] = whole
            copies = [
                links.remote(vec.at[number + 1], vec_got.at[slot + i], peer)
                for i, peer in enumerate(rounds[number + 1])
            ]
        else:
            vecsum_ref[...] = whole
    kept.wait()
    for copy in back:
        copy.wait_recv()
    out_ref[...] = (residual_ref[...] + dot(pick_ref[...], landed[...])).astype(BF)
    share_own.wait()
    for copy in share:
        copy.wait_recv()
    both = dwsum_ref.at[rows_at(c * half, half)]
    twins = links.remote(both, both, twin)
    twins.wait()
    swap.wait_send()
    for copy in list(reduced) + back + spread + share + small:
        copy.wait_send()


def last_call(term, gres, block_input, gain, mixed, pick, residual, dw, vec):
    return pl.pallas_call(
        last_kernel,
        out_shape=(
            jax.ShapeDtypeStruct((ROWS, WIDTH), BF),
            jax.ShapeDtypeStruct((ROWS, WIDTH), F32),
            jax.ShapeDtypeStruct(dw.shape, BF),
            jax.ShapeDtypeStruct((8, WIDTH), F32),
        ),
        in_specs=[VMEM] * 9,
        out_specs=[VMEM] * 4,
        scratch_shapes=reduce_scratch()
        + [pltpu.VMEM((SLOTS, WIDTH), BF)] * 2
        + [
            pltpu.VMEM((2 * WIDTH, dw.shape[1]), BF),
            pltpu.VMEM((2 * WIDTH, dw.shape[1]), BF),
            pltpu.VMEM((15, 128, dw.shape[1]), BF),
            pltpu.VMEM((128, dw.shape[1]), BF),
            pltpu.VMEM((3, 8, WIDTH), F32),
            pltpu.VMEM((13, 8, WIDTH), F32),
        ]
        + sems(1 + 6 + 32 + 15 + 16 + 13 + 1),
        compiler_params=pltpu.CompilerParams(
            collective_id=4, has_side_effects=True, vmem_limit_bytes=48 * MIB
        ),
        cost_estimate=pl.CostEstimate(flops=0, bytes_accessed=100 * MIB, transcendentals=0),
        name="last_sums",
    )(term, gres, block_input, gain, mixed, pick, residual, dw, vec)


def hid_shift(rows, step):
    return lax.ppermute(rows, "hid", [(i, (i + step) % N_HID) for i in range(N_HID)])


def added(*terms):
    return sum(term.astype(F32) for term in terms).astype(BF)


def on_device(
    block_input, norm1_gain, norm1_bias, w_qkv, w_out, norm2_gain, norm2_bias,
    w_in, w_down, expert_ids, out_grad,
):
    gain1, bias1, gain2, bias2 = (
        v.reshape(1, WIDTH) for v in (norm1_gain, norm1_bias, norm2_gain, norm2_bias)
    )
    normed, pick, grad_send = start_call(block_input, gain1, bias1, expert_ids, out_grad)
    joined, g0 = first_call(normed, grad_send)
    g1 = hid_shift(g0, 1)
    g2 = hid_shift(g0, -1)
    g3a = hid_shift(g1[0], 1)
    g3b = hid_shift(g2[1], -1)
    q, k, v, heads, logs, term = forward_call(joined, w_qkv, w_out)
    residual, rows = second_call(term, block_input, gain2, bias2, pick)
    act, grad_pre, up, grads = expert_call(rows, (g0, g1, g2, g3a, g3b), w_in, w_down)
    gres, grad_joined, vec = third_call(up, pick, residual, out_grad, gain2)
    down = jnp.einsum("lrf,lfd->lrd", act, w_down, preferred_element_type=F32).astype(BF)
    blocks = [[down[j, i * ROWS : (i + 1) * ROWS] for i in range(4)] for j in (0, 1)]
    far_up = hid_shift(blocks[0][3], 1)
    far_down = hid_shift(blocks[1][3], -1)
    up1 = hid_shift(blocks[1][2], 1)
    down0 = hid_shift(blocks[0][1], -1)
    up0 = hid_shift(added(blocks[0][2], far_up), 1)
    down1 = hid_shift(added(blocks[1][1], far_down), -1)
    mixed = jnp.stack(
        [added(blocks[0][0], up0, down0), added(blocks[1][0], up1, down1)]
    )
    d_w_in = jnp.einsum("lrd,lrf->ldf", rows, grad_pre, preferred_element_type=F32)
    d_w_down = jnp.einsum("lrf,lrd->lfd", act, grads, preferred_element_type=F32)
    back_term, dw = backward_call(grad_joined, w_out, w_qkv, joined, q, k, v, heads, logs)
    output, grad_input, dw_sum, vec_sum = last_call(
        back_term, gres, block_input, gain1, mixed, pick, residual, dw, vec
    )
    width = w_qkv.shape[2]
    d_w_qkv = dw_sum[: 3 * WIDTH].reshape(3, WIDTH, width).astype(F32)
    d_w_out = (
        dw_sum[3 * WIDTH :].reshape(4, width, width).transpose(1, 0, 2).reshape(width, WIDTH).astype(F32)
    )
    return (
        output, grad_input, vec_sum[0], vec_sum[1], d_w_qkv, d_w_out,
        vec_sum[2], vec_sum[3], d_w_in, d_w_down,
    )


def solution(mesh):
    in_specs = (
        P(("exp", "hid"), None), P(), P(), P(None, None, "hid"), P("hid", None), P(), P(),
        P("exp", None, "hid"), P("exp", "hid", None), P(("exp", "hid"), None), P(("exp", "hid"), None),
    )
    out_specs = (
        P(("exp", "hid"), None), P(("exp", "hid"), None), P(), P(), P(None, None, "hid"), P("hid", None),
        P(), P(), P("exp", None, "hid"), P("exp", "hid", None),
    )
    return jax.shard_map(on_device, mesh=mesh, in_specs=in_specs, out_specs=out_specs, check_vma=False)
```

```python
import jax
import jax.numpy as jnp
from jax import lax
from jax.experimental import pallas as pl
from jax.experimental.pallas import tpu as pltpu
from jax.sharding import PartitionSpec as P

HD = 64
EPSILON = 1e-05
NEG_LARGE = -1e30
BF = jnp.bfloat16
F32 = jnp.float32
MESH = pl.DeviceIdType.MESH
ANY = pl.BlockSpec(memory_space=pl.ANY)
VMEM = pl.BlockSpec(memory_space=pltpu.VMEM)
N_HID = 4
N_EXP = 32
ROWS = 256
WIDTH = 1024
SLOTS = 512
MIB = 1 << 20


def dot(a, b):
    return jnp.dot(a, b, preferred_element_type=F32)


def dot_nt(a, b):
    return lax.dot_general(a, b, (((1,), (1,)), ((), ())), preferred_element_type=F32)


def dot_tn(a, b):
    return lax.dot_general(a, b, (((0,), (0,)), ((), ())), preferred_element_type=F32)


def place():
    return lax.axis_index("exp"), lax.axis_index("hid")


def hid_of(h, step):
    return lax.rem(h + step + N_HID, N_HID)


def exp_of(e, dz, dx, dc):
    z, x, c = e // 8, lax.rem(e // 2, 4), lax.rem(e, 2)
    return (lax.rem(z + dz, 4) * 4 + lax.rem(x + dx, 4)) * 2 + lax.rem(c + dc, 2)


def plane_steps(order):
    return [
        (dz, dx, dc)
        for dz in order
        for dx in (0, 1, 3, 2)
        for dc in (0, 1)
        if (dz, dx, dc) != (0, 0, 0)
    ]


def signal(peers):
    barrier = pltpu.get_barrier_semaphore()
    for peer in peers:
        pl.semaphore_signal(barrier, inc=1, device_id=peer, device_id_type=MESH)


def await_signals(peers):
    pl.semaphore_wait(pltpu.get_barrier_semaphore(), len(peers))


class Links:
    def __init__(self, send_sem, recv_sem):
        self.send_sem, self.recv_sem, self.used = send_sem, recv_sem, 0

    def remote(self, src, dst, peer):
        i = self.used
        self.used += 1
        copy = pltpu.make_async_remote_copy(
            src_ref=src,
            dst_ref=dst,
            send_sem=self.send_sem.at[i],
            recv_sem=self.recv_sem.at[i],
            device_id=peer,
            device_id_type=MESH,
        )
        copy.start()
        return copy

    def local(self, src, dst):
        i = self.used
        self.used += 1
        copy = pltpu.make_async_copy(src, dst, self.send_sem.at[i])
        copy.start()
        return copy


def rows_at(start, size, unit=16):
    return pl.ds(pl.multiple_of(start, unit), size)


def split_experts(block):
    n = block.shape[0] // 16
    wide = block.astype(F32).reshape(n, 2, 8, block.shape[1])
    return [wide[:, i].reshape(n * 8, block.shape[1]).astype(BF) for i in (0, 1)]


def merge_experts(first, second):
    n, width = first.shape[0] // 8, first.shape[1]
    pair = jnp.concatenate(
        [first.reshape(n, 1, 8, width), second.reshape(n, 1, 8, width)], axis=1
    )
    return pair.reshape(n * 16, width).astype(BF)


def norm_parts(rows):
    centered = rows - jnp.mean(rows, -1, keepdims=True)
    scale = lax.rsqrt(jnp.mean(centered * centered, -1, keepdims=True) + EPSILON)
    return centered * scale, scale


def norm_back(grad, hat, scale, gain):
    gh = grad * gain
    inner = jnp.mean(gh * hat, -1, keepdims=True)
    return scale * (gh - jnp.mean(gh, -1, keepdims=True) - hat * inner)


def slot_picks(ids):
    named = jnp.where(ids == lax.broadcasted_iota(jnp.int32, (128, ROWS), 0), 1.0, 0.0)
    earlier = jnp.where(
        lax.broadcasted_iota(jnp.int32, (ROWS, ROWS), 0)
        < lax.broadcasted_iota(jnp.int32, (ROWS, ROWS), 1),
        1.0,
        0.0,
    )
    running = dot(named.astype(BF), earlier.astype(BF))
    position = jnp.sum(running * named, axis=0, keepdims=True).astype(jnp.int32)
    slot = ids * 8 + position
    return jnp.where(slot == lax.broadcasted_iota(jnp.int32, (SLOTS, ROWS), 0), 1.0, 0.0).astype(BF)


def gather_begin(links, src, out, e, h):
    up, down = (e, hid_of(h, 1)), (e, hid_of(h, -1))
    mine = out.at[rows_at(h * ROWS, ROWS)]
    first = links.remote(src, mine, up)
    second = links.remote(src, mine, down)
    return first, second, links.local(src, mine)


def gather_relay(links, begun, out, e, h):
    up, down = (e, hid_of(h, 1)), (e, hid_of(h, -1))
    half = ROWS // 2
    first, second, own = begun
    first.wait_recv()
    piece = out.at[rows_at(hid_of(h, -1) * ROWS, half)]
    third = links.remote(piece, piece, up)
    second.wait_recv()
    piece = out.at[rows_at(hid_of(h, 1) * ROWS + half, half)]
    fourth = links.remote(piece, piece, down)
    return first, second, third, fourth, own


def gather_end(copies):
    first, second, third, fourth, own = copies
    own.wait()
    third.wait()
    fourth.wait()
    first.wait_send()
    second.wait_send()


def reduce_begin(links, term, got, half_up, half_down, e, h):
    up, down = (e, hid_of(h, 1)), (e, hid_of(h, -1))
    half = ROWS // 2
    far, above, below = hid_of(h, 2) * ROWS, hid_of(h, 1) * ROWS, hid_of(h, -1) * ROWS
    one = links.remote(term.at[rows_at(far, half)], half_up, up)
    two = links.remote(term.at[rows_at(far + half, half)], half_down, down)
    three = links.remote(term.at[rows_at(above + half, half)], got.at[0, pl.ds(half, half)], up)
    four = links.remote(term.at[rows_at(below, half)], got.at[1, pl.ds(0, half)], down)
    return one, two, three, four


def reduce_middle(links, begun, term, got, half_up, half_down, pass_up, pass_down, e, h):
    up, down = (e, hid_of(h, 1)), (e, hid_of(h, -1))
    half = ROWS // 2
    above, below = hid_of(h, 1) * ROWS, hid_of(h, -1) * ROWS
    one, two, three, four = begun
    one.wait_recv()
    pass_up[...] = (
        term[rows_at(above, half), :].astype(F32) + half_up[...].astype(F32)
    ).astype(BF)
    five = links.remote(pass_up, got.at[0, pl.ds(0, half)], up)
    two.wait_recv()
    pass_down[...] = (
        term[rows_at(below + half, half), :].astype(F32) + half_down[...].astype(F32)
    ).astype(BF)
    six = links.remote(pass_down, got.at[1, pl.ds(half, half)], down)
    return one, two, three, four, five, six


def reduce_end(copies, term, got, h):
    for copy in copies[2:]:
        copy.wait_recv()
    return (
        term[rows_at(h * ROWS, ROWS), :].astype(F32)
        + got[0].astype(F32)
        + got[1].astype(F32)
    )


def reduce_scratch():
    half = ROWS // 2
    return [pltpu.VMEM((2, ROWS, WIDTH), BF)] + [pltpu.VMEM((half, WIDTH), BF)] * 4


def sems(count):
    return [pltpu.SemaphoreType.DMA((count,)), pltpu.SemaphoreType.DMA((count,))]


def hid_peers(e, h):
    return [(e, hid_of(h, 1)), (e, hid_of(h, -1))]


def plane_peers(e, h):
    return [(exp_of(e, *step), h) for step in plane_steps((0, 1, 3, 2))]


def head_lanes(shape, head):
    return lax.broadcasted_iota(jnp.int32, shape, 1) // HD == head


def causal_tail(scores_t):
    keys, queries = scores_t.shape
    tail = scores_t[keys - queries :]
    allowed = lax.broadcasted_iota(jnp.int32, tail.shape, 0) <= lax.broadcasted_iota(
        jnp.int32, tail.shape, 1
    )
    tail = jnp.where(allowed, tail, NEG_LARGE)
    if keys == queries:
        return tail
    return jnp.concatenate([scores_t[: keys - queries], tail], axis=0)


def attend_block(block, q, k, v, heads, logs, total):
    keys, here, width = (block + 1) * ROWS, pl.ds(block * ROWS, ROWS), q.shape[1]
    total[...] = jnp.zeros_like(total)

    def head_step(head, carry):
        lanes = head_lanes((ROWS, width), head)
        query = jnp.where(lanes, q[here, :] * BF(HD**-0.5), BF(0))
        scores = causal_tail(dot_nt(k[pl.ds(0, keys), :], query))
        top = jnp.max(scores, axis=0, keepdims=True)
        exps = jnp.exp(scores - top)
        summed = jnp.sum(exps, axis=0, keepdims=True)
        logs[pl.ds(head, 1), here] = top + jnp.log(summed)
        probs = (exps * (1.0 / summed)).astype(BF)
        mixed = dot_tn(probs, v[pl.ds(0, keys), :])
        total[...] = jnp.where(lanes, mixed, total[...])
        return carry

    lax.fori_loop(0, width // HD, head_step, 0)
    heads[here, :] = total[...].astype(BF)


def attend_block_back(block, q, k, v, gheads, logs, gq, gk, gv, dq):
    keys, here, width = (block + 1) * ROWS, pl.ds(block * ROWS, ROWS), q.shape[1]
    dq[...] = jnp.zeros_like(dq)

    def head_step(head, carry):
        lanes = head_lanes((ROWS, width), head)
        query = jnp.where(lanes, q[here, :] * BF(HD**-0.5), BF(0))
        grad = jnp.where(lanes, gheads[here, :], BF(0))
        scores = causal_tail(dot_nt(k[pl.ds(0, keys), :], query))
        probs = jnp.exp(scores - logs[pl.ds(head, 1), here])
        weighted = probs * dot_nt(v[pl.ds(0, keys), :], grad)
        inner = jnp.sum(weighted, axis=0, keepdims=True)
        grad_scores = (weighted - probs * inner).astype(BF)
        gv[pl.ds(0, keys), :] += dot(probs.astype(BF), grad)
        gk[pl.ds(0, keys), :] += dot(grad_scores, query)
        dq[...] = jnp.where(lanes, dot_tn(grad_scores, k[pl.ds(0, keys), :]), dq[...])
        return carry

    lax.fori_loop(0, width // HD, head_step, 0)
    gq[here, :] = (dq[...] * HD**-0.5).astype(BF)


def front_kernel(
    x_ref, gain1_ref, bias1_ref, gain2_ref, bias2_ref, ids_ref, grad_hbm, wqkv_hbm, wout_hbm,
    joined_out, q_out, k_out, v_out, hall_out, wall_out, logs_ref, residual_ref, pick_ref,
    g0_out, g1_out, g2_out, rows_ref,
    normed, joined, grad, wqkv, wout, wall, q, k, v, heads, hall, total,
    outgoing_g, landed_g, staged_g, outgoing, landed, staged, send_sem, recv_sem,
):
    e, h = place()
    z, chip, core = e // 8, e // 2, lax.rem(e, 2)
    up, down, far = (e, hid_of(h, 1)), (e, hid_of(h, -1)), (e, hid_of(h, 2))
    peers = [up, down, far] + plane_peers(e, h)
    signal(peers)
    links = Links(send_sem, recv_sem)
    loads = [links.local(wout_hbm, wout), links.local(grad_hbm, grad), links.local(wqkv_hbm, wqkv)]
    hat, _ = norm_parts(x_ref[...].astype(F32))
    normed[...] = (hat * gain1_ref[...] + bias1_ref[...]).astype(BF)
    await_signals(peers)
    gather = gather_begin(links, normed, joined, e, h)
    loads[0].wait()
    wall_at = (rows_at(chip * 16, 16), pl.ds(pl.multiple_of(core * 512, 512), 512))
    share, share_place = wout.at[wall_at], wall.at[(h,) + wall_at]
    wall_sends = [links.remote(share, share_place, peer) for peer in (up, down, far)]
    wall_kept = links.local(share, share_place)
    pick = slot_picks(ids_ref[...])
    pick_ref[...] = pick
    loads[1].wait()
    outgoing_g[...] = dot(pick, grad[...]).astype(BF)
    mine = landed_g.at[rows_at(e * 16, 16)]
    g_sends = []
    for step in plane_steps((0, 1, 3, 2)):
        t = exp_of(e, *step)
        g_sends.append(links.remote(outgoing_g.at[rows_at(t * 16, 16)], mine, (t, h)))
    g_kept = links.local(outgoing_g.at[rows_at(e * 16, 16)], mine)
    wall_kept.wait()
    for copy in wall_sends:
        copy.wait_recv()
    shares = wall.at[(slice(None),) + wall_at]
    wall_spread = [links.remote(shares, shares, peer) for peer in plane_peers(e, h)]

    def project(block):
        here = rows_at(block * ROWS, ROWS)
        rows = joined[here, :]
        for i, ref in enumerate((q, k, v)):
            ref[here, :] = dot(rows, wqkv[i]).astype(BF)

    gather[2].wait()
    loads[2].wait()
    project(h)
    gathered = gather_relay(links, gather, joined, e, h)
    project(hid_of(h, -1))
    project(hid_of(h, 1))
    g_kept.wait()
    for copy in g_sends:
        copy.wait_recv()
    for i in range(4):
        pair = split_experts(landed_g[pl.ds(i * 128, 128), :])
        for j in (0, 1):
            staged_g[j, pl.ds(i * 64, 64), :] = pair[j]
    g_first = [links.remote(staged_g, g1_out, up), links.remote(staged_g, g2_out, down)]
    outs = [links.local(staged_g, g0_out)]
    for copy in gathered[2:4]:
        copy.wait_recv()
    project(hid_of(h, 2))
    outs += [links.local(src, dst) for src, dst in ((joined, joined_out), (q, q_out), (k, k_out), (v, v_out))]
    head_sends = []
    for peer in (far, up, down, (e, h)):
        for b in range(N_HID):

            @pl.when(peer[1] == b)
            def _(b=b):
                attend_block(b, q, k, v, heads, logs_ref, total)

        piece = heads.at[rows_at(peer[1] * ROWS, ROWS)]
        if peer[1] is h:
            head_own = links.local(piece, hall.at[h])
        else:
            head_sends.append(links.remote(piece, hall.at[h], peer))
    for copy in wall_spread:
        copy.wait_recv()
    outs.append(links.local(wall, wall_out))
    head_own.wait()
    for copy in head_sends:
        copy.wait_recv()
    outs.append(links.local(hall, hall_out))
    attn_sum = dot(hall[0], wall[0])
    for i in range(1, N_HID):
        attn_sum = attn_sum + dot(hall[i], wall[i])
    residual = x_ref[...].astype(F32) + attn_sum
    residual_ref[...] = residual
    hat, _ = norm_parts(residual)
    routed = (hat * gain2_ref[...] + bias2_ref[...]).astype(BF)
    outgoing[...] = dot(pick_ref[...], routed).astype(BF)
    mine = landed.at[rows_at(e * 16, 16)]
    order = (0, 1, 3, 2)
    sent = {}
    for dz in order:
        sent[dz] = []
        for step in plane_steps((dz,)):
            t = exp_of(e, *step)
            sent[dz].append(links.remote(outgoing.at[rows_at(t * 16, 16)], mine, (t, h)))
    kept = links.local(outgoing.at[rows_at(e * 16, 16)], mine)
    waits = []
    pending = None

    def relay(chunk):
        at, first, second = chunk
        first.wait_recv()
        third = links.remote(
            rows_ref.at[0, rows_at(ROWS + at, 64)], rows_ref.at[0, rows_at(3 * ROWS + at, 64)], up
        )
        second.wait_recv()
        fourth = links.remote(
            rows_ref.at[1, rows_at(2 * ROWS + at, 64)], rows_ref.at[1, rows_at(3 * ROWS + at, 64)], down
        )
        waits.extend((third, fourth))

    for dz in order:
        if dz == 0:
            kept.wait()
        for copy in sent[dz]:
            copy.wait_recv()
        from_z = lax.rem(z - dz + 4, 4)
        at = from_z * 64
        pair = split_experts(landed[rows_at(from_z * 128, 128), :])
        for j in (0, 1):
            staged[j, rows_at(at, 64), :] = pair[j]
        piece = staged.at[:, rows_at(at, 64)]
        first = links.remote(piece, rows_ref.at[:, rows_at(ROWS + at, 64)], up)
        second = links.remote(piece, rows_ref.at[:, rows_at(2 * ROWS + at, 64)], down)
        own = links.local(piece, rows_ref.at[:, rows_at(at, 64)])
        if pending is not None:
            relay(pending)
        pending = (at, first, second)
        waits.append(own)
        sent[dz].extend((first, second))
    relay(pending)
    for copy in waits + outs + g_first:
        copy.wait()
    for dz in order:
        for copy in sent[dz]:
            copy.wait_send()
    for copy in list(gathered[:4]) + wall_sends + wall_spread + g_sends + head_sends:
        copy.wait_send()


def front_call(block_input, gain1, bias1, gain2, bias2, ids, out_grad, w_qkv, w_out):
    rows, width = N_HID * ROWS, w_qkv.shape[2]
    flat = jax.ShapeDtypeStruct((rows, width), BF)
    pair = jax.ShapeDtypeStruct((2, ROWS, WIDTH), BF)
    shares = (N_HID, ROWS, WIDTH)
    held = pltpu.VMEM((rows, width), BF)
    slots = pltpu.VMEM((SLOTS, WIDTH), BF)
    staged = pltpu.VMEM((2, ROWS, WIDTH), BF)
    block = pltpu.VMEM((ROWS, WIDTH), BF)
    return pl.pallas_call(
        front_kernel,
        out_shape=(
            jax.ShapeDtypeStruct((rows, WIDTH), BF),
            flat, flat, flat,
            jax.ShapeDtypeStruct((N_HID, ROWS, width), BF),
            jax.ShapeDtypeStruct(shares, BF),
            jax.ShapeDtypeStruct((8, rows), F32),
            jax.ShapeDtypeStruct((ROWS, WIDTH), F32),
            jax.ShapeDtypeStruct((SLOTS, ROWS), BF),
            pair, pair, pair,
            jax.ShapeDtypeStruct((2, rows, WIDTH), BF),
        ),
        in_specs=[VMEM] * 6 + [ANY] * 3,
        out_specs=[ANY] * 6 + [VMEM] * 3 + [ANY] * 4,
        scratch_shapes=[
            block, pltpu.VMEM((rows, WIDTH), BF), block, pltpu.VMEM(w_qkv.shape, BF), block, pltpu.VMEM(shares, BF),
            held, held, held, held, pltpu.VMEM((N_HID, ROWS, width), BF), pltpu.VMEM((ROWS, width), F32),
            slots, slots, staged, slots, slots, staged,
        ]
        + sems(3 + 5 + 4 + 32 + 31 + 2 + 5 + 4 + 2 + 32 + 20),
        compiler_params=pltpu.CompilerParams(
            collective_id=1, has_side_effects=True, vmem_limit_bytes=52 * MIB
        ),
        cost_estimate=pl.CostEstimate(flops=6 * 10**9, bytes_accessed=100 * MIB, transcendentals=0),
        name="front",
    )(block_input, gain1, bias1, gain2, bias2, ids, out_grad, w_qkv, w_out)


PARTS = ((0, 1), (1, 1), (0, 2), (1, 2), (0, 3), (1, 3))


def store_part(value, expert, block, own_ref, part_refs):
    @pl.when(block == 0)
    def _():
        own_ref[expert] = value

    for (i, j), ref in zip(PARTS, part_refs):

        @pl.when((expert == i) & (block == j))
        def _(ref=ref):
            ref[...] = value


def part_specs():
    flat = pl.BlockSpec((ROWS, WIDTH), lambda i, j: (0, 0))
    return [pl.BlockSpec((2, ROWS, WIDTH), lambda i, j: (0, 0, 0))] + [flat] * len(PARTS)


def part_shapes():
    return (jax.ShapeDtypeStruct((2, ROWS, WIDTH), BF),) + (jax.ShapeDtypeStruct((ROWS, WIDTH), BF),) * len(PARTS)


def hidden_kernel(x_ref, win_ref, act_ref, slope_ref):
    pre = dot(x_ref[0], win_ref[0])
    root = 0.7978845608028654
    square = pre * pre
    curve = jnp.tanh(root * (pre + 0.044715 * (square * pre)))
    half = 0.5 * (1.0 + curve)
    act_ref[0] = (pre * half).astype(BF)
    slope_ref[0] = half + 0.5 * pre * (1.0 - curve * curve) * (root * (1.0 + 3 * 0.044715 * square))


PART = pl.BlockSpec((1, ROWS, WIDTH), lambda i, j: (i, j, 0))
WEIGHT = pl.BlockSpec((1, WIDTH, WIDTH), lambda i, j: (i, 0, 0))


def hidden_call(rows, w_in):
    return pl.pallas_call(
        hidden_kernel,
        grid=(2, N_HID),
        out_shape=(jax.ShapeDtypeStruct(rows.shape, BF), jax.ShapeDtypeStruct(rows.shape, F32)),
        in_specs=[PART, WEIGHT],
        out_specs=[PART, PART],
        compiler_params=pltpu.CompilerParams(vmem_limit_bytes=40 * MIB),
        cost_estimate=pl.CostEstimate(flops=43 * 10**8, bytes_accessed=20 * MIB, transcendentals=2 * 10**6),
        name="experts_hidden",
    )(rows, w_in)


def expert_kernel(
    slope_ref, g0_ref, g1_ref, g2_ref, g3a_ref, g3b_ref, win_ref, wdown_ref,
    gpre_ref, grad_ref, own_ref, *part_refs
):
    expert, block = pl.program_id(0), pl.program_id(1)
    for i, ref in enumerate((g0_ref, g1_ref, g2_ref)):

        @pl.when(block == i)
        def _(ref=ref):
            grad_ref[...] = ref[...]

    for i, ref in enumerate((g3a_ref, g3b_ref)):

        @pl.when((block == 3) & (expert == i))
        def _(ref=ref):
            grad_ref[0] = ref[...]

    grad_act = dot_nt(grad_ref[0], wdown_ref[0])
    grad_pre = (grad_act * slope_ref[0]).astype(BF)
    gpre_ref[0] = grad_pre
    store_part(dot_nt(grad_pre, win_ref[0]).astype(BF), expert, block, own_ref, part_refs)


def expert_call(slope, grads, w_in, w_down):
    whole = jax.ShapeDtypeStruct(slope.shape, BF)
    fixed = pl.BlockSpec((1, ROWS, WIDTH), lambda i, j: (i, 0, 0))
    flat = pl.BlockSpec((ROWS, WIDTH), lambda i, j: (0, 0))
    return pl.pallas_call(
        expert_kernel,
        grid=(2, N_HID),
        out_shape=(whole,) * 2 + part_shapes(),
        in_specs=[PART, fixed, fixed, fixed, flat, flat, WEIGHT, WEIGHT],
        out_specs=[PART] * 2 + part_specs(),
        compiler_params=pltpu.CompilerParams(vmem_limit_bytes=52 * MIB),
        cost_estimate=pl.CostEstimate(flops=87 * 10**8, bytes_accessed=32 * MIB, transcendentals=0),
        name="experts_grads",
    )(slope, *grads, w_in, w_down)


def down_kernel(act_ref, wdown_ref, own_ref, *part_refs):
    value = dot(act_ref[0], wdown_ref[0]).astype(BF)
    store_part(value, pl.program_id(0), pl.program_id(1), own_ref, part_refs)


def down_call(act, w_down):
    return pl.pallas_call(
        down_kernel,
        grid=(2, N_HID),
        out_shape=part_shapes(),
        in_specs=[
            pl.BlockSpec((1, ROWS, WIDTH), lambda i, j: (i, j, 0)),
            pl.BlockSpec((1, WIDTH, WIDTH), lambda i, j: (i, 0, 0)),
        ],
        out_specs=part_specs(),
        compiler_params=pltpu.CompilerParams(vmem_limit_bytes=40 * MIB),
        cost_estimate=pl.CostEstimate(flops=43 * 10**8, bytes_accessed=12 * MIB, transcendentals=0),
        name="experts_down",
    )(act, w_down)


CHIPS = [(dz, dx, 0) for dz in (0, 1, 3, 2) for dx in (0, 1, 3, 2) if (dz, dx) != (0, 0)]
CUT = 96


def back_kernel(
    up_own, up_pass_up, up_pass_down, up_far_up, up_far_down, up_near_up, up_near_down,
    pick_ref, residual_ref, gain1_ref, gain2_ref, logs_ref,
    grad_hbm, x_hbm, wall_hbm, wqkv_hbm, joined_hbm, q_hbm, k_hbm, v_hbm, hall_hbm,
    m_own_hbm, m_low1, m_high1, m_low2, m_high2, m_low3, m_high3,
    out_ref, ginput_ref, dwq_ref, dwo_ref, vecsum_ref,
    grad_in, x, wall, wqkv, joined, q, k, v, hall, m_own, m_pass_up, m_pass_down,
    pass_up, pass_down, got, outgoing, landed, gres, gas, gheads_out, gheads,
    dwo, dwo_got, dwo_half, dwo_pieces, dwo_sum, dwo_hid, dwo_part,
    m_far_up, m_far_down, m_near_up, m_near_down, m_got, m_outgoing, m_landed,
    gq, gk, gv, dq, term, t_got, half_up, half_down, t_pass_up, t_pass_down,
    dwq, dwq_got, dwq_half, dwq_pieces, dwq_sum, vec, vec_got, send_sem, recv_sem,
):
    e, h = place()
    z, chip, core = e // 8, e // 2, lax.rem(e, 2)
    up, down, far = (e, hid_of(h, 1)), (e, hid_of(h, -1)), (e, hid_of(h, 2))
    twin = (exp_of(e, 0, 0, 1), h)
    across = [(exp_of(e, *step), h) for step in CHIPS]
    plane = plane_peers(e, h)
    peers = [up, down, far] + plane
    signal(peers)
    links = Links(send_sem, recv_sem)
    load = {}
    for name, src, dst in (
        ("grad", grad_hbm, grad_in), ("wall", wall_hbm, wall), ("hall", hall_hbm, hall), ("q", q_hbm, q), ("k", k_hbm, k),
        ("v", v_hbm, v), ("wqkv", wqkv_hbm, wqkv), ("joined", joined_hbm, joined), ("x", x_hbm, x),
        ("m", m_own_hbm, m_own), ("mu", m_low2, m_pass_up), ("md", m_high1, m_pass_down),
    ):
        load[name] = links.local(src, dst)
    await_signals(peers)
    ended = []
    order = (2, 1, 3, 0)
    passed = []
    for dz in order:
        at = lax.rem(z + dz, 4) * 64
        piece = rows_at(at, 64)
        pass_up[piece, :] = (up_pass_up[piece, :].astype(F32) + up_far_up[piece, :].astype(F32)).astype(BF)
        five = links.remote(pass_up.at[piece], got.at[0, piece], up)
        pass_down[piece, :] = (up_pass_down[piece, :].astype(F32) + up_far_down[piece, :].astype(F32)).astype(BF)
        six = links.remote(pass_down.at[piece], got.at[1, piece], down)
        passed.append((at, five, six))
        ended += [five, six]
    mine = landed.at[rows_at(e * 16, 16)]
    back = []
    for dz, (at, five, six) in zip(order, passed):
        five.wait_recv()
        six.wait_recv()
        piece = rows_at(at, 64)
        pair = [
            up_own[j, piece, :].astype(F32) + got[j, piece, :].astype(F32) + near[piece, :].astype(F32)
            for j, near in enumerate((up_near_down, up_near_up))
        ]
        outgoing[rows_at(at * 2, 128), :] = merge_experts(*pair)
        for step in plane_steps((dz,)):
            t = exp_of(e, *step)
            back.append(links.remote(outgoing.at[rows_at(t * 16, 16)], mine, (t, h)))
    kept = links.local(outgoing.at[rows_at(e * 16, 16)], mine)
    kept.wait()
    load["grad"].wait()
    load["wall"].wait()
    load["hall"].wait()
    for copy in back:
        copy.wait_recv()
    ended += back
    routed = dot_tn(pick_ref[...], landed[...])
    hat, scale = norm_parts(residual_ref[...])
    vec[0] = jnp.zeros_like(vec[0])
    vec[0, 2:3, :] = jnp.sum(routed * hat, axis=0, keepdims=True)
    vec[0, 3:4, :] = jnp.sum(routed, axis=0, keepdims=True)
    whole = grad_in[...].astype(F32) + norm_back(routed, hat, scale, gain2_ref[...])
    gres[...] = whole
    gas[...] = whole.astype(BF)
    head_sends = []
    for i, peer in enumerate((far, up, down)):
        gheads_out[i] = dot_nt(gas[...], wall[peer[1]]).astype(BF)
        head_sends.append(links.remote(gheads_out.at[i], gheads.at[rows_at(h * ROWS, ROWS)], peer))
    ended += head_sends
    gheads[rows_at(h * ROWS, ROWS), :] = dot_nt(gas[...], wall[h]).astype(BF)
    m_first = [
        links.remote(m_low3, m_far_up, up),
        links.remote(m_high3, m_far_down, down),
        links.remote(m_high2, m_near_up, up),
        links.remote(m_low1, m_near_down, down),
    ]
    ended += m_first
    for i in range(N_HID):
        dwo[i] = dot_tn(hall[i], gas[...]).astype(BF)
    other = pl.ds(pl.multiple_of((1 - core) * 512, 512), 512)
    own = pl.ds(pl.multiple_of(core * 512, 512), 512)
    dwo_swap = links.remote(dwo.at[:, :, other], dwo_got, twin)
    ended.append(dwo_swap)
    for name in ("q", "k", "v"):
        load[name].wait()
    for copy in head_sends:
        copy.wait_recv()
    gk[...] = jnp.zeros_like(gk)
    gv[...] = jnp.zeros_like(gv)

    def attention(block):
        attend_block_back(block, q, k, v, gheads, logs_ref, gq, gk, gv, dq)

    attention(0)
    attention(1)
    dwo_swap.wait_recv()
    for i in range(N_HID):
        dwo_half[i] = (dwo[i, :, own].astype(F32) + dwo_got[i].astype(F32)).astype(BF)
    dwo_spread = [
        links.remote(dwo_half.at[:, rows_at(peer[0] // 2 * 16, 16)], dwo_pieces.at[i], peer)
        for i, peer in enumerate(across)
    ]
    ended += dwo_spread
    attention(2)
    for copy in dwo_spread:
        copy.wait_recv()
    whole = dwo_half[:, rows_at(chip * 16, 16), :].astype(F32)
    for i in range(len(across)):
        whole = whole + dwo_pieces[i].astype(F32)
    dwo_sum[...] = whole.astype(BF)
    dwo_cross = [
        links.remote(dwo_sum.at[peer[1]], dwo_hid.at[i], peer) for i, peer in enumerate((far, up, down))
    ]
    ended += dwo_cross
    attention(3)
    for copy in dwo_cross:
        copy.wait_recv()
    whole = dwo_sum[h].astype(F32)
    for i in range(3):
        whole = whole + dwo_hid[i].astype(F32)
    dwo_part[...] = whole.astype(BF)
    dwo_place = dwo_ref.at[rows_at(chip * 16, 16), own]
    dwo_share = [links.remote(dwo_part, dwo_place, peer) for peer in plane]
    ended += dwo_share
    dwo_own = links.local(dwo_part, dwo_place)
    load["mu"].wait()
    load["md"].wait()
    m_first[0].wait_recv()
    m_pass_up[...] = (m_pass_up[...].astype(F32) + m_far_up[...].astype(F32)).astype(BF)
    five = links.remote(m_pass_up, m_got.at[0], up)
    m_first[1].wait_recv()
    m_pass_down[...] = (m_pass_down[...].astype(F32) + m_far_down[...].astype(F32)).astype(BF)
    six = links.remote(m_pass_down, m_got.at[1], down)
    ended += [five, six]
    load["wqkv"].wait()
    load["joined"].wait()
    parts = (gq[...], gk[...].astype(BF), gv[...].astype(BF))
    term[...] = sum(dot_nt(part, wqkv[i]) for i, part in enumerate(parts)).astype(BF)
    begun = reduce_begin(links, term, t_got, half_up, half_down, e, h)
    for i, part in enumerate(parts):
        dwq[pl.ds(i * WIDTH, WIDTH), :] = dot_tn(joined[...], part).astype(BF)
    count = dwq.shape[0] // 2
    dwq_swap = links.remote(dwq.at[rows_at((1 - core) * count, count)], dwq_got, twin)
    ended.append(dwq_swap)
    reduced = reduce_middle(links, begun, term, t_got, half_up, half_down, t_pass_up, t_pass_down, e, h)
    ended += reduced
    dwq_swap.wait_recv()
    dwq_half[...] = (dwq[rows_at(core * count, count), :].astype(F32) + dwq_got[...].astype(F32)).astype(BF)
    dwq_spread = [
        links.remote(dwq_half.at[rows_at(peer[0] // 2 * CUT, CUT)], dwq_pieces.at[i], peer)
        for i, peer in enumerate(across)
    ]
    ended += dwq_spread
    load["m"].wait()
    m_first[2].wait_recv()
    m_first[3].wait_recv()
    five.wait_recv()
    six.wait_recv()
    for i in range(4):
        piece = pl.ds(i * 64, 64)
        pair = [
            m_own[j, piece, :].astype(F32) + m_got[j, piece, :].astype(F32) + near[piece, :].astype(F32)
            for j, near in enumerate((m_near_down, m_near_up))
        ]
        m_outgoing[pl.ds(i * 128, 128), :] = merge_experts(*pair)
    mine = m_landed.at[rows_at(e * 16, 16)]
    m_back = []
    for step in plane_steps((2, 1, 3, 0)):
        t = exp_of(e, *step)
        m_back.append(links.remote(m_outgoing.at[rows_at(t * 16, 16)], mine, (t, h)))
    m_kept = links.local(m_outgoing.at[rows_at(e * 16, 16)], mine)
    ended += m_back
    load["x"].wait()
    grad = reduce_end(reduced, term, t_got, h)
    hat, scale = norm_parts(x[...].astype(F32))
    ginput_ref[...] = gres[...] + norm_back(grad, hat, scale, gain1_ref[...])
    vec[0, 0:1, :] = jnp.sum(grad * hat, axis=0, keepdims=True)
    vec[0, 1:2, :] = jnp.sum(grad, axis=0, keepdims=True)
    rounds = (
        [up, down, far],
        [(exp_of(e, 0, dx, dc), h) for dx in range(4) for dc in (0, 1) if (dx, dc) != (0, 0)],
        [(exp_of(e, dz, 0, 0), h) for dz in (1, 2, 3)],
    )
    slot = 0
    copies = [links.remote(vec.at[0], vec_got.at[slot + i], peer) for i, peer in enumerate(rounds[0])]
    for copy in dwq_spread:
        copy.wait_recv()
    whole = dwq_half[rows_at(chip * CUT, CUT), :].astype(F32)
    for i in range(len(across)):
        whole = whole + dwq_pieces[i].astype(F32)
    dwq_sum[...] = whole.astype(BF)
    dwq_place = dwq_ref.at[rows_at(core * count + chip * CUT, CUT)]
    dwq_share = [links.remote(dwq_sum, dwq_place, peer) for peer in across]
    ended += dwq_share
    dwq_own = links.local(dwq_sum, dwq_place)
    for number in range(3):
        for copy in copies:
            copy.wait_recv()
        whole = vec[number]
        for i in range(len(rounds[number])):
            whole = whole + vec_got[slot + i]
        slot += len(rounds[number])
        ended += copies
        if number < 2:
            vec[number + 1] = whole
            copies = [
                links.remote(vec.at[number + 1], vec_got.at[slot + i], peer)
                for i, peer in enumerate(rounds[number + 1])
            ]
        else:
            vecsum_ref[...] = whole
    m_kept.wait()
    for copy in m_back:
        copy.wait_recv()
    out_ref[...] = (residual_ref[...] + dot_tn(pick_ref[...], m_landed[...])).astype(BF)
    dwq_own.wait()
    for copy in dwq_share:
        copy.wait_recv()
    both = dwq_ref.at[rows_at(core * count, count)]
    twins = links.remote(both, both, twin)
    dwo_own.wait()
    for copy in dwo_share:
        copy.wait_recv()
    twins.wait()
    for copy in ended:
        copy.wait_send()


def back_call(up_own, up_passes, up_fars, up_nears, pick, residual, gain1, gain2, logs, out_grad, block_input, wall, w_qkv, joined, q, k, v, hall, down_own, down_parts):
    rows, width = q.shape
    block = pltpu.VMEM((ROWS, WIDTH), BF)
    half = pltpu.VMEM((ROWS // 2, WIDTH), BF)
    pair = pltpu.VMEM((2, ROWS, WIDTH), BF)
    slots = pltpu.VMEM((SLOTS, WIDTH), BF)
    held = pltpu.VMEM((rows, width), BF)
    wide = pltpu.VMEM((rows, WIDTH), BF)
    shares = pltpu.VMEM((N_HID, ROWS, WIDTH), BF)
    half_shares = pltpu.VMEM((N_HID, ROWS, WIDTH // 2), BF)
    quarter = pltpu.VMEM((3 * WIDTH // 2, width), BF)
    return pl.pallas_call(
        back_kernel,
        out_shape=(
            jax.ShapeDtypeStruct((ROWS, WIDTH), BF),
            jax.ShapeDtypeStruct((ROWS, WIDTH), F32),
            jax.ShapeDtypeStruct((3 * WIDTH, width), BF),
            jax.ShapeDtypeStruct((ROWS, WIDTH), BF),
            jax.ShapeDtypeStruct((8, WIDTH), F32),
        ),
        in_specs=[VMEM] * 12 + [ANY] * 16,
        out_specs=[VMEM] * 5,
        scratch_shapes=[
            block, block, shares, pltpu.VMEM(w_qkv.shape, BF), wide, held, held, held,
            pltpu.VMEM((N_HID, ROWS, width), BF), pair, block, block,
            block, block, pair, slots, slots, pltpu.VMEM((ROWS, WIDTH), F32), block,
            pltpu.VMEM((3, ROWS, width), BF), held,
            shares, half_shares, half_shares, pltpu.VMEM((15, N_HID, 16, WIDTH // 2), BF),
            pltpu.VMEM((N_HID, 16, WIDTH // 2), BF), pltpu.VMEM((3, 16, WIDTH // 2), BF), pltpu.VMEM((16, WIDTH // 2), BF),
            block, block, block, block, pair, slots, slots,
            held, pltpu.VMEM((rows, width), F32), pltpu.VMEM((rows, width), F32), pltpu.VMEM((ROWS, width), F32),
            wide, pair, half, half, half, half,
            pltpu.VMEM((3 * WIDTH, width), BF), quarter, quarter, pltpu.VMEM((15, CUT, width), BF), pltpu.VMEM((CUT, width), BF),
            pltpu.VMEM((3, 8, WIDTH), F32), pltpu.VMEM((13, 8, WIDTH), F32),
        ]
        + sems(12 + 8 + 32 + 3 + 4 + 1 + 15 + 3 + 32 + 2 + 6 + 1 + 15 + 32 + 16 + 13 + 1),
        compiler_params=pltpu.CompilerParams(
            collective_id=2, has_side_effects=True, vmem_limit_bytes=60 * MIB
        ),
        cost_estimate=pl.CostEstimate(flops=12 * 10**9, bytes_accessed=100 * MIB, transcendentals=0),
        name="back",
    )(up_own, *up_passes, *up_fars, *up_nears, pick, residual, gain1, gain2, logs, out_grad, block_input, wall, w_qkv, joined, q, k, v, hall, down_own, *down_parts)


def hid_shift(rows, step):
    return lax.ppermute(rows, "hid", [(i, (i + step) % N_HID) for i in range(N_HID)])


def first_step(parts):
    (low1, high1, low2, high2, low3, high3) = parts
    fars = hid_shift(low3, 1), hid_shift(high3, -1)
    nears = hid_shift(high2, 1), hid_shift(low1, -1)
    return (low2, high1), fars, nears


def after(arrays, *first):
    return lax.optimization_barrier((arrays, first))[0]


def on_device(
    block_input, norm1_gain, norm1_bias, w_qkv, w_out, norm2_gain, norm2_bias,
    w_in, w_down, expert_ids, out_grad,
):
    gain1, bias1, gain2, bias2 = (
        v.reshape(1, WIDTH) for v in (norm1_gain, norm1_bias, norm2_gain, norm2_bias)
    )
    joined, q, k, v, hall, wall, logs, residual, pick, g0, g1, g2, rows = front_call(
        block_input, gain1, bias1, gain2, bias2, expert_ids.reshape(1, ROWS), out_grad, w_qkv, w_out
    )
    g3a = hid_shift(g1[0], 1)
    g3b = hid_shift(g2[1], -1)
    act, slope = hidden_call(rows, w_in)
    down_own, *down_parts = down_call(act, w_down)
    g3a, g3b = after((g3a, g3b), down_own)
    grad_pre, grads, up_own, *up_parts = expert_call(slope, (g0, g1, g2, g3a, g3b), w_in, w_down)
    up_passes, up_fars, up_nears = first_step(up_parts)
    d_w_in = jnp.einsum("lrd,lrf->ldf", rows, grad_pre, preferred_element_type=F32)
    d_w_down = jnp.einsum("lrf,lrd->lfd", act, grads, preferred_element_type=F32)
    up_fars, up_nears = after((up_fars, up_nears), d_w_in, d_w_down)
    output, grad_input, dw_qkv, dw_out, vec_sum = back_call(
        up_own, up_passes, up_fars, up_nears, pick, residual, gain1, gain2, logs, out_grad, block_input,
        wall, w_qkv, joined, q, k, v, hall, down_own, down_parts,
    )
    d_w_qkv = dw_qkv.reshape(w_qkv.shape).astype(F32)
    d_w_out = dw_out.astype(F32)
    return (
        output, grad_input, vec_sum[0], vec_sum[1], d_w_qkv, d_w_out,
        vec_sum[2], vec_sum[3], d_w_in, d_w_down,
    )


def solution(mesh):
    in_specs = (
        P(("exp", "hid"), None), P(), P(), P(None, None, "hid"), P("hid", None), P(), P(),
        P("exp", None, "hid"), P("exp", "hid", None), P(("exp", "hid"), None), P(("exp", "hid"), None),
    )
    out_specs = (
        P(("exp", "hid"), None), P(("exp", "hid"), None), P(), P(), P(None, None, "hid"), P("hid", None),
        P(), P(), P("exp", None, "hid"), P("exp", "hid", None),
    )
    return jax.shard_map(on_device, mesh=mesh, in_specs=in_specs, out_specs=out_specs, check_vma=False)
```

```python
import jax
import jax.numpy as jnp
from jax import lax
from jax.experimental import pallas as pl
from jax.experimental.pallas import tpu as pltpu
from jax.sharding import PartitionSpec as P

HD = 64
EPSILON = 1e-05
NEG_LARGE = -1e30
BF = jnp.bfloat16
F32 = jnp.float32
MESH = pl.DeviceIdType.MESH
ANY = pl.BlockSpec(memory_space=pl.ANY)
VMEM = pl.BlockSpec(memory_space=pltpu.VMEM)
N_HID = 4
N_EXP = 32
ROWS = 256
WIDTH = 1024
SLOTS = 512
MIB = 1 << 20


def dot(a, b):
    return jnp.dot(a, b, preferred_element_type=F32)


def dot_nt(a, b):
    return lax.dot_general(a, b, (((1,), (1,)), ((), ())), preferred_element_type=F32)


def dot_tn(a, b):
    return lax.dot_general(a, b, (((0,), (0,)), ((), ())), preferred_element_type=F32)


def place():
    return lax.axis_index("exp"), lax.axis_index("hid")


def hid_of(h, step):
    return lax.rem(h + step + N_HID, N_HID)


def exp_of(e, dz, dx, dc):
    z, x, c = e // 8, lax.rem(e // 2, 4), lax.rem(e, 2)
    return (lax.rem(z + dz, 4) * 4 + lax.rem(x + dx, 4)) * 2 + lax.rem(c + dc, 2)


def plane_steps(order):
    return [
        (dz, dx, dc)
        for dz in order
        for dx in (0, 1, 3, 2)
        for dc in (0, 1)
        if (dz, dx, dc) != (0, 0, 0)
    ]


def signal(peers):
    barrier = pltpu.get_barrier_semaphore()
    for peer in peers:
        pl.semaphore_signal(barrier, inc=1, device_id=peer, device_id_type=MESH)


def await_signals(peers):
    pl.semaphore_wait(pltpu.get_barrier_semaphore(), len(peers))


class Links:
    def __init__(self, send_sem, recv_sem):
        self.send_sem, self.recv_sem, self.used = send_sem, recv_sem, 0

    def remote(self, src, dst, peer):
        i = self.used
        self.used += 1
        copy = pltpu.make_async_remote_copy(
            src_ref=src,
            dst_ref=dst,
            send_sem=self.send_sem.at[i],
            recv_sem=self.recv_sem.at[i],
            device_id=peer,
            device_id_type=MESH,
        )
        copy.start()
        return copy

    def local(self, src, dst):
        i = self.used
        self.used += 1
        copy = pltpu.make_async_copy(src, dst, self.send_sem.at[i])
        copy.start()
        return copy


def rows_at(start, size, unit=16):
    return pl.ds(pl.multiple_of(start, unit), size)


def split_experts(block):
    n = block.shape[0] // 16
    wide = block.astype(F32).reshape(n, 2, 8, block.shape[1])
    return [wide[:, i].reshape(n * 8, block.shape[1]).astype(BF) for i in (0, 1)]


def merge_experts(first, second):
    n, width = first.shape[0] // 8, first.shape[1]
    pair = jnp.concatenate(
        [first.reshape(n, 1, 8, width), second.reshape(n, 1, 8, width)], axis=1
    )
    return pair.reshape(n * 16, width).astype(BF)


def norm_parts(rows):
    centered = rows - jnp.mean(rows, -1, keepdims=True)
    scale = lax.rsqrt(jnp.mean(centered * centered, -1, keepdims=True) + EPSILON)
    return centered * scale, scale


def norm_back(grad, hat, scale, gain):
    gh = grad * gain
    inner = jnp.mean(gh * hat, -1, keepdims=True)
    return scale * (gh - jnp.mean(gh, -1, keepdims=True) - hat * inner)


def slot_picks(ids):
    named = jnp.where(ids == lax.broadcasted_iota(jnp.int32, (128, ROWS), 0), 1.0, 0.0)
    earlier = jnp.where(
        lax.broadcasted_iota(jnp.int32, (ROWS, ROWS), 0)
        < lax.broadcasted_iota(jnp.int32, (ROWS, ROWS), 1),
        1.0,
        0.0,
    )
    running = dot(named.astype(BF), earlier.astype(BF))
    position = jnp.sum(running * named, axis=0, keepdims=True).astype(jnp.int32)
    slot = ids * 8 + position
    return jnp.where(slot == lax.broadcasted_iota(jnp.int32, (SLOTS, ROWS), 0), 1.0, 0.0).astype(BF)


def gather_begin(links, src, out, e, h):
    up, down = (e, hid_of(h, 1)), (e, hid_of(h, -1))
    mine = out.at[rows_at(h * ROWS, ROWS)]
    first = links.remote(src, mine, up)
    second = links.remote(src, mine, down)
    return first, second, links.local(src, mine)


def gather_relay(links, begun, out, e, h):
    up, down = (e, hid_of(h, 1)), (e, hid_of(h, -1))
    half = ROWS // 2
    first, second, own = begun
    first.wait_recv()
    piece = out.at[rows_at(hid_of(h, -1) * ROWS, half)]
    third = links.remote(piece, piece, up)
    second.wait_recv()
    piece = out.at[rows_at(hid_of(h, 1) * ROWS + half, half)]
    fourth = links.remote(piece, piece, down)
    return first, second, third, fourth, own


def gather_end(copies):
    first, second, third, fourth, own = copies
    own.wait()
    third.wait()
    fourth.wait()
    first.wait_send()
    second.wait_send()


def reduce_begin(links, term, got, half_up, half_down, e, h):
    up, down = (e, hid_of(h, 1)), (e, hid_of(h, -1))
    half = ROWS // 2
    far, above, below = hid_of(h, 2) * ROWS, hid_of(h, 1) * ROWS, hid_of(h, -1) * ROWS
    one = links.remote(term.at[rows_at(far, half)], half_up, up)
    two = links.remote(term.at[rows_at(far + half, half)], half_down, down)
    three = links.remote(term.at[rows_at(above + half, half)], got.at[0, pl.ds(half, half)], up)
    four = links.remote(term.at[rows_at(below, half)], got.at[1, pl.ds(0, half)], down)
    return one, two, three, four


def reduce_middle(links, begun, term, got, half_up, half_down, pass_up, pass_down, e, h):
    up, down = (e, hid_of(h, 1)), (e, hid_of(h, -1))
    half = ROWS // 2
    above, below = hid_of(h, 1) * ROWS, hid_of(h, -1) * ROWS
    one, two, three, four = begun
    one.wait_recv()
    pass_up[...] = (
        term[rows_at(above, half), :].astype(F32) + half_up[...].astype(F32)
    ).astype(BF)
    five = links.remote(pass_up, got.at[0, pl.ds(0, half)], up)
    two.wait_recv()
    pass_down[...] = (
        term[rows_at(below + half, half), :].astype(F32) + half_down[...].astype(F32)
    ).astype(BF)
    six = links.remote(pass_down, got.at[1, pl.ds(half, half)], down)
    return one, two, three, four, five, six


def reduce_end(copies, term, got, h):
    for copy in copies[2:]:
        copy.wait_recv()
    return (
        term[rows_at(h * ROWS, ROWS), :].astype(F32)
        + got[0].astype(F32)
        + got[1].astype(F32)
    )


def reduce_scratch():
    half = ROWS // 2
    return [pltpu.VMEM((2, ROWS, WIDTH), BF)] + [pltpu.VMEM((half, WIDTH), BF)] * 4


def sems(count):
    return [pltpu.SemaphoreType.DMA((count,)), pltpu.SemaphoreType.DMA((count,))]


def hid_peers(e, h):
    return [(e, hid_of(h, 1)), (e, hid_of(h, -1))]


def plane_peers(e, h):
    return [(exp_of(e, *step), h) for step in plane_steps((0, 1, 3, 2))]


def head_lanes(shape, head):
    return lax.broadcasted_iota(jnp.int32, shape, 1) // HD == head


def causal_tail(scores_t):
    keys, queries = scores_t.shape
    tail = scores_t[keys - queries :]
    allowed = lax.broadcasted_iota(jnp.int32, tail.shape, 0) <= lax.broadcasted_iota(
        jnp.int32, tail.shape, 1
    )
    tail = jnp.where(allowed, tail, NEG_LARGE)
    if keys == queries:
        return tail
    return jnp.concatenate([scores_t[: keys - queries], tail], axis=0)


def by_head(rows):
    return [
        jnp.where(head_lanes(rows.shape, head), rows, jnp.zeros_like(rows))
        for head in range(rows.shape[1] // HD)
    ]


def own_lanes(parts):
    whole = parts[0]
    for head in range(1, len(parts)):
        whole = jnp.where(head_lanes(whole.shape, head), parts[head], whole)
    return whole


def attend_block(block, q, k, v, heads, logs):
    keys, here = pl.ds(0, (block + 1) * ROWS), pl.ds(block * ROWS, ROWS)
    parts = []
    for head, query in enumerate(by_head(q[here, :] * BF(HD**-0.5))):
        scores = causal_tail(dot_nt(k[keys, :], query))
        top = jnp.max(scores, axis=0, keepdims=True)
        exps = jnp.exp(scores - top)
        summed = jnp.sum(exps, axis=0, keepdims=True)
        logs[head : head + 1, here] = top + jnp.log(summed)
        parts.append(dot_tn((exps * (1.0 / summed)).astype(BF), v[keys, :]))
    heads[here, :] = own_lanes(parts).astype(BF)


def attend_block_back(block, q, k, v, gheads, logs, gq, gk, gv):
    keys, here = pl.ds(0, (block + 1) * ROWS), pl.ds(block * ROWS, ROWS)
    queries, grads = by_head(q[here, :] * BF(HD**-0.5)), by_head(gheads[here, :])
    keys_t = k[keys, :].T
    parts, sum_v, sum_k = [], 0.0, 0.0
    for head, (query, grad) in enumerate(zip(queries, grads)):
        scores = causal_tail(dot_nt(k[keys, :], query))
        probs = jnp.exp(scores - logs[head : head + 1, here])
        weighted = probs * dot_nt(v[keys, :], grad)
        inner = jnp.sum(weighted, axis=0, keepdims=True)
        grad_scores = (weighted - probs * inner).astype(BF)
        sum_v = sum_v + dot(probs.astype(BF), grad)
        sum_k = sum_k + dot(grad_scores, query)
        parts.append(dot(keys_t[head * HD : (head + 1) * HD], grad_scores))
    gq[here, :] = (jnp.concatenate(parts, axis=0).T * HD**-0.5).astype(BF)
    gv[keys, :] += sum_v
    gk[keys, :] += sum_k


def front_kernel(
    x_ref, gain1_ref, bias1_ref, gain2_ref, bias2_ref, ids_ref, grad_hbm, wqkv_hbm, wout_hbm, win_hbm, wdown_hbm,
    joined_out, q_out, k_out, v_out, hall_out, wall_out, logs_ref, residual_ref, pick_ref,
    rows_out, grads_out, act_out, gpre_out, own_out, low_out, high_out, go_up_out, go_down_out,
    m_own_out, m_low_out, m_high_out, m_go_up_out, m_go_down_out,
    normed, joined, grad, wqkv, wout, wall, q, k, v, heads, hall,
    outgoing_g, landed_g, outgoing, landed, win, wdown, rows, grads, act, slope, gpre, back, mixed, send_sem, recv_sem,
):
    e, h = place()
    z, chip, core = e // 8, e // 2, lax.rem(e, 2)
    up, down, far = (e, hid_of(h, 1)), (e, hid_of(h, -1)), (e, hid_of(h, 2))
    peers = [up, down, far] + plane_peers(e, h)
    signal(peers)
    links = Links(send_sem, recv_sem)
    loads = [links.local(wout_hbm, wout), links.local(grad_hbm, grad), links.local(wqkv_hbm, wqkv)]
    weights = [links.local(win_hbm, win), links.local(wdown_hbm, wdown)]
    hat, _ = norm_parts(x_ref[...].astype(F32))
    normed[...] = (hat * gain1_ref[...] + bias1_ref[...]).astype(BF)
    await_signals(peers)
    gather = gather_begin(links, normed, joined, e, h)
    loads[0].wait()
    wall_at = (rows_at(chip * 16, 16), pl.ds(pl.multiple_of(core * 512, 512), 512))
    share, share_place = wout.at[wall_at], wall.at[(h,) + wall_at]
    wall_sends = [links.remote(share, share_place, peer) for peer in (up, down, far)]
    wall_kept = links.local(share, share_place)
    pick = slot_picks(ids_ref[...])
    pick_ref[...] = pick
    loads[1].wait()
    outgoing_g[...] = dot(pick, grad[...]).astype(BF)
    mine = landed_g.at[rows_at(e * 16, 16)]
    g_sends = []
    for step in plane_steps((0, 1, 3, 2)):
        t = exp_of(e, *step)
        g_sends.append(links.remote(outgoing_g.at[rows_at(t * 16, 16)], mine, (t, h)))
    g_kept = links.local(outgoing_g.at[rows_at(e * 16, 16)], mine)
    wall_kept.wait()
    for copy in wall_sends:
        copy.wait_recv()
    shares = wall.at[(slice(None),) + wall_at]
    wall_spread = [links.remote(shares, shares, peer) for peer in plane_peers(e, h)]

    def project(block):
        here = rows_at(block * ROWS, ROWS)
        block_rows = joined[here, :]
        for i, ref in enumerate((q, k, v)):
            ref[here, :] = dot(block_rows, wqkv[i]).astype(BF)

    gather[2].wait()
    loads[2].wait()
    project(h)
    gathered = gather_relay(links, gather, joined, e, h)
    project(hid_of(h, -1))
    project(hid_of(h, 1))
    g_kept.wait()
    for copy in g_sends:
        copy.wait_recv()
    for i in range(4):
        pair = split_experts(landed_g[pl.ds(i * 128, 128), :])
        for j in (0, 1):
            grads[j, pl.ds(i * 64, 64), :] = pair[j]

    def near(j):
        piece = grads.at[j, pl.ds(0, ROWS)]
        return [
            links.remote(piece, grads.at[j, pl.ds(ROWS, ROWS)], up),
            links.remote(piece, grads.at[j, pl.ds(2 * ROWS, ROWS)], down),
        ]

    g_near = near(0)
    outs = []
    for copy in gathered[2:4]:
        copy.wait_recv()
    project(hid_of(h, 2))
    outs += [links.local(src, dst) for src, dst in ((joined, joined_out), (q, q_out), (k, k_out), (v, v_out))]
    head_sends = []
    for peer in (far, up, down, (e, h)):
        for b in range(N_HID):

            @pl.when(peer[1] == b)
            def _(b=b):
                attend_block(b, q, k, v, heads, logs_ref)

        piece = heads.at[rows_at(peer[1] * ROWS, ROWS)]
        if peer[1] is h:
            head_own = links.local(piece, hall.at[h])
        else:
            head_sends.append(links.remote(piece, hall.at[h], peer))
    g_near += near(1)
    for copy in wall_spread:
        copy.wait_recv()
    outs.append(links.local(wall, wall_out))
    head_own.wait()
    for copy in head_sends:
        copy.wait_recv()
    outs.append(links.local(hall, hall_out))
    attn_sum = dot(hall[0], wall[0])
    for i in range(1, N_HID):
        attn_sum = attn_sum + dot(hall[i], wall[i])
    residual = x_ref[...].astype(F32) + attn_sum
    residual_ref[...] = residual
    hat, _ = norm_parts(residual)
    routed = (hat * gain2_ref[...] + bias2_ref[...]).astype(BF)
    outgoing[...] = dot(pick_ref[...], routed).astype(BF)
    mine = landed.at[rows_at(e * 16, 16)]
    order = (0, 1, 3, 2)
    sent = {}
    for dz in order:
        sent[dz] = []
        for step in plane_steps((dz,)):
            t = exp_of(e, *step)
            sent[dz].append(links.remote(outgoing.at[rows_at(t * 16, 16)], mine, (t, h)))
    kept = links.local(outgoing.at[rows_at(e * 16, 16)], mine)
    waits = []
    pending = None

    def relay(chunk):
        at, first, second = chunk
        first.wait_recv()
        third = links.remote(rows.at[0, rows_at(ROWS + at, 64)], rows.at[0, rows_at(3 * ROWS + at, 64)], up)
        second.wait_recv()
        fourth = links.remote(
            rows.at[1, rows_at(2 * ROWS + at, 64)], rows.at[1, rows_at(3 * ROWS + at, 64)], down
        )
        waits.extend((third, fourth))

    for dz in order:
        if dz == 0:
            kept.wait()
        for copy in sent[dz]:
            copy.wait_recv()
        from_z = lax.rem(z - dz + 4, 4)
        at = from_z * 64
        pair = split_experts(landed[rows_at(from_z * 128, 128), :])
        for j in (0, 1):
            rows[j, rows_at(at, 64), :] = pair[j]
        piece = rows.at[:, rows_at(at, 64)]
        first = links.remote(piece, rows.at[:, rows_at(ROWS + at, 64)], up)
        second = links.remote(piece, rows.at[:, rows_at(2 * ROWS + at, 64)], down)
        if pending is not None:
            relay(pending)
        pending = (at, first, second)
        sent[dz].extend((first, second))

    def hidden(expert, block):
        here = rows_at(block * ROWS, ROWS)
        pre = dot(rows[expert, here, :], win[expert])
        root = 0.7978845608028654
        square = pre * pre
        curve = jnp.tanh(pre * (root + (root * 0.044715) * square))
        half = 0.5 + 0.5 * curve
        active = pre * half
        act[expert, here, :] = active.astype(BF)
        slope[expert] = half + active * (1.0 - curve) * (root + (3 * 0.044715 * root) * square)

    def gradient(expert, block):
        here = rows_at(block * ROWS, ROWS)
        grad_act = dot_nt(grads[expert, here, :], wdown[expert])
        grad_pre = (grad_act * slope[expert]).astype(BF)
        gpre[expert, here, :] = grad_pre
        back[expert, here, :] = dot_nt(grad_pre, win[expert]).astype(BF)

    def both(first_block, count):
        def step(i, carry):
            expert, block = lax.rem(i, 2), first_block + i // 2
            hidden(expert, block)
            gradient(expert, block)
            return carry

        lax.fori_loop(0, 2 * count, step, 0)

    def forward(first_block, count):
        def step(i, carry):
            expert, here = lax.rem(i, 2), rows_at((first_block + i // 2) * ROWS, ROWS)
            mixed[expert, here, :] = dot(act[expert, here, :], wdown[expert]).astype(BF)
            return carry

        lax.fori_loop(0, 2 * count, step, 0)

    def far_step(i, carry):
        hidden(i, 3)
        return carry

    def far_back(i, carry):
        gradient(i, 3)
        return carry

    def deliver(src, places):
        for (expert, block), place in places:
            outs.append(links.local(src.at[expert, pl.ds(block * ROWS, ROWS)], place))

    def write(src, dst, first_block, count):
        piece = pl.ds(first_block * ROWS, count * ROWS)
        outs.append(links.local(src.at[:, piece], dst.at[:, piece]))

    for copy in weights:
        copy.wait()
    both(0, 1)
    forward(0, 1)
    relay(pending)
    for copy in g_near:
        copy.wait_recv()
    g_far = [
        links.remote(grads.at[0, pl.ds(ROWS, ROWS)], grads.at[0, pl.ds(3 * ROWS, ROWS)], up),
        links.remote(grads.at[1, pl.ds(2 * ROWS, ROWS)], grads.at[1, pl.ds(3 * ROWS, ROWS)], down),
    ]
    write(gpre, gpre_out, 0, 1)
    deliver(back, (((0, 0), own_out.at[0]), ((1, 0), own_out.at[1])))
    deliver(mixed, (((0, 0), m_own_out.at[0]), ((1, 0), m_own_out.at[1])))
    both(1, 2)
    write(rows, rows_out, 0, 3)
    write(grads, grads_out, 0, 3)
    write(gpre, gpre_out, 1, 2)
    deliver(
        back,
        (((0, 2), low_out), ((1, 1), high_out), ((1, 2), go_up_out.at[1]), ((0, 1), go_down_out.at[1])),
    )
    for copy in waits:
        copy.wait_recv()
    lax.fori_loop(0, 2, far_step, 0)
    write(rows, rows_out, 3, 1)
    write(act, act_out, 0, 4)
    forward(1, 3)
    deliver(
        mixed,
        (
            ((0, 2), m_low_out), ((1, 1), m_high_out), ((1, 2), m_go_up_out.at[1]), ((0, 1), m_go_down_out.at[1]),
            ((0, 3), m_go_up_out.at[0]), ((1, 3), m_go_down_out.at[0]),
        ),
    )
    for copy in g_far:
        copy.wait_recv()
    lax.fori_loop(0, 2, far_back, 0)
    write(grads, grads_out, 3, 1)
    write(gpre, gpre_out, 3, 1)
    deliver(back, (((0, 3), go_up_out.at[0]), ((1, 3), go_down_out.at[0])))
    for copy in outs:
        copy.wait()
    for dz in order:
        for copy in sent[dz]:
            copy.wait_send()
    for copy in list(gathered[:4]) + wall_sends + wall_spread + g_sends + head_sends + g_near + g_far + waits:
        copy.wait_send()


def front_call(block_input, gain1, bias1, gain2, bias2, ids, out_grad, w_qkv, w_out, w_in, w_down):
    rows, width = N_HID * ROWS, w_qkv.shape[2]
    flat = jax.ShapeDtypeStruct((rows, width), BF)
    pair = jax.ShapeDtypeStruct((2, ROWS, WIDTH), BF)
    shares = (N_HID, ROWS, WIDTH)
    held = pltpu.VMEM((rows, width), BF)
    slots = pltpu.VMEM((SLOTS, WIDTH), BF)
    block = pltpu.VMEM((ROWS, WIDTH), BF)
    one = jax.ShapeDtypeStruct((ROWS, WIDTH), BF)
    whole = jax.ShapeDtypeStruct((2, rows, WIDTH), BF)
    held_rows = pltpu.VMEM((2, rows, WIDTH), BF)
    weight = pltpu.VMEM(w_in.shape, BF)
    return pl.pallas_call(
        front_kernel,
        out_shape=(
            jax.ShapeDtypeStruct((rows, WIDTH), BF),
            flat, flat, flat,
            jax.ShapeDtypeStruct((N_HID, ROWS, width), BF),
            jax.ShapeDtypeStruct(shares, BF),
            jax.ShapeDtypeStruct((8, rows), F32),
            jax.ShapeDtypeStruct((ROWS, WIDTH), F32),
            jax.ShapeDtypeStruct((SLOTS, ROWS), BF),
            whole, whole, whole, whole,
            pair, one, one, pair, pair,
            pair, one, one, pair, pair,
        ),
        in_specs=[VMEM] * 6 + [ANY] * 5,
        out_specs=[ANY] * 6 + [VMEM] * 3 + [ANY] * 14,
        scratch_shapes=[
            block, pltpu.VMEM((rows, WIDTH), BF), block, pltpu.VMEM(w_qkv.shape, BF), block, pltpu.VMEM(shares, BF),
            held, held, held, held, pltpu.VMEM((N_HID, ROWS, width), BF),
            slots, slots, slots, slots, weight, weight, held_rows, held_rows, held_rows,
            pltpu.VMEM((2, ROWS, WIDTH), F32), held_rows, held_rows, held_rows,
        ]
        + sems(5 + 5 + 4 + 32 + 31 + 4 + 2 + 4 + 4 + 2 + 32 + 16 + 30),
        compiler_params=pltpu.CompilerParams(
            collective_id=1, has_side_effects=True, vmem_limit_bytes=62 * MIB
        ),
        cost_estimate=pl.CostEstimate(flops=20 * 10**9, bytes_accessed=100 * MIB, transcendentals=0),
        name="front",
    )(block_input, gain1, bias1, gain2, bias2, ids, out_grad, w_qkv, w_out, w_in, w_down)


def weights_kernel(rows_ref, gpre_ref, act_ref, grads_ref, dwin_ref, dwdown_ref):
    dwin_ref[0] = dot_tn(rows_ref[0], gpre_ref[0])
    dwdown_ref[0] = dot_tn(act_ref[0], grads_ref[0])


def weights_call(rows, grad_pre, act, grads):
    half = WIDTH // 2
    whole = pl.BlockSpec((1, WIDTH, WIDTH), lambda i, j: (i, 0, 0))
    columns = pl.BlockSpec((1, WIDTH, half), lambda i, j: (i, 0, j))
    result = jax.ShapeDtypeStruct(rows.shape, F32)
    return pl.pallas_call(
        weights_kernel,
        grid=(2, 2),
        out_shape=(result, result),
        in_specs=[whole, columns, columns, whole],
        out_specs=[columns, pl.BlockSpec((1, half, WIDTH), lambda i, j: (i, j, 0))],
        compiler_params=pltpu.CompilerParams(vmem_limit_bytes=60 * MIB),
        cost_estimate=pl.CostEstimate(flops=86 * 10**8, bytes_accessed=32 * MIB, transcendentals=0),
        name="weights",
    )(rows, grad_pre, act, grads)


CHIPS = [(dz, dx, 0) for dz in (0, 1, 3, 2) for dx in (0, 1, 3, 2) if (dz, dx) != (0, 0)]
CUT = 96


def back_kernel(
    up_own, up_pass_up, up_pass_down, up_below, up_above,
    pick_ref, residual_ref, gain1_ref, gain2_ref, logs_ref,
    grad_hbm, x_hbm, wall_hbm, wqkv_hbm, joined_hbm, q_hbm, k_hbm, v_hbm, hall_hbm,
    m_own_hbm, m_low_hbm, m_high_hbm, m_go_up, m_go_down,
    out_ref, ginput_ref, dwq_ref, dwo_ref, vecsum_ref,
    grad_in, x, wall, wqkv, joined, q, k, v, hall, m_own, m_pass_up, m_pass_down,
    pass_up, pass_down, got, outgoing, landed, gres, gas, gheads_out, gheads,
    dwo, dwo_got, dwo_half, dwo_pieces, dwo_sum, dwo_hid, dwo_part,
    m_far_up, m_far_down, m_near_up, m_near_down, m_got, m_outgoing, m_landed,
    gq, gk, gv, term, t_got, half_up, half_down, t_pass_up, t_pass_down,
    dwq, dwq_got, dwq_half, dwq_pieces, dwq_sum, vec, vec_got, send_sem, recv_sem,
):
    e, h = place()
    z, chip, core = e // 8, e // 2, lax.rem(e, 2)
    up, down, far = (e, hid_of(h, 1)), (e, hid_of(h, -1)), (e, hid_of(h, 2))
    twin = (exp_of(e, 0, 0, 1), h)
    across = [(exp_of(e, *step), h) for step in CHIPS]
    plane = plane_peers(e, h)
    peers = [up, down, far] + plane
    peers += [(exp_of(e, dz, 0, 0), hid_of(h, dy)) for dz in (1, 2, 3) for dy in (1, 2, 3)]
    signal(peers)
    links = Links(send_sem, recv_sem)
    load = {}
    for name, src, dst in (
        ("grad", grad_hbm, grad_in), ("wall", wall_hbm, wall), ("hall", hall_hbm, hall), ("q", q_hbm, q), ("k", k_hbm, k),
        ("v", v_hbm, v), ("wqkv", wqkv_hbm, wqkv), ("joined", joined_hbm, joined), ("x", x_hbm, x),
        ("m", m_own_hbm, m_own), ("mu", m_low_hbm, m_pass_up), ("md", m_high_hbm, m_pass_down),
    ):
        load[name] = links.local(src, dst)
    await_signals(peers)
    ended = []
    order = (2, 1, 3, 0)
    passed = []
    for dz in order:
        at = lax.rem(z + dz, 4) * 64
        piece = rows_at(at, 64)
        pass_up[piece, :] = (up_pass_up[piece, :].astype(F32) + up_below[0, piece, :].astype(F32)).astype(BF)
        five = links.remote(pass_up.at[piece], got.at[0, piece], up)
        pass_down[piece, :] = (up_pass_down[piece, :].astype(F32) + up_above[0, piece, :].astype(F32)).astype(BF)
        six = links.remote(pass_down.at[piece], got.at[1, piece], down)
        passed.append((at, five, six))
        ended += [five, six]
    m_far = [links.remote(m_go_up.at[0], m_far_up, up), links.remote(m_go_down.at[0], m_far_down, down)]
    ended += m_far
    mine = landed.at[rows_at(e * 16, 16)]
    back = []
    for dz, (at, five, six) in zip(order, passed):
        five.wait_recv()
        six.wait_recv()
        piece = rows_at(at, 64)
        pair = [
            up_own[j, piece, :].astype(F32) + got[j, piece, :].astype(F32) + near[1, piece, :].astype(F32)
            for j, near in enumerate((up_above, up_below))
        ]
        outgoing[rows_at(at * 2, 128), :] = merge_experts(*pair)
        for step in plane_steps((dz,)):
            t = exp_of(e, *step)
            back.append(links.remote(outgoing.at[rows_at(t * 16, 16)], mine, (t, h)))
    kept = links.local(outgoing.at[rows_at(e * 16, 16)], mine)
    kept.wait()
    load["grad"].wait()
    load["wall"].wait()
    load["hall"].wait()
    for copy in back:
        copy.wait_recv()
    ended += back
    routed = dot_tn(pick_ref[...], landed[...])
    hat, scale = norm_parts(residual_ref[...])
    vec[0] = jnp.zeros_like(vec[0])
    vec[0, 2:3, :] = jnp.sum(routed * hat, axis=0, keepdims=True)
    vec[0, 3:4, :] = jnp.sum(routed, axis=0, keepdims=True)
    whole = grad_in[...].astype(F32) + norm_back(routed, hat, scale, gain2_ref[...])
    gres[...] = whole
    gas[...] = whole.astype(BF)
    head_sends = []
    for i, peer in enumerate((far, up, down)):
        gheads_out[i] = dot_nt(gas[...], wall[peer[1]]).astype(BF)
        head_sends.append(links.remote(gheads_out.at[i], gheads.at[rows_at(h * ROWS, ROWS)], peer))
    ended += head_sends
    gheads[rows_at(h * ROWS, ROWS), :] = dot_nt(gas[...], wall[h]).astype(BF)
    m_near = [links.remote(m_go_up.at[1], m_near_up, up), links.remote(m_go_down.at[1], m_near_down, down)]
    ended += m_near
    for i in range(N_HID):
        dwo[i] = dot_tn(hall[i], gas[...]).astype(BF)
    other = pl.ds(pl.multiple_of((1 - core) * 512, 512), 512)
    own = pl.ds(pl.multiple_of(core * 512, 512), 512)
    dwo_swap = links.remote(dwo.at[:, :, other], dwo_got, twin)
    ended.append(dwo_swap)
    for name in ("q", "k", "v"):
        load[name].wait()
    for copy in head_sends:
        copy.wait_recv()
    gk[...] = jnp.zeros_like(gk)
    gv[...] = jnp.zeros_like(gv)

    def attention(block):
        attend_block_back(block, q, k, v, gheads, logs_ref, gq, gk, gv)

    attention(0)
    attention(1)
    load["mu"].wait()
    load["md"].wait()
    m_far[0].wait_recv()
    m_pass_up[...] = (m_pass_up[...].astype(F32) + m_far_up[...].astype(F32)).astype(BF)
    five = links.remote(m_pass_up, m_got.at[0], up)
    m_far[1].wait_recv()
    m_pass_down[...] = (m_pass_down[...].astype(F32) + m_far_down[...].astype(F32)).astype(BF)
    six = links.remote(m_pass_down, m_got.at[1], down)
    ended += [five, six]
    dwo_swap.wait_recv()
    for i in range(N_HID):
        dwo_half[i] = (dwo[i, :, own].astype(F32) + dwo_got[i].astype(F32)).astype(BF)
    dwo_spread = [
        links.remote(dwo_half.at[:, rows_at(peer[0] // 2 * 16, 16)], dwo_pieces.at[i], peer)
        for i, peer in enumerate(across)
    ]
    ended += dwo_spread
    attention(2)
    for copy in dwo_spread:
        copy.wait_recv()
    whole = dwo_half[:, rows_at(chip * 16, 16), :].astype(F32)
    for i in range(len(across)):
        whole = whole + dwo_pieces[i].astype(F32)
    dwo_sum[...] = whole.astype(BF)
    dwo_cross = [
        links.remote(dwo_sum.at[peer[1]], dwo_hid.at[i], peer) for i, peer in enumerate((far, up, down))
    ]
    ended += dwo_cross
    attention(3)
    for copy in dwo_cross:
        copy.wait_recv()
    whole = dwo_sum[h].astype(F32)
    for i in range(3):
        whole = whole + dwo_hid[i].astype(F32)
    dwo_part[...] = whole.astype(BF)
    dwo_place = dwo_ref.at[rows_at(chip * 16, 16), own]
    dwo_share = [links.remote(dwo_part, dwo_place, peer) for peer in plane]
    ended += dwo_share
    dwo_own = links.local(dwo_part, dwo_place)
    load["m"].wait()
    for copy in m_near:
        copy.wait_recv()
    five.wait_recv()
    six.wait_recv()
    for i in range(4):
        piece = pl.ds(i * 64, 64)
        pair = [
            m_own[j, piece, :].astype(F32) + m_got[j, piece, :].astype(F32) + near[piece, :].astype(F32)
            for j, near in enumerate((m_near_down, m_near_up))
        ]
        m_outgoing[pl.ds(i * 128, 128), :] = merge_experts(*pair)
    mine = m_landed.at[rows_at(e * 16, 16)]
    m_back = []
    for step in plane_steps((2, 1, 3, 0)):
        t = exp_of(e, *step)
        m_back.append(links.remote(m_outgoing.at[rows_at(t * 16, 16)], mine, (t, h)))
    m_kept = links.local(m_outgoing.at[rows_at(e * 16, 16)], mine)
    ended += m_back
    load["wqkv"].wait()
    load["joined"].wait()
    parts = (gq[...], gk[...].astype(BF), gv[...].astype(BF))
    term[...] = sum(dot_nt(part, wqkv[i]) for i, part in enumerate(parts)).astype(BF)
    begun = reduce_begin(links, term, t_got, half_up, half_down, e, h)
    for i, part in enumerate(parts):
        dwq[pl.ds(i * WIDTH, WIDTH), :] = dot_tn(joined[...], part).astype(BF)
    count = dwq.shape[0] // 2
    dwq_swap = links.remote(dwq.at[rows_at((1 - core) * count, count)], dwq_got, twin)
    ended.append(dwq_swap)
    reduced = reduce_middle(links, begun, term, t_got, half_up, half_down, t_pass_up, t_pass_down, e, h)
    ended += reduced
    dwq_swap.wait_recv()
    dwq_half[...] = (dwq[rows_at(core * count, count), :].astype(F32) + dwq_got[...].astype(F32)).astype(BF)
    dwq_spread = [
        links.remote(dwq_half.at[rows_at(peer[0] // 2 * CUT, CUT)], dwq_pieces.at[i], peer)
        for i, peer in enumerate(across)
    ]
    ended += dwq_spread
    load["x"].wait()
    grad = reduce_end(reduced, term, t_got, h)
    hat, scale = norm_parts(x[...].astype(F32))
    ginput_ref[...] = gres[...] + norm_back(grad, hat, scale, gain1_ref[...])
    vec[0, 0:1, :] = jnp.sum(grad * hat, axis=0, keepdims=True)
    vec[0, 1:2, :] = jnp.sum(grad, axis=0, keepdims=True)
    rounds = (
        [(exp_of(e, dz, 0, 0), hid_of(h, dy)) for dz in range(4) for dy in range(4) if (dz, dy) != (0, 0)],
        [(exp_of(e, 0, dx, dc), h) for dx in range(4) for dc in (0, 1) if (dx, dc) != (0, 0)],
    )
    slot = 0
    copies = [links.remote(vec.at[0], vec_got.at[slot + i], peer) for i, peer in enumerate(rounds[0])]
    for copy in dwq_spread:
        copy.wait_recv()
    whole = dwq_half[rows_at(chip * CUT, CUT), :].astype(F32)
    for i in range(len(across)):
        whole = whole + dwq_pieces[i].astype(F32)
    dwq_sum[...] = whole.astype(BF)
    dwq_place = dwq_ref.at[rows_at(core * count + chip * CUT, CUT)]
    dwq_share = [links.remote(dwq_sum, dwq_place, peer) for peer in across]
    ended += dwq_share
    dwq_own = links.local(dwq_sum, dwq_place)
    for number in range(2):
        for copy in copies:
            copy.wait_recv()
        whole = vec[number]
        for i in range(len(rounds[number])):
            whole = whole + vec_got[slot + i]
        slot += len(rounds[number])
        ended += copies
        if number < 1:
            vec[number + 1] = whole
            copies = [
                links.remote(vec.at[number + 1], vec_got.at[slot + i], peer)
                for i, peer in enumerate(rounds[number + 1])
            ]
        else:
            vecsum_ref[...] = whole
    m_kept.wait()
    for copy in m_back:
        copy.wait_recv()
    out_ref[...] = (residual_ref[...] + dot_tn(pick_ref[...], m_landed[...])).astype(BF)
    dwq_own.wait()
    for copy in dwq_share:
        copy.wait_recv()
    both = dwq_ref.at[rows_at(core * count, count)]
    twins = links.remote(both, both, twin)
    dwo_own.wait()
    for copy in dwo_share:
        copy.wait_recv()
    twins.wait()
    for copy in ended:
        copy.wait_send()


def back_call(up_parts, pick, residual, gain1, gain2, logs, out_grad, block_input, wall, w_qkv, joined, q, k, v, hall, down_parts):
    rows, width = q.shape
    block = pltpu.VMEM((ROWS, WIDTH), BF)
    half = pltpu.VMEM((ROWS // 2, WIDTH), BF)
    pair = pltpu.VMEM((2, ROWS, WIDTH), BF)
    slots = pltpu.VMEM((SLOTS, WIDTH), BF)
    held = pltpu.VMEM((rows, width), BF)
    wide = pltpu.VMEM((rows, WIDTH), BF)
    shares = pltpu.VMEM((N_HID, ROWS, WIDTH), BF)
    half_shares = pltpu.VMEM((N_HID, ROWS, WIDTH // 2), BF)
    quarter = pltpu.VMEM((3 * WIDTH // 2, width), BF)
    return pl.pallas_call(
        back_kernel,
        out_shape=(
            jax.ShapeDtypeStruct((ROWS, WIDTH), BF),
            jax.ShapeDtypeStruct((ROWS, WIDTH), F32),
            jax.ShapeDtypeStruct((3 * WIDTH, width), BF),
            jax.ShapeDtypeStruct((ROWS, WIDTH), BF),
            jax.ShapeDtypeStruct((8, WIDTH), F32),
        ),
        in_specs=[VMEM] * 10 + [ANY] * 14,
        out_specs=[VMEM] * 5,
        scratch_shapes=[
            block, block, shares, pltpu.VMEM(w_qkv.shape, BF), wide, held, held, held,
            pltpu.VMEM((N_HID, ROWS, width), BF), pair, block, block,
            block, block, pair, slots, slots, pltpu.VMEM((ROWS, WIDTH), F32), block,
            pltpu.VMEM((3, ROWS, width), BF), held,
            shares, half_shares, half_shares, pltpu.VMEM((15, N_HID, 16, WIDTH // 2), BF),
            pltpu.VMEM((N_HID, 16, WIDTH // 2), BF), pltpu.VMEM((3, 16, WIDTH // 2), BF), pltpu.VMEM((16, WIDTH // 2), BF),
            block, block, block, block, pair, slots, slots,
            held, pltpu.VMEM((rows, width), F32), pltpu.VMEM((rows, width), F32),
            wide, pair, half, half, half, half,
            pltpu.VMEM((3 * WIDTH, width), BF), quarter, quarter, pltpu.VMEM((15, CUT, width), BF), pltpu.VMEM((CUT, width), BF),
            pltpu.VMEM((2, 8, WIDTH), F32), pltpu.VMEM((22, 8, WIDTH), F32),
        ]
        + sems(12 + 8 + 32 + 3 + 4 + 1 + 15 + 3 + 32 + 2 + 6 + 1 + 15 + 32 + 16 + 22 + 1),
        compiler_params=pltpu.CompilerParams(
            collective_id=2, has_side_effects=True, vmem_limit_bytes=62 * MIB
        ),
        cost_estimate=pl.CostEstimate(flops=12 * 10**9, bytes_accessed=100 * MIB, transcendentals=0),
        name="back",
    )(*up_parts, pick, residual, gain1, gain2, logs, out_grad, block_input, wall, w_qkv, joined, q, k, v, hall, *down_parts)


def hid_shift(rows, step):
    return lax.ppermute(rows, "hid", [(i, (i + step) % N_HID) for i in range(N_HID)])


def after(arrays, *first):
    return lax.optimization_barrier((arrays, first))[0]


def on_device(
    block_input, norm1_gain, norm1_bias, w_qkv, w_out, norm2_gain, norm2_bias,
    w_in, w_down, expert_ids, out_grad,
):
    gain1, bias1, gain2, bias2 = (
        v.reshape(1, WIDTH) for v in (norm1_gain, norm1_bias, norm2_gain, norm2_bias)
    )
    (
        joined, q, k, v, hall, wall, logs, residual, pick,
        rows, grads, act, grad_pre, up_own, up_low, up_high, go_up, go_down, *down_parts,
    ) = front_call(
        block_input, gain1, bias1, gain2, bias2, expert_ids.reshape(1, ROWS), out_grad, w_qkv, w_out, w_in, w_down
    )
    below, above = hid_shift(go_up, 1), hid_shift(go_down, -1)
    d_w_in, d_w_down = weights_call(rows, grad_pre, act, grads)
    below, above = after((below, above), d_w_in, d_w_down)
    output, grad_input, dw_qkv, dw_out, vec_sum = back_call(
        (up_own, up_low, up_high, below, above), pick, residual, gain1, gain2, logs, out_grad, block_input,
        wall, w_qkv, joined, q, k, v, hall, down_parts,
    )
    d_w_qkv = dw_qkv.reshape(w_qkv.shape).astype(F32)
    d_w_out = dw_out.astype(F32)
    return (
        output, grad_input, vec_sum[0], vec_sum[1], d_w_qkv, d_w_out,
        vec_sum[2], vec_sum[3], d_w_in, d_w_down,
    )


def solution(mesh):
    in_specs = (
        P(("exp", "hid"), None), P(), P(), P(None, None, "hid"), P("hid", None), P(), P(),
        P("exp", None, "hid"), P("exp", "hid", None), P(("exp", "hid"), None), P(("exp", "hid"), None),
    )
    out_specs = (
        P(("exp", "hid"), None), P(("exp", "hid"), None), P(), P(), P(None, None, "hid"), P("hid", None),
        P(), P(), P("exp", None, "hid"), P("exp", "hid", None),
    )
    return jax.shard_map(on_device, mesh=mesh, in_specs=in_specs, out_specs=out_specs, check_vma=False)
```

```python
import jax
import jax.numpy as jnp
from jax import lax
from jax.experimental import pallas as pl
from jax.experimental.pallas import tpu as pltpu
from jax.sharding import PartitionSpec as P

HD = 64
EPSILON = 1e-05
NEG_LARGE = -1e30
BF = jnp.bfloat16
F32 = jnp.float32
MESH = pl.DeviceIdType.MESH
ANY = pl.BlockSpec(memory_space=pl.ANY)
VMEM = pl.BlockSpec(memory_space=pltpu.VMEM)
N_HID = 4
N_EXP = 32
ROWS = 256
WIDTH = 1024
SLOTS = 512
MIB = 1 << 20


def dot(a, b):
    return jnp.dot(a, b, preferred_element_type=F32)


def dot_nt(a, b):
    return lax.dot_general(a, b, (((1,), (1,)), ((), ())), preferred_element_type=F32)


def dot_tn(a, b):
    return lax.dot_general(a, b, (((0,), (0,)), ((), ())), preferred_element_type=F32)


def place():
    return lax.axis_index("exp"), lax.axis_index("hid")


def hid_of(h, step):
    return lax.rem(h + step + N_HID, N_HID)


def exp_of(e, dz, dx, dc):
    z, x, c = e // 8, lax.rem(e // 2, 4), lax.rem(e, 2)
    return (lax.rem(z + dz, 4) * 4 + lax.rem(x + dx, 4)) * 2 + lax.rem(c + dc, 2)


def plane_steps(order):
    return [
        (dz, dx, dc)
        for dz in order
        for dx in (0, 1, 3, 2)
        for dc in (0, 1)
        if (dz, dx, dc) != (0, 0, 0)
    ]


def signal(peers):
    barrier = pltpu.get_barrier_semaphore()
    for peer in peers:
        pl.semaphore_signal(barrier, inc=1, device_id=peer, device_id_type=MESH)


def await_signals(peers):
    pl.semaphore_wait(pltpu.get_barrier_semaphore(), len(peers))


class Links:
    def __init__(self, send_sem, recv_sem):
        self.send_sem, self.recv_sem, self.used = send_sem, recv_sem, 0

    def remote(self, src, dst, peer):
        i = self.used
        self.used += 1
        copy = pltpu.make_async_remote_copy(
            src_ref=src,
            dst_ref=dst,
            send_sem=self.send_sem.at[i],
            recv_sem=self.recv_sem.at[i],
            device_id=peer,
            device_id_type=MESH,
        )
        copy.start()
        return copy

    def local(self, src, dst):
        i = self.used
        self.used += 1
        copy = pltpu.make_async_copy(src, dst, self.send_sem.at[i])
        copy.start()
        return copy


def rows_at(start, size, unit=16):
    return pl.ds(pl.multiple_of(start, unit), size)


def split_experts(block):
    n = block.shape[0] // 16
    wide = block.astype(F32).reshape(n, 2, 8, block.shape[1])
    return [wide[:, i].reshape(n * 8, block.shape[1]).astype(BF) for i in (0, 1)]


def merge_experts(first, second):
    n, width = first.shape[0] // 8, first.shape[1]
    pair = jnp.concatenate(
        [first.reshape(n, 1, 8, width), second.reshape(n, 1, 8, width)], axis=1
    )
    return pair.reshape(n * 16, width).astype(BF)


def norm_parts(rows):
    centered = rows - jnp.mean(rows, -1, keepdims=True)
    scale = lax.rsqrt(jnp.mean(centered * centered, -1, keepdims=True) + EPSILON)
    return centered * scale, scale


def norm_back(grad, hat, scale, gain):
    gh = grad * gain
    inner = jnp.mean(gh * hat, -1, keepdims=True)
    return scale * (gh - jnp.mean(gh, -1, keepdims=True) - hat * inner)


def slot_picks(ids):
    named = jnp.where(ids == lax.broadcasted_iota(jnp.int32, (128, ROWS), 0), 1.0, 0.0)
    earlier = jnp.where(
        lax.broadcasted_iota(jnp.int32, (ROWS, ROWS), 0)
        < lax.broadcasted_iota(jnp.int32, (ROWS, ROWS), 1),
        1.0,
        0.0,
    )
    running = dot(named.astype(BF), earlier.astype(BF))
    position = jnp.sum(running * named, axis=0, keepdims=True).astype(jnp.int32)
    slot = ids * 8 + position
    return jnp.where(slot == lax.broadcasted_iota(jnp.int32, (SLOTS, ROWS), 0), 1.0, 0.0).astype(BF)


def gather_begin(links, src, out, e, h):
    half = ROWS // 2
    copies = []
    for first, peer in ((0, (e, hid_of(h, 1))), (half, (e, hid_of(h, -1)))):
        for start in (first, half - first):
            piece = out.at[rows_at(h * ROWS + start, half)]
            copies.append(links.remote(src.at[pl.ds(start, half)], piece, peer))
    return copies, links.local(src, out.at[rows_at(h * ROWS, ROWS)])


def gather_relay(links, copies, out, e, h):
    half = ROWS // 2
    relayed = []
    for copy, block, start, peer in (
        (copies[0], hid_of(h, -1), 0, (e, hid_of(h, 1))),
        (copies[2], hid_of(h, 1), half, (e, hid_of(h, -1))),
    ):
        copy.wait_recv()
        piece = out.at[rows_at(block * ROWS + start, half)]
        relayed.append(links.remote(piece, piece, peer))
    return relayed


def reduce_begin(links, term, got, half_up, half_down, e, h):
    up, down = (e, hid_of(h, 1)), (e, hid_of(h, -1))
    half = ROWS // 2
    far, above, below = hid_of(h, 2) * ROWS, hid_of(h, 1) * ROWS, hid_of(h, -1) * ROWS
    one = links.remote(term.at[rows_at(far, half)], half_up, up)
    two = links.remote(term.at[rows_at(far + half, half)], half_down, down)
    three = links.remote(term.at[rows_at(above + half, half)], got.at[0, pl.ds(half, half)], up)
    four = links.remote(term.at[rows_at(below, half)], got.at[1, pl.ds(0, half)], down)
    return one, two, three, four


def reduce_middle(links, begun, term, got, half_up, half_down, pass_up, pass_down, e, h):
    up, down = (e, hid_of(h, 1)), (e, hid_of(h, -1))
    half = ROWS // 2
    above, below = hid_of(h, 1) * ROWS, hid_of(h, -1) * ROWS
    one, two, three, four = begun
    one.wait_recv()
    pass_up[...] = (
        term[rows_at(above, half), :].astype(F32) + half_up[...].astype(F32)
    ).astype(BF)
    five = links.remote(pass_up, got.at[0, pl.ds(0, half)], up)
    two.wait_recv()
    pass_down[...] = (
        term[rows_at(below + half, half), :].astype(F32) + half_down[...].astype(F32)
    ).astype(BF)
    six = links.remote(pass_down, got.at[1, pl.ds(half, half)], down)
    return one, two, three, four, five, six


def reduce_end(copies, term, got, h):
    for copy in copies[2:]:
        copy.wait_recv()
    return (
        term[rows_at(h * ROWS, ROWS), :].astype(F32)
        + got[0].astype(F32)
        + got[1].astype(F32)
    )


def reduce_scratch():
    half = ROWS // 2
    return [pltpu.VMEM((2, ROWS, WIDTH), BF)] + [pltpu.VMEM((half, WIDTH), BF)] * 4


def sems(count):
    return [pltpu.SemaphoreType.DMA((count,)), pltpu.SemaphoreType.DMA((count,))]


def hid_peers(e, h):
    return [(e, hid_of(h, 1)), (e, hid_of(h, -1))]


def plane_peers(e, h):
    return [(exp_of(e, *step), h) for step in plane_steps((0, 1, 3, 2))]


def head_lanes(shape, head):
    return lax.broadcasted_iota(jnp.int32, shape, 1) // HD == head


def causal_tail(scores_t):
    keys, queries = scores_t.shape
    tail = scores_t[keys - queries :]
    allowed = lax.broadcasted_iota(jnp.int32, tail.shape, 0) <= lax.broadcasted_iota(
        jnp.int32, tail.shape, 1
    )
    tail = jnp.where(allowed, tail, NEG_LARGE)
    if keys == queries:
        return tail
    return jnp.concatenate([scores_t[: keys - queries], tail], axis=0)


def by_head(rows):
    return [
        jnp.where(head_lanes(rows.shape, head), rows, jnp.zeros_like(rows))
        for head in range(rows.shape[1] // HD)
    ]


def own_lanes(parts):
    whole = parts[0]
    for head in range(1, len(parts)):
        whole = jnp.where(head_lanes(whole.shape, head), parts[head], whole)
    return whole


def attend_block(block, q, k, v, heads, logs):
    keys, here = pl.ds(0, (block + 1) * ROWS), pl.ds(block * ROWS, ROWS)
    parts = []
    for head, query in enumerate(by_head(q[here, :] * BF(HD**-0.5))):
        scores = causal_tail(dot_nt(k[keys, :], query))
        top = jnp.max(scores, axis=0, keepdims=True)
        exps = jnp.exp(scores - top)
        summed = jnp.sum(exps, axis=0, keepdims=True)
        logs[head : head + 1, here] = top + jnp.log(summed)
        parts.append(dot_tn((exps * (1.0 / summed)).astype(BF), v[keys, :]))
    heads[here, :] = own_lanes(parts).astype(BF)


def attend_block_back(block, q, k, v, gheads, logs, gq, gk, gv):
    keys, here = pl.ds(0, (block + 1) * ROWS), pl.ds(block * ROWS, ROWS)
    queries, grads = by_head(q[here, :] * BF(HD**-0.5)), by_head(gheads[here, :])
    keys_t = k[keys, :].T
    parts, sum_v, sum_k = [], 0.0, 0.0
    for head, (query, grad) in enumerate(zip(queries, grads)):
        scores = causal_tail(dot_nt(k[keys, :], query))
        probs = jnp.exp(scores - logs[head : head + 1, here])
        weighted = probs * dot_nt(v[keys, :], grad)
        inner = jnp.sum(weighted, axis=0, keepdims=True)
        grad_scores = (weighted - probs * inner).astype(BF)
        sum_v = sum_v + dot(probs.astype(BF), grad)
        sum_k = sum_k + dot(grad_scores, query)
        parts.append(dot(keys_t[head * HD : (head + 1) * HD], grad_scores))
    gq[here, :] = (jnp.concatenate(parts, axis=0).T * HD**-0.5).astype(BF)
    gv[keys, :] += sum_v
    gk[keys, :] += sum_k


def front_kernel(
    x_ref, gain1_ref, bias1_ref, gain2_ref, bias2_ref, ids_ref, grad_hbm, wqkv_hbm, wout_hbm, win_hbm, wdown_hbm,
    joined_out, q_out, k_out, v_out, hall_out, wall_out, logs_ref, residual_ref, pick_ref,
    rows_out, grads_out, act_out, gpre_out, own_out, low_out, high_out, go_up_out, go_down_out, near_below_out, near_above_out,
    m_own_out, m_low_out, m_high_out, m_go_up_out, m_go_down_out,
    normed, joined, grad, wqkv, wout, wall, q, k, v, heads, hall,
    outgoing_g, landed_g, outgoing, landed, win, wdown, rows, grads, act, slope, gpre, back, mixed, send_sem, recv_sem,
):
    e, h = place()
    z, x_at, core = e // 8, lax.rem(e // 2, 4), lax.rem(e, 2)
    up, down, far = (e, hid_of(h, 1)), (e, hid_of(h, -1)), (e, hid_of(h, 2))
    peers = [up, down, far] + plane_peers(e, h)
    signal(peers)
    links = Links(send_sem, recv_sem)
    loads = [links.local(wout_hbm, wout), links.local(grad_hbm, grad), links.local(wqkv_hbm, wqkv)]
    weights = [links.local(win_hbm, win), links.local(wdown_hbm, wdown)]
    hat, _ = norm_parts(x_ref[...].astype(F32))
    normed[...] = (hat * gain1_ref[...] + bias1_ref[...]).astype(BF)
    await_signals(peers)
    gather, gather_own = gather_begin(links, normed, joined, e, h)
    loads[0].wait()
    columns = pl.ds(pl.multiple_of(core * 512, 512), 512)
    along_z, along_x = x_at * 64 + z * 16, z * 64 + x_at * 16
    turned = h // 2
    wall_row = rows_at(along_z * (1 - turned) + along_x * turned, 16)
    share, share_place = wout.at[wall_row, columns], wall.at[h, wall_row, columns]
    wall_sends = [links.remote(share, share_place, peer) for peer in (up, down, far)]
    wall_kept = links.local(share, share_place)
    pick = slot_picks(ids_ref[...])
    pick_ref[...] = pick
    loads[1].wait()
    outgoing_g[...] = dot(pick, grad[...]).astype(BF)
    mine = landed_g.at[rows_at(e * 16, 16)]
    g_sends = []
    for step in plane_steps((0, 1, 3, 2)):
        t = exp_of(e, *step)
        g_sends.append(links.remote(outgoing_g.at[rows_at(t * 16, 16)], mine, (t, h)))
    g_kept = links.local(outgoing_g.at[rows_at(e * 16, 16)], mine)
    wall_kept.wait()
    for copy in wall_sends:
        copy.wait_recv()

    def to_ring(axis, piece):
        steps = [(0, d, 0) if axis == "x" else (d, 0, 0) for d in (1, 3, 2)]
        return [links.remote(piece, piece, (exp_of(e, *step), h)) for step in steps]

    low_half, high_half = pl.ds(0, 2), pl.ds(2, 2)
    wall_first = to_ring("z", wall.at[low_half, rows_at(along_z, 16), columns])
    wall_first += to_ring("x", wall.at[high_half, rows_at(along_x, 16), columns])

    def project(block):
        here = rows_at(block * ROWS, ROWS)
        block_rows = joined[here, :]
        for i, ref in enumerate((q, k, v)):
            ref[here, :] = dot(block_rows, wqkv[i]).astype(BF)

    gather_own.wait()
    loads[2].wait()
    project(h)
    relayed = gather_relay(links, gather, joined, e, h)
    for copy in wall_first:
        copy.wait_recv()
    wall_second = to_ring("x", wall.at[low_half, rows_at(x_at * 64, 64), columns])
    wall_second += to_ring("z", wall.at[high_half, rows_at(z * 64, 64), columns])
    gather[1].wait_recv()
    project(hid_of(h, -1))
    gather[3].wait_recv()
    project(hid_of(h, 1))
    g_kept.wait()
    for copy in g_sends:
        copy.wait_recv()
    for i in range(4):
        pair = split_experts(landed_g[pl.ds(i * 128, 128), :])
        for j in (0, 1):
            grads[j, pl.ds(i * 64, 64), :] = pair[j]

    def near(j):
        piece = grads.at[j, pl.ds(0, ROWS)]
        return [
            links.remote(piece, grads.at[j, pl.ds(ROWS, ROWS)], up),
            links.remote(piece, grads.at[j, pl.ds(2 * ROWS, ROWS)], down),
        ]

    g_near = near(0) + near(1)
    outs = []
    for copy in relayed:
        copy.wait_recv()
    project(hid_of(h, 2))
    outs += [links.local(src, dst) for src, dst in ((joined, joined_out), (q, q_out), (k, k_out), (v, v_out))]
    for copy in wall_second:
        copy.wait_recv()
    wall_core = wall.at[:, :, columns]
    wall_third = [links.remote(wall_core, wall_core, (exp_of(e, 0, 0, 1), h))]
    head_sends = []
    for peer in (far, up, down, (e, h)):
        for b in range(N_HID):

            @pl.when(peer[1] == b)
            def _(b=b):
                attend_block(b, q, k, v, heads, logs_ref)

        piece = heads.at[rows_at(peer[1] * ROWS, ROWS)]
        if peer[1] is h:
            head_own = links.local(piece, hall.at[h])
        else:
            head_sends.append(links.remote(piece, hall.at[h], peer))
    for copy in g_near:
        copy.wait_recv()
    g_far = [
        links.remote(grads.at[0, pl.ds(ROWS, ROWS)], grads.at[0, pl.ds(3 * ROWS, ROWS)], up),
        links.remote(grads.at[1, pl.ds(2 * ROWS, ROWS)], grads.at[1, pl.ds(3 * ROWS, ROWS)], down),
    ]
    for copy in wall_third:
        copy.wait_recv()
    outs.append(links.local(wall, wall_out))
    head_own.wait()
    for copy in head_sends:
        copy.wait_recv()
    outs.append(links.local(hall, hall_out))
    attn_sum = dot(hall[0], wall[0])
    for i in range(1, N_HID):
        attn_sum = attn_sum + dot(hall[i], wall[i])
    residual = x_ref[...].astype(F32) + attn_sum
    residual_ref[...] = residual
    hat, _ = norm_parts(residual)
    routed = (hat * gain2_ref[...] + bias2_ref[...]).astype(BF)
    outgoing[...] = dot(pick_ref[...], routed).astype(BF)
    mine = landed.at[rows_at(e * 16, 16)]
    order = (0, 1, 3, 2)
    sent = {}
    for dz in order:
        sent[dz] = []
        for step in plane_steps((dz,)):
            t = exp_of(e, *step)
            sent[dz].append(links.remote(outgoing.at[rows_at(t * 16, 16)], mine, (t, h)))
    kept = links.local(outgoing.at[rows_at(e * 16, 16)], mine)
    waits = []
    pending = None

    def relay(chunk):
        at, first, second = chunk
        first.wait_recv()
        third = links.remote(rows.at[0, rows_at(ROWS + at, 64)], rows.at[0, rows_at(3 * ROWS + at, 64)], up)
        second.wait_recv()
        fourth = links.remote(
            rows.at[1, rows_at(2 * ROWS + at, 64)], rows.at[1, rows_at(3 * ROWS + at, 64)], down
        )
        waits.extend((third, fourth))

    for dz in order:
        if dz == 0:
            kept.wait()
        for copy in sent[dz]:
            copy.wait_recv()
        from_z = lax.rem(z - dz + 4, 4)
        at = from_z * 64
        pair = split_experts(landed[rows_at(from_z * 128, 128), :])
        for j in (0, 1):
            rows[j, rows_at(at, 64), :] = pair[j]
        piece = rows.at[:, rows_at(at, 64)]
        first = links.remote(piece, rows.at[:, rows_at(ROWS + at, 64)], up)
        second = links.remote(piece, rows.at[:, rows_at(2 * ROWS + at, 64)], down)
        if pending is not None:
            relay(pending)
        pending = (at, first, second)
        sent[dz].extend((first, second))

    def hidden(expert, block):
        here = rows_at(block * ROWS, ROWS)
        pre = dot(rows[expert, here, :], win[expert])
        root = 0.7978845608028654
        square = pre * pre
        curve = jnp.tanh(pre * (root + (root * 0.044715) * square))
        half = 0.5 + 0.5 * curve
        active = pre * half
        act[expert, here, :] = active.astype(BF)
        slope[expert] = half + active * (1.0 - curve) * (root + (3 * 0.044715 * root) * square)

    def gradient(expert, block):
        here = rows_at(block * ROWS, ROWS)
        grad_act = dot_nt(grads[expert, here, :], wdown[expert])
        grad_pre = (grad_act * slope[expert]).astype(BF)
        gpre[expert, here, :] = grad_pre
        back[expert, here, :] = dot_nt(grad_pre, win[expert]).astype(BF)

    def both(first_block, count):
        def step(i, carry):
            expert, block = lax.rem(i, 2), first_block + i // 2
            hidden(expert, block)
            gradient(expert, block)
            return carry

        lax.fori_loop(0, 2 * count, step, 0)

    def forward(first_block, count):
        def step(i, carry):
            expert, here = lax.rem(i, 2), rows_at((first_block + i // 2) * ROWS, ROWS)
            mixed[expert, here, :] = dot(act[expert, here, :], wdown[expert]).astype(BF)
            return carry

        lax.fori_loop(0, 2 * count, step, 0)

    def far_step(i, carry):
        hidden(i, 3)
        return carry

    def far_back(i, carry):
        gradient(i, 3)
        return carry

    def deliver(src, places):
        for (expert, block), place in places:
            outs.append(links.local(src.at[expert, pl.ds(block * ROWS, ROWS)], place))

    def write(src, dst, first_block, count):
        piece = pl.ds(first_block * ROWS, count * ROWS)
        outs.append(links.local(src.at[:, piece], dst.at[:, piece]))

    for copy in weights:
        copy.wait()
    both(0, 1)
    forward(0, 1)
    relay(pending)
    write(gpre, gpre_out, 0, 1)
    deliver(back, (((0, 0), own_out.at[0]), ((1, 0), own_out.at[1])))
    deliver(mixed, (((0, 0), m_own_out.at[0]), ((1, 0), m_own_out.at[1])))
    both(1, 2)
    write(rows, rows_out, 0, 3)
    write(grads, grads_out, 0, 3)
    write(gpre, gpre_out, 1, 2)
    back_near = [
        links.remote(back.at[1, pl.ds(2 * ROWS, ROWS)], near_below_out, up),
        links.remote(back.at[0, pl.ds(ROWS, ROWS)], near_above_out, down),
    ]
    deliver(back, (((0, 2), low_out), ((1, 1), high_out)))
    for copy in waits:
        copy.wait_recv()
    lax.fori_loop(0, 2, far_step, 0)
    write(rows, rows_out, 3, 1)
    write(act, act_out, 0, 4)
    forward(1, 3)
    deliver(
        mixed,
        (
            ((0, 2), m_low_out), ((1, 1), m_high_out), ((1, 2), m_go_up_out.at[1]), ((0, 1), m_go_down_out.at[1]),
            ((0, 3), m_go_up_out.at[0]), ((1, 3), m_go_down_out.at[0]),
        ),
    )
    for copy in g_far:
        copy.wait_recv()
    lax.fori_loop(0, 2, far_back, 0)
    write(grads, grads_out, 3, 1)
    write(gpre, gpre_out, 3, 1)
    deliver(back, (((0, 3), go_up_out), ((1, 3), go_down_out)))
    for copy in outs + back_near:
        copy.wait()
    for dz in order:
        for copy in sent[dz]:
            copy.wait_send()
    for copy in gather + relayed + wall_sends + wall_first + wall_second + wall_third + g_sends + head_sends + g_near + g_far + waits:
        copy.wait_send()


def front_call(block_input, gain1, bias1, gain2, bias2, ids, out_grad, w_qkv, w_out, w_in, w_down):
    rows, width = N_HID * ROWS, w_qkv.shape[2]
    flat = jax.ShapeDtypeStruct((rows, width), BF)
    pair = jax.ShapeDtypeStruct((2, ROWS, WIDTH), BF)
    shares = (N_HID, ROWS, WIDTH)
    held = pltpu.VMEM((rows, width), BF)
    slots = pltpu.VMEM((SLOTS, WIDTH), BF)
    block = pltpu.VMEM((ROWS, WIDTH), BF)
    one = jax.ShapeDtypeStruct((ROWS, WIDTH), BF)
    whole = jax.ShapeDtypeStruct((2, rows, WIDTH), BF)
    held_rows = pltpu.VMEM((2, rows, WIDTH), BF)
    weight = pltpu.VMEM(w_in.shape, BF)
    return pl.pallas_call(
        front_kernel,
        out_shape=(
            jax.ShapeDtypeStruct((rows, WIDTH), BF),
            flat, flat, flat,
            jax.ShapeDtypeStruct((N_HID, ROWS, width), BF),
            jax.ShapeDtypeStruct(shares, BF),
            jax.ShapeDtypeStruct((8, rows), F32),
            jax.ShapeDtypeStruct((ROWS, WIDTH), F32),
            jax.ShapeDtypeStruct((SLOTS, ROWS), BF),
            whole, whole, whole, whole,
            pair, one, one, one, one, one, one,
            pair, one, one, pair, pair,
        ),
        in_specs=[VMEM] * 6 + [ANY] * 5,
        out_specs=[ANY] * 6 + [VMEM] * 3 + [ANY] * 16,
        scratch_shapes=[
            block, pltpu.VMEM((rows, WIDTH), BF), block, pltpu.VMEM(w_qkv.shape, BF), block, pltpu.VMEM(shares, BF),
            held, held, held, held, pltpu.VMEM((N_HID, ROWS, width), BF),
            slots, slots, slots, slots, weight, weight, held_rows, held_rows, held_rows,
            pltpu.VMEM((2, ROWS, WIDTH), F32), held_rows, held_rows, held_rows,
        ]
        + sems(5 + 7 + 4 + 32 + 13 + 4 + 2 + 4 + 4 + 2 + 32 + 16 + 30),
        compiler_params=pltpu.CompilerParams(
            collective_id=1, has_side_effects=True, vmem_limit_bytes=62 * MIB
        ),
        cost_estimate=pl.CostEstimate(flops=20 * 10**9, bytes_accessed=100 * MIB, transcendentals=0),
        name="front",
    )(block_input, gain1, bias1, gain2, bias2, ids, out_grad, w_qkv, w_out, w_in, w_down)


def weights_kernel(rows_ref, gpre_ref, act_ref, grads_ref, dwin_ref, dwdown_ref):
    dwin_ref[0] = dot_tn(rows_ref[0], gpre_ref[0])
    dwdown_ref[0] = dot_tn(act_ref[0], grads_ref[0])


def weights_call(rows, grad_pre, act, grads):
    half = WIDTH // 2
    whole = pl.BlockSpec((1, WIDTH, WIDTH), lambda i, j: (i, 0, 0))
    columns = pl.BlockSpec((1, WIDTH, half), lambda i, j: (i, 0, j))
    result = jax.ShapeDtypeStruct(rows.shape, F32)
    return pl.pallas_call(
        weights_kernel,
        grid=(2, 2),
        out_shape=(result, result),
        in_specs=[whole, columns, columns, whole],
        out_specs=[columns, pl.BlockSpec((1, half, WIDTH), lambda i, j: (i, j, 0))],
        compiler_params=pltpu.CompilerParams(vmem_limit_bytes=60 * MIB),
        cost_estimate=pl.CostEstimate(flops=86 * 10**8, bytes_accessed=32 * MIB, transcendentals=0),
        name="weights",
    )(rows, grad_pre, act, grads)


RING = (1, 3, 2)


def back_kernel(
    up_pass_up, up_pass_down, up_below, up_above, near_below, near_above, gain1_ref, gain2_ref, logs_ref,
    up_own_hbm, pick_hbm, residual_hbm, grad_hbm, x_hbm, wall_hbm, wqkv_hbm, joined_hbm, q_hbm, k_hbm, v_hbm, hall_hbm,
    m_own_hbm, m_low_hbm, m_high_hbm, m_go_up, m_go_down,
    out_ref, ginput_ref, dwq_ref, dwo_ref, vecsum_ref,
    up_own, pick, residual, grad_in, x, wall, wqkv, joined, q, k, v, hall, m_own, m_pass_up, m_pass_down,
    pass_up, pass_down, got, outgoing, landed, gres, gas, gheads_out, gheads,
    dwo, dwo_got, dwo_half, dwo_got1, dwo_x, dwo_got2, dwo_sum, dwo_hid,
    m_far_up, m_far_down, m_near_up, m_near_down, m_got, m_outgoing, m_landed,
    gq, gk, gv, term, t_got, half_up, half_down, t_pass_up, t_pass_down,
    dwq, dwq_got, dwq_half, dwq_got1, dwq_mid, dwq_got2, vec, vec_got, send_sem, recv_sem,
):
    e, h = place()
    z, x_at, core = e // 8, lax.rem(e // 2, 4), lax.rem(e, 2)
    up, down, far = (e, hid_of(h, 1)), (e, hid_of(h, -1)), (e, hid_of(h, 2))
    twin = (exp_of(e, 0, 0, 1), h)
    plane = plane_peers(e, h)
    peers = [up, down, far] + plane
    peers += [(exp_of(e, dz, 0, 0), hid_of(h, dy)) for dz in (1, 2, 3) for dy in (1, 2, 3)]
    signal(peers)
    links = Links(send_sem, recv_sem)

    def along(axis, d):
        return (exp_of(e, 0, d, 0) if axis == "x" else exp_of(e, d, 0, 0), h)

    def position(axis):
        return x_at if axis == "x" else z

    def scatter(axis, piece_of, got_ref):
        return [
            links.remote(piece_of(lax.rem(position(axis) + d, 4)), got_ref.at[i], along(axis, d))
            for i, d in enumerate(RING)
        ]

    def share(axis, piece):
        return [links.remote(piece, piece, along(axis, d)) for d in RING]

    def arrived(copies):
        for copy in copies:
            copy.wait_recv()
        ended.extend(copies)

    def total(own_piece, got_ref):
        whole = own_piece.astype(F32)
        for i in range(len(RING)):
            whole = whole + got_ref[i].astype(F32)
        return whole.astype(BF)

    ended = []
    load = {}
    for name, src, dst in (
        ("own", up_own_hbm, up_own), ("pick", pick_hbm, pick), ("residual", residual_hbm, residual),
        ("grad", grad_hbm, grad_in), ("wall", wall_hbm, wall), ("hall", hall_hbm, hall), ("q", q_hbm, q), ("k", k_hbm, k),
        ("v", v_hbm, v), ("wqkv", wqkv_hbm, wqkv), ("joined", joined_hbm, joined), ("x", x_hbm, x),
        ("m", m_own_hbm, m_own), ("mu", m_low_hbm, m_pass_up), ("md", m_high_hbm, m_pass_down),
    ):
        load[name] = links.local(src, dst)
    await_signals(peers)
    order = (2, 1, 3, 0)
    passed = []
    for dz in order:
        at = lax.rem(z + dz, 4) * 64
        piece = rows_at(at, 64)
        pass_up[piece, :] = (up_pass_up[piece, :].astype(F32) + up_below[piece, :].astype(F32)).astype(BF)
        five = links.remote(pass_up.at[piece], got.at[0, piece], up)
        pass_down[piece, :] = (up_pass_down[piece, :].astype(F32) + up_above[piece, :].astype(F32)).astype(BF)
        six = links.remote(pass_down.at[piece], got.at[1, piece], down)
        passed.append((at, five, six))
        ended += [five, six]
    mine = landed.at[rows_at(e * 16, 16)]
    back = []
    load["own"].wait()
    for dz, (at, five, six) in zip(order, passed):
        five.wait_recv()
        six.wait_recv()
        piece = rows_at(at, 64)
        pair = [
            up_own[j, piece, :].astype(F32) + got[j, piece, :].astype(F32) + near[piece, :].astype(F32)
            for j, near in enumerate((near_above, near_below))
        ]
        outgoing[rows_at(at * 2, 128), :] = merge_experts(*pair)
        for step in plane_steps((dz,)):
            t = exp_of(e, *step)
            back.append(links.remote(outgoing.at[rows_at(t * 16, 16)], mine, (t, h)))
    m_far = [links.remote(m_go_up.at[0], m_far_up, up), links.remote(m_go_down.at[0], m_far_down, down)]
    ended += m_far
    kept = links.local(outgoing.at[rows_at(e * 16, 16)], mine)
    kept.wait()
    for name in ("pick", "residual", "grad", "wall"):
        load[name].wait()
    load["hall"].wait()
    for copy in back:
        copy.wait_recv()
    ended += back
    routed = dot_tn(pick[...], landed[...])
    hat, scale = norm_parts(residual[...])
    vec[0] = jnp.zeros_like(vec[0])
    vec[0, 2:3, :] = jnp.sum(routed * hat, axis=0, keepdims=True)
    vec[0, 3:4, :] = jnp.sum(routed, axis=0, keepdims=True)
    whole = grad_in[...].astype(F32) + norm_back(routed, hat, scale, gain2_ref[...])
    gres[...] = whole
    gas[...] = whole.astype(BF)
    head_sends = []
    for i, peer in enumerate((far, up, down)):
        gheads_out[i] = dot_nt(gas[...], wall[peer[1]]).astype(BF)
        head_sends.append(links.remote(gheads_out.at[i], gheads.at[rows_at(h * ROWS, ROWS)], peer))
    ended += head_sends
    gheads[rows_at(h * ROWS, ROWS), :] = dot_nt(gas[...], wall[h]).astype(BF)
    m_near = [links.remote(m_go_up.at[1], m_near_up, up), links.remote(m_go_down.at[1], m_near_down, down)]
    ended += m_near
    for i in range(N_HID):
        dwo[i] = dot_tn(hall[i], gas[...]).astype(BF)
    other = pl.ds(pl.multiple_of((1 - core) * 512, 512), 512)
    own = pl.ds(pl.multiple_of(core * 512, 512), 512)
    dwo_swap = links.remote(dwo.at[:, :, other], dwo_got, twin)
    for name in ("q", "k", "v"):
        load[name].wait()
    for copy in head_sends:
        copy.wait_recv()
    gk[...] = jnp.zeros_like(gk)
    gv[...] = jnp.zeros_like(gv)

    def attention(block):
        attend_block_back(block, q, k, v, gheads, logs_ref, gq, gk, gv)

    attention(0)
    arrived([dwo_swap])
    for i in range(N_HID):
        dwo_half[i] = (dwo[i, :, own].astype(F32) + dwo_got[i].astype(F32)).astype(BF)
    dwo_first = scatter("x", lambda t: dwo_half.at[:, rows_at(t * 64, 64)], dwo_got1)
    attention(1)
    attention(2)
    load["mu"].wait()
    load["md"].wait()
    m_far[0].wait_recv()
    m_pass_up[...] = (m_pass_up[...].astype(F32) + m_far_up[...].astype(F32)).astype(BF)
    five = links.remote(m_pass_up, m_got.at[0], up)
    m_far[1].wait_recv()
    m_pass_down[...] = (m_pass_down[...].astype(F32) + m_far_down[...].astype(F32)).astype(BF)
    six = links.remote(m_pass_down, m_got.at[1], down)
    ended += [five, six]
    attention(3)
    load["wqkv"].wait()
    load["joined"].wait()
    parts = (gq[...], gk[...].astype(BF), gv[...].astype(BF))
    for i, part in enumerate(parts):
        dwq[pl.ds(i * WIDTH, WIDTH), :] = dot_tn(joined[...], part).astype(BF)
    count = dwq.shape[0] // 2
    dwq_swap = links.remote(dwq.at[rows_at((1 - core) * count, count)], dwq_got, twin)
    arrived(dwo_first)
    dwo_x[...] = total(dwo_half[:, rows_at(x_at * 64, 64), :], dwo_got1)
    dwo_second = scatter("z", lambda t: dwo_x.at[:, rows_at(t * 16, 16)], dwo_got2)
    term[...] = sum(dot_nt(part, wqkv[i]) for i, part in enumerate(parts)).astype(BF)
    begun = reduce_begin(links, term, t_got, half_up, half_down, e, h)
    arrived(dwo_second)
    dwo_sum[...] = total(dwo_x[:, rows_at(z * 16, 16), :], dwo_got2)
    dwo_cross = [
        links.remote(dwo_sum.at[peer[1]], dwo_hid.at[i], peer) for i, peer in enumerate((far, up, down))
    ]
    arrived([dwq_swap])
    dwq_half[...] = (dwq[rows_at(core * count, count), :].astype(F32) + dwq_got[...].astype(F32)).astype(BF)
    wide, narrow = count // 8, count // 32
    ways = (("z", "x", 0), ("x", "z", count // 2))
    dwq_first = [
        scatter(one, lambda t, base=base: dwq_half.at[rows_at(base + t * wide, wide)], dwq_got1.at[j])
        for j, (one, two, base) in enumerate(ways)
    ]
    load["m"].wait()
    for copy in m_near:
        copy.wait_recv()
    five.wait_recv()
    six.wait_recv()
    for i in range(4):
        piece = pl.ds(i * 64, 64)
        pair = [
            m_own[j, piece, :].astype(F32) + m_got[j, piece, :].astype(F32) + near[piece, :].astype(F32)
            for j, near in enumerate((m_near_down, m_near_up))
        ]
        m_outgoing[pl.ds(i * 128, 128), :] = merge_experts(*pair)
    mine = m_landed.at[rows_at(e * 16, 16)]
    m_back = []
    for step in plane_steps((2, 1, 3, 0)):
        t = exp_of(e, *step)
        m_back.append(links.remote(m_outgoing.at[rows_at(t * 16, 16)], mine, (t, h)))
    m_kept = links.local(m_outgoing.at[rows_at(e * 16, 16)], mine)
    dwq_second = []
    for j, (one, two, base) in enumerate(ways):
        arrived(dwq_first[j])
        dwq_mid[j] = total(dwq_half[rows_at(base + position(one) * wide, wide), :], dwq_got1.at[j])
        dwq_second.append(scatter(two, lambda t, j=j: dwq_mid.at[j, rows_at(t * narrow, narrow)], dwq_got2.at[j]))
    arrived(dwo_cross)
    dwo_at = rows_at(x_at * 64 + z * 16, 16)
    dwo_ref[dwo_at, own] = total(dwo_sum[h], dwo_hid)
    dwo_third = share("z", dwo_ref.at[dwo_at, own])
    reduced = reduce_middle(links, begun, term, t_got, half_up, half_down, t_pass_up, t_pass_down, e, h)
    ended += reduced
    dwq_third = []
    for j, (one, two, base) in enumerate(ways):
        arrived(dwq_second[j])
        at = rows_at(core * count + base + position(one) * wide + position(two) * narrow, narrow)
        dwq_ref[at, :] = total(dwq_mid[j, rows_at(position(two) * narrow, narrow), :], dwq_got2.at[j])
        dwq_third.append(share(two, dwq_ref.at[at]))
    arrived(dwo_third)
    dwo_fourth = share("x", dwo_ref.at[rows_at(x_at * 64, 64), own])
    dwq_fourth = []
    for j, (one, two, base) in enumerate(ways):
        arrived(dwq_third[j])
        dwq_fourth.append(share(one, dwq_ref.at[rows_at(core * count + base + position(one) * wide, wide)]))
    load["x"].wait()
    grad = reduce_end(reduced, term, t_got, h)
    hat, scale = norm_parts(x[...].astype(F32))
    ginput_ref[...] = gres[...] + norm_back(grad, hat, scale, gain1_ref[...])
    vec[0, 0:1, :] = jnp.sum(grad * hat, axis=0, keepdims=True)
    vec[0, 1:2, :] = jnp.sum(grad, axis=0, keepdims=True)
    rounds = (
        [(exp_of(e, dz, 0, 0), hid_of(h, dy)) for dz in range(4) for dy in range(4) if (dz, dy) != (0, 0)],
        [(exp_of(e, 0, dx, dc), h) for dx in range(4) for dc in (0, 1) if (dx, dc) != (0, 0)],
    )
    first_round = [links.remote(vec.at[0], vec_got.at[i], peer) for i, peer in enumerate(rounds[0])]
    for j in range(len(ways)):
        arrived(dwq_fourth[j])
    dwq_twin = dwq_ref.at[rows_at(core * count, count)]
    twins = [links.remote(dwq_twin, dwq_twin, twin)]
    arrived(dwo_fourth)
    dwo_twin = dwo_ref.at[:, own]
    twins.append(links.remote(dwo_twin, dwo_twin, twin))
    arrived(first_round)
    whole = vec[0]
    for i in range(len(rounds[0])):
        whole = whole + vec_got[i]
    vec[1] = whole
    second_round = [
        links.remote(vec.at[1], vec_got.at[len(rounds[0]) + i], peer) for i, peer in enumerate(rounds[1])
    ]
    m_kept.wait()
    arrived(m_back)
    out_ref[...] = (residual[...] + dot_tn(pick[...], m_landed[...])).astype(BF)
    arrived(second_round)
    whole = vec[1]
    for i in range(len(rounds[1])):
        whole = whole + vec_got[len(rounds[0]) + i]
    vecsum_ref[...] = whole
    arrived(twins)
    for copy in ended:
        copy.wait_send()


def back_call(up_parts, gain1, gain2, logs, pick, residual, out_grad, block_input, wall, w_qkv, joined, q, k, v, hall, down_parts):
    rows, width = q.shape
    block = pltpu.VMEM((ROWS, WIDTH), BF)
    half = pltpu.VMEM((ROWS // 2, WIDTH), BF)
    pair = pltpu.VMEM((2, ROWS, WIDTH), BF)
    slots = pltpu.VMEM((SLOTS, WIDTH), BF)
    held = pltpu.VMEM((rows, width), BF)
    wide = pltpu.VMEM((rows, WIDTH), BF)
    shares = pltpu.VMEM((N_HID, ROWS, WIDTH), BF)
    half_shares = pltpu.VMEM((N_HID, ROWS, WIDTH // 2), BF)
    quarter = pltpu.VMEM((3 * WIDTH // 2, width), BF)
    return pl.pallas_call(
        back_kernel,
        out_shape=(
            jax.ShapeDtypeStruct((ROWS, WIDTH), BF),
            jax.ShapeDtypeStruct((ROWS, WIDTH), F32),
            jax.ShapeDtypeStruct((3 * WIDTH, width), BF),
            jax.ShapeDtypeStruct((ROWS, WIDTH), BF),
            jax.ShapeDtypeStruct((8, WIDTH), F32),
        ),
        in_specs=[VMEM] * 9 + [ANY] * 17,
        out_specs=[VMEM] * 5,
        scratch_shapes=[
            pair, pltpu.VMEM((SLOTS, ROWS), BF), pltpu.VMEM((ROWS, WIDTH), F32),
            block, block, shares, pltpu.VMEM(w_qkv.shape, BF), wide, held, held, held,
            pltpu.VMEM((N_HID, ROWS, width), BF), pair, block, block,
            block, block, pair, slots, slots, pltpu.VMEM((ROWS, WIDTH), F32), block,
            pltpu.VMEM((3, ROWS, width), BF), held,
            shares, half_shares, half_shares, pltpu.VMEM((3, N_HID, 64, WIDTH // 2), BF), pltpu.VMEM((N_HID, 64, WIDTH // 2), BF),
            pltpu.VMEM((3, N_HID, 16, WIDTH // 2), BF), pltpu.VMEM((N_HID, 16, WIDTH // 2), BF), pltpu.VMEM((3, 16, WIDTH // 2), BF),
            block, block, block, block, pair, slots, slots,
            held, pltpu.VMEM((rows, width), F32), pltpu.VMEM((rows, width), F32),
            wide, pair, half, half, half, half,
            pltpu.VMEM((3 * WIDTH, width), BF), quarter, quarter, pltpu.VMEM((2, 3, 192, width), BF),
            pltpu.VMEM((2, 192, width), BF), pltpu.VMEM((2, 3, 48, width), BF),
            pltpu.VMEM((2, 8, WIDTH), F32), pltpu.VMEM((22, 8, WIDTH), F32),
        ]
        + sems(15 + 8 + 32 + 3 + 4 + 2 + 1 + 15 + 6 + 1 + 24 + 32 + 22 + 2),
        compiler_params=pltpu.CompilerParams(
            collective_id=2, has_side_effects=True, vmem_limit_bytes=62 * MIB
        ),
        cost_estimate=pl.CostEstimate(flops=12 * 10**9, bytes_accessed=100 * MIB, transcendentals=0),
        name="back",
    )(*up_parts[1:], gain1, gain2, logs, up_parts[0], pick, residual, out_grad, block_input, wall, w_qkv, joined, q, k, v, hall, *down_parts)


def finish_kernel(out_ref, ginput_ref, dwq_ref, dwo_ref, vec_ref, out, ginput, dwq, dwo, *vectors):
    out[...] = out_ref[...]
    ginput[...] = ginput_ref[...]
    dwq[...] = dwq_ref[...].astype(F32)
    dwo[...] = dwo_ref[...].astype(F32)
    for i, ref in enumerate(vectors):
        ref[...] = vec_ref[i : i + 1, :]


def finish_call(out, ginput, dwq, dwo, vec):
    def rows_of(array, parts):
        return pl.BlockSpec((array.shape[0] // parts, array.shape[1]), lambda i: (i, 0))

    blocks = [rows_of(array, 4) for array in (out, ginput, dwq, dwo)]
    fixed = pl.BlockSpec((8, WIDTH), lambda i: (0, 0))
    vector = pl.BlockSpec((1, WIDTH), lambda i: (0, 0))
    return pl.pallas_call(
        finish_kernel,
        grid=(4,),
        out_shape=(
            jax.ShapeDtypeStruct(out.shape, BF), jax.ShapeDtypeStruct(ginput.shape, F32),
            jax.ShapeDtypeStruct(dwq.shape, F32), jax.ShapeDtypeStruct(dwo.shape, F32),
        ) + (jax.ShapeDtypeStruct((1, WIDTH), F32),) * 4,
        in_specs=blocks + [fixed],
        out_specs=blocks + [vector] * 4,
        compiler_params=pltpu.CompilerParams(vmem_limit_bytes=60 * MIB),
        cost_estimate=pl.CostEstimate(flops=0, bytes_accessed=9 * MIB, transcendentals=0),
        name="results",
    )(out, ginput, dwq, dwo, vec)


def hid_shift(rows, step):
    return lax.ppermute(rows, "hid", [(i, (i + step) % N_HID) for i in range(N_HID)])


def after(arrays, *first):
    return lax.optimization_barrier((arrays, first))[0]


def on_device(
    block_input, norm1_gain, norm1_bias, w_qkv, w_out, norm2_gain, norm2_bias,
    w_in, w_down, expert_ids, out_grad,
):
    gain1, bias1, gain2, bias2 = (
        v.reshape(1, WIDTH) for v in (norm1_gain, norm1_bias, norm2_gain, norm2_bias)
    )
    (
        joined, q, k, v, hall, wall, logs, residual, pick,
        rows, grads, act, grad_pre, up_own, up_low, up_high, go_up, go_down, near_below, near_above, *down_parts,
    ) = front_call(
        block_input, gain1, bias1, gain2, bias2, expert_ids.reshape(1, ROWS), out_grad, w_qkv, w_out, w_in, w_down
    )
    below, above = hid_shift(go_up, 1), hid_shift(go_down, -1)
    d_w_in, d_w_down = weights_call(rows, grad_pre, act, grads)
    below, above = after((below, above), d_w_in, d_w_down)
    output, grad_input, dw_qkv, dw_out, vec_sum = back_call(
        (up_own, up_low, up_high, below, above, near_below, near_above), gain1, gain2, logs, pick, residual, out_grad, block_input,
        wall, w_qkv, joined, q, k, v, hall, down_parts,
    )
    output, grad_input, d_w_qkv, d_w_out, *vectors = finish_call(output, grad_input, dw_qkv, dw_out, vec_sum)
    d_gain1, d_bias1, d_gain2, d_bias2 = (v.reshape(WIDTH) for v in vectors)
    return (
        output, grad_input, d_gain1, d_bias1, d_w_qkv.reshape(w_qkv.shape), d_w_out,
        d_gain2, d_bias2, d_w_in, d_w_down,
    )


def solution(mesh):
    in_specs = (
        P(("exp", "hid"), None), P(), P(), P(None, None, "hid"), P("hid", None), P(), P(),
        P("exp", None, "hid"), P("exp", "hid", None), P(("exp", "hid"), None), P(("exp", "hid"), None),
    )
    out_specs = (
        P(("exp", "hid"), None), P(("exp", "hid"), None), P(), P(), P(None, None, "hid"), P("hid", None),
        P(), P(), P("exp", None, "hid"), P("exp", "hid", None),
    )
    return jax.shard_map(on_device, mesh=mesh, in_specs=in_specs, out_specs=out_specs, check_vma=False)
```

```python
import jax
import jax.numpy as jnp
from jax import lax
from jax.experimental import pallas as pl
from jax.experimental.pallas import tpu as pltpu
from jax.sharding import PartitionSpec as P

HD = 64
EPSILON = 1e-05
NEG_LARGE = -1e30
BF = jnp.bfloat16
F32 = jnp.float32
MESH = pl.DeviceIdType.MESH
ANY = pl.BlockSpec(memory_space=pl.ANY)
VMEM = pl.BlockSpec(memory_space=pltpu.VMEM)
N_HID = 4
N_EXP = 32
ROWS = 256
WIDTH = 1024
SLOTS = 512
MIB = 1 << 20


def dot(a, b):
    return jnp.dot(a, b, preferred_element_type=F32)


def dot_nt(a, b):
    return lax.dot_general(a, b, (((1,), (1,)), ((), ())), preferred_element_type=F32)


def dot_tn(a, b):
    return lax.dot_general(a, b, (((0,), (0,)), ((), ())), preferred_element_type=F32)


def place():
    return lax.axis_index("exp"), lax.axis_index("hid")


def hid_of(h, step):
    return lax.rem(h + step + N_HID, N_HID)


def exp_of(e, dz, dx, dc):
    z, x, c = e // 8, lax.rem(e // 2, 4), lax.rem(e, 2)
    return (lax.rem(z + dz, 4) * 4 + lax.rem(x + dx, 4)) * 2 + lax.rem(c + dc, 2)


def plane_steps(order):
    return [
        (dz, dx, dc)
        for dz in order
        for dx in (0, 1, 3, 2)
        for dc in (0, 1)
        if (dz, dx, dc) != (0, 0, 0)
    ]


def signal(peers):
    barrier = pltpu.get_barrier_semaphore()
    for peer in peers:
        pl.semaphore_signal(barrier, inc=1, device_id=peer, device_id_type=MESH)


def await_signals(peers):
    pl.semaphore_wait(pltpu.get_barrier_semaphore(), len(peers))


class Links:
    def __init__(self, send_sem, recv_sem):
        self.send_sem, self.recv_sem, self.used = send_sem, recv_sem, 0

    def remote(self, src, dst, peer):
        i = self.used
        self.used += 1
        copy = pltpu.make_async_remote_copy(
            src_ref=src,
            dst_ref=dst,
            send_sem=self.send_sem.at[i],
            recv_sem=self.recv_sem.at[i],
            device_id=peer,
            device_id_type=MESH,
        )
        copy.start()
        return copy

    def local(self, src, dst):
        i = self.used
        self.used += 1
        copy = pltpu.make_async_copy(src, dst, self.send_sem.at[i])
        copy.start()
        return copy


def rows_at(start, size, unit=16):
    return pl.ds(pl.multiple_of(start, unit), size)


def split_experts(block):
    n = block.shape[0] // 16
    wide = block.astype(F32).reshape(n, 2, 8, block.shape[1])
    return [wide[:, i].reshape(n * 8, block.shape[1]).astype(BF) for i in (0, 1)]


def merge_experts(first, second):
    n, width = first.shape[0] // 8, first.shape[1]
    pair = jnp.concatenate(
        [first.reshape(n, 1, 8, width), second.reshape(n, 1, 8, width)], axis=1
    )
    return pair.reshape(n * 16, width).astype(BF)


def norm_parts(rows):
    centered = rows - jnp.mean(rows, -1, keepdims=True)
    scale = lax.rsqrt(jnp.mean(centered * centered, -1, keepdims=True) + EPSILON)
    return centered * scale, scale


def norm_back(grad, hat, scale, gain):
    gh = grad * gain
    inner = jnp.mean(gh * hat, -1, keepdims=True)
    return scale * (gh - jnp.mean(gh, -1, keepdims=True) - hat * inner)


def slot_picks(ids):
    named = jnp.where(ids == lax.broadcasted_iota(jnp.int32, (128, ROWS), 0), 1.0, 0.0)
    earlier = jnp.where(
        lax.broadcasted_iota(jnp.int32, (ROWS, ROWS), 0)
        < lax.broadcasted_iota(jnp.int32, (ROWS, ROWS), 1),
        1.0,
        0.0,
    )
    running = dot(named.astype(BF), earlier.astype(BF))
    position = jnp.sum(running * named, axis=0, keepdims=True).astype(jnp.int32)
    slot = ids * 8 + position
    return jnp.where(slot == lax.broadcasted_iota(jnp.int32, (SLOTS, ROWS), 0), 1.0, 0.0).astype(BF)


def gather_begin(links, src, out, e, h):
    half = ROWS // 2
    copies = []
    for first, peer in ((0, (e, hid_of(h, 1))), (half, (e, hid_of(h, -1)))):
        for start in (first, half - first):
            piece = out.at[rows_at(h * ROWS + start, half)]
            copies.append(links.remote(src.at[pl.ds(start, half)], piece, peer))
    return copies, links.local(src, out.at[rows_at(h * ROWS, ROWS)])


def gather_relay(links, copies, out, e, h):
    half = ROWS // 2
    relayed = []
    for copy, block, start, peer in (
        (copies[0], hid_of(h, -1), 0, (e, hid_of(h, 1))),
        (copies[2], hid_of(h, 1), half, (e, hid_of(h, -1))),
    ):
        copy.wait_recv()
        piece = out.at[rows_at(block * ROWS + start, half)]
        relayed.append(links.remote(piece, piece, peer))
    return relayed


def reduce_begin(links, term, got, half_up, half_down, e, h):
    up, down = (e, hid_of(h, 1)), (e, hid_of(h, -1))
    half = ROWS // 2
    far, above, below = hid_of(h, 2) * ROWS, hid_of(h, 1) * ROWS, hid_of(h, -1) * ROWS
    one = links.remote(term.at[rows_at(far, half)], half_up, up)
    two = links.remote(term.at[rows_at(far + half, half)], half_down, down)
    three = links.remote(term.at[rows_at(above + half, half)], got.at[0, pl.ds(half, half)], up)
    four = links.remote(term.at[rows_at(below, half)], got.at[1, pl.ds(0, half)], down)
    return one, two, three, four


def reduce_middle(links, begun, term, got, half_up, half_down, pass_up, pass_down, e, h):
    up, down = (e, hid_of(h, 1)), (e, hid_of(h, -1))
    half = ROWS // 2
    above, below = hid_of(h, 1) * ROWS, hid_of(h, -1) * ROWS
    one, two, three, four = begun
    one.wait_recv()
    pass_up[...] = (
        term[rows_at(above, half), :].astype(F32) + half_up[...].astype(F32)
    ).astype(BF)
    five = links.remote(pass_up, got.at[0, pl.ds(0, half)], up)
    two.wait_recv()
    pass_down[...] = (
        term[rows_at(below + half, half), :].astype(F32) + half_down[...].astype(F32)
    ).astype(BF)
    six = links.remote(pass_down, got.at[1, pl.ds(half, half)], down)
    return one, two, three, four, five, six


def reduce_end(copies, term, got, h):
    for copy in copies[2:]:
        copy.wait_recv()
    return (
        term[rows_at(h * ROWS, ROWS), :].astype(F32)
        + got[0].astype(F32)
        + got[1].astype(F32)
    )


def reduce_scratch():
    half = ROWS // 2
    return [pltpu.VMEM((2, ROWS, WIDTH), BF)] + [pltpu.VMEM((half, WIDTH), BF)] * 4


def sems(count):
    return [pltpu.SemaphoreType.DMA((count,)), pltpu.SemaphoreType.DMA((count,))]


def hid_peers(e, h):
    return [(e, hid_of(h, 1)), (e, hid_of(h, -1))]


def plane_peers(e, h):
    return [(exp_of(e, *step), h) for step in plane_steps((0, 1, 3, 2))]


def head_lanes(shape, head):
    return lax.broadcasted_iota(jnp.int32, shape, 1) // HD == head


def causal_tail(scores_t):
    keys, queries = scores_t.shape
    tail = scores_t[keys - queries :]
    allowed = lax.broadcasted_iota(jnp.int32, tail.shape, 0) <= lax.broadcasted_iota(
        jnp.int32, tail.shape, 1
    )
    tail = jnp.where(allowed, tail, NEG_LARGE)
    if keys == queries:
        return tail
    return jnp.concatenate([scores_t[: keys - queries], tail], axis=0)


def by_head(rows):
    return [
        jnp.where(head_lanes(rows.shape, head), rows, jnp.zeros_like(rows))
        for head in range(rows.shape[1] // HD)
    ]


def own_lanes(parts):
    whole = parts[0]
    for head in range(1, len(parts)):
        whole = jnp.where(head_lanes(whole.shape, head), parts[head], whole)
    return whole


def attend_block(block, q, k, v, heads, logs):
    keys, here = pl.ds(0, (block + 1) * ROWS), pl.ds(block * ROWS, ROWS)
    parts = []
    for head, query in enumerate(by_head(q[here, :] * BF(HD**-0.5))):
        scores = causal_tail(dot_nt(k[keys, :], query))
        top = jnp.max(scores, axis=0, keepdims=True)
        exps = jnp.exp(scores - top)
        summed = jnp.sum(exps, axis=0, keepdims=True)
        logs[head : head + 1, here] = top + jnp.log(summed)
        parts.append(dot_tn((exps * (1.0 / summed)).astype(BF), v[keys, :]))
    heads[here, :] = own_lanes(parts).astype(BF)


def attend_block_back(block, q, k, v, gheads, logs, gq, gk, gv):
    keys, here = pl.ds(0, (block + 1) * ROWS), pl.ds(block * ROWS, ROWS)
    queries, grads = by_head(q[here, :] * BF(HD**-0.5)), by_head(gheads[here, :])
    keys_t = k[keys, :].T
    parts, sum_v, sum_k = [], 0.0, 0.0
    for head, (query, grad) in enumerate(zip(queries, grads)):
        scores = causal_tail(dot_nt(k[keys, :], query))
        probs = jnp.exp(scores - logs[head : head + 1, here])
        weighted = probs * dot_nt(v[keys, :], grad)
        inner = jnp.sum(weighted, axis=0, keepdims=True)
        grad_scores = (weighted - probs * inner).astype(BF)
        sum_v = sum_v + dot(probs.astype(BF), grad)
        sum_k = sum_k + dot(grad_scores, query)
        parts.append(dot(keys_t[head * HD : (head + 1) * HD], grad_scores))
    gq[here, :] = (jnp.concatenate(parts, axis=0).T * HD**-0.5).astype(BF)
    gv[keys, :] += sum_v
    gk[keys, :] += sum_k


def front_kernel(
    x_ref, gain1_ref, bias1_ref, gain2_ref, bias2_ref, ids_ref, grad_hbm, wqkv_hbm, wout_hbm, win_hbm, wdown_hbm,
    joined_out, q_out, k_out, v_out, hall_out, wall_out, logs_ref, residual_ref, pick_ref,
    rows_out, grads_out, act_out, gpre_out, own_out, low_out, high_out, go_up_out, go_down_out, near_below_out, near_above_out,
    m_own_out, m_low_out, m_high_out, m_go_up_out, m_go_down_out,
    normed, joined, grad, wqkv, wout, wall, q, k, v, heads, hall,
    outgoing_g, landed_g, outgoing, landed, win, wdown, rows, grads, act, slope, gpre, back, mixed, send_sem, recv_sem,
):
    e, h = place()
    z, x_at, core = e // 8, lax.rem(e // 2, 4), lax.rem(e, 2)
    up, down, far = (e, hid_of(h, 1)), (e, hid_of(h, -1)), (e, hid_of(h, 2))
    peers = [up, down, far] + plane_peers(e, h)
    signal(peers)
    links = Links(send_sem, recv_sem)
    loads = [links.local(wout_hbm, wout), links.local(grad_hbm, grad), links.local(wqkv_hbm, wqkv)]
    weights = [links.local(win_hbm, win), links.local(wdown_hbm, wdown)]
    hat, _ = norm_parts(x_ref[...].astype(F32))
    normed[...] = (hat * gain1_ref[...] + bias1_ref[...]).astype(BF)
    await_signals(peers)
    gather, gather_own = gather_begin(links, normed, joined, e, h)
    loads[0].wait()
    columns = pl.ds(pl.multiple_of(core * 512, 512), 512)
    along_z, along_x = x_at * 64 + z * 16, z * 64 + x_at * 16
    turned = h // 2
    wall_row = rows_at(along_z * (1 - turned) + along_x * turned, 16)
    share, share_place = wout.at[wall_row, columns], wall.at[h, wall_row, columns]
    wall_sends = [links.remote(share, share_place, peer) for peer in (up, down, far)]
    wall_kept = links.local(share, share_place)
    pick = slot_picks(ids_ref[...])
    pick_ref[...] = pick
    loads[1].wait()
    outgoing_g[...] = dot(pick, grad[...]).astype(BF)
    mine = landed_g.at[rows_at(e * 16, 16)]
    g_sends = []
    for step in plane_steps((0, 1, 3, 2)):
        t = exp_of(e, *step)
        g_sends.append(links.remote(outgoing_g.at[rows_at(t * 16, 16)], mine, (t, h)))
    g_kept = links.local(outgoing_g.at[rows_at(e * 16, 16)], mine)
    wall_kept.wait()
    for copy in wall_sends:
        copy.wait_recv()

    def to_ring(axis, piece):
        steps = [(0, d, 0) if axis == "x" else (d, 0, 0) for d in (1, 3, 2)]
        return [links.remote(piece, piece, (exp_of(e, *step), h)) for step in steps]

    low_half, high_half = pl.ds(0, 2), pl.ds(2, 2)
    wall_first = to_ring("z", wall.at[low_half, rows_at(along_z, 16), columns])
    wall_first += to_ring("x", wall.at[high_half, rows_at(along_x, 16), columns])

    def project(block):
        here = rows_at(block * ROWS, ROWS)
        block_rows = joined[here, :]
        for i, ref in enumerate((q, k, v)):
            ref[here, :] = dot(block_rows, wqkv[i]).astype(BF)

    gather_own.wait()
    loads[2].wait()
    project(h)
    relayed = gather_relay(links, gather, joined, e, h)
    for copy in wall_first:
        copy.wait_recv()
    wall_second = to_ring("x", wall.at[low_half, rows_at(x_at * 64, 64), columns])
    wall_second += to_ring("z", wall.at[high_half, rows_at(z * 64, 64), columns])
    gather[1].wait_recv()
    project(hid_of(h, -1))
    gather[3].wait_recv()
    project(hid_of(h, 1))
    g_kept.wait()
    for copy in g_sends:
        copy.wait_recv()
    for i in range(4):
        pair = split_experts(landed_g[pl.ds(i * 128, 128), :])
        for j in (0, 1):
            grads[j, pl.ds(i * 64, 64), :] = pair[j]

    def near(j):
        piece = grads.at[j, pl.ds(0, ROWS)]
        return [
            links.remote(piece, grads.at[j, pl.ds(ROWS, ROWS)], up),
            links.remote(piece, grads.at[j, pl.ds(2 * ROWS, ROWS)], down),
        ]

    g_near = near(0) + near(1)
    outs = []
    for copy in relayed:
        copy.wait_recv()
    project(hid_of(h, 2))
    outs += [links.local(src, dst) for src, dst in ((joined, joined_out), (q, q_out), (k, k_out), (v, v_out))]
    for copy in wall_second:
        copy.wait_recv()
    wall_core = wall.at[:, :, columns]
    wall_third = [links.remote(wall_core, wall_core, (exp_of(e, 0, 0, 1), h))]
    head_sends = []
    for peer in (far, up, down, (e, h)):
        for b in range(N_HID):

            @pl.when(peer[1] == b)
            def _(b=b):
                attend_block(b, q, k, v, heads, logs_ref)

        piece = heads.at[rows_at(peer[1] * ROWS, ROWS)]
        if peer[1] is h:
            head_own = links.local(piece, hall.at[h])
        else:
            head_sends.append(links.remote(piece, hall.at[h], peer))
    for copy in g_near:
        copy.wait_recv()
    g_far = [
        links.remote(grads.at[0, pl.ds(ROWS, ROWS)], grads.at[0, pl.ds(3 * ROWS, ROWS)], up),
        links.remote(grads.at[1, pl.ds(2 * ROWS, ROWS)], grads.at[1, pl.ds(3 * ROWS, ROWS)], down),
    ]
    for copy in wall_third:
        copy.wait_recv()
    outs.append(links.local(wall, wall_out))
    head_own.wait()
    for copy in head_sends:
        copy.wait_recv()
    outs.append(links.local(hall, hall_out))
    attn_sum = dot(hall[0], wall[0])
    for i in range(1, N_HID):
        attn_sum = attn_sum + dot(hall[i], wall[i])
    residual = x_ref[...].astype(F32) + attn_sum
    residual_ref[...] = residual
    hat, _ = norm_parts(residual)
    routed = (hat * gain2_ref[...] + bias2_ref[...]).astype(BF)
    outgoing[...] = dot(pick_ref[...], routed).astype(BF)
    mine = landed.at[rows_at(e * 16, 16)]
    order = (0, 1, 3, 2)
    sent = {}
    for dz in order:
        sent[dz] = []
        for step in plane_steps((dz,)):
            t = exp_of(e, *step)
            sent[dz].append(links.remote(outgoing.at[rows_at(t * 16, 16)], mine, (t, h)))
    kept = links.local(outgoing.at[rows_at(e * 16, 16)], mine)
    waits = []
    pending = None

    def relay(chunk):
        at, first, second = chunk
        first.wait_recv()
        third = links.remote(rows.at[0, rows_at(ROWS + at, 64)], rows.at[0, rows_at(3 * ROWS + at, 64)], up)
        second.wait_recv()
        fourth = links.remote(
            rows.at[1, rows_at(2 * ROWS + at, 64)], rows.at[1, rows_at(3 * ROWS + at, 64)], down
        )
        waits.extend((third, fourth))

    for dz in order:
        if dz == 0:
            kept.wait()
        for copy in sent[dz]:
            copy.wait_recv()
        from_z = lax.rem(z - dz + 4, 4)
        at = from_z * 64
        pair = split_experts(landed[rows_at(from_z * 128, 128), :])
        for j in (0, 1):
            rows[j, rows_at(at, 64), :] = pair[j]
        piece = rows.at[:, rows_at(at, 64)]
        first = links.remote(piece, rows.at[:, rows_at(ROWS + at, 64)], up)
        second = links.remote(piece, rows.at[:, rows_at(2 * ROWS + at, 64)], down)
        if pending is not None:
            relay(pending)
        pending = (at, first, second)
        sent[dz].extend((first, second))

    def hidden(expert, block):
        here = rows_at(block * ROWS, ROWS)
        pre = dot(rows[expert, here, :], win[expert])
        root = 0.7978845608028654
        square = pre * pre
        curve = jnp.tanh(pre * (root + (root * 0.044715) * square))
        half = 0.5 + 0.5 * curve
        active = pre * half
        act[expert, here, :] = active.astype(BF)
        slope[expert] = half + active * (1.0 - curve) * (root + (3 * 0.044715 * root) * square)

    def gradient(expert, block):
        here = rows_at(block * ROWS, ROWS)
        grad_act = dot_nt(grads[expert, here, :], wdown[expert])
        grad_pre = (grad_act * slope[expert]).astype(BF)
        gpre[expert, here, :] = grad_pre
        back[expert, here, :] = dot_nt(grad_pre, win[expert]).astype(BF)

    def both(first_block, count):
        def step(i, carry):
            expert, block = lax.rem(i, 2), first_block + i // 2
            hidden(expert, block)
            gradient(expert, block)
            return carry

        lax.fori_loop(0, 2 * count, step, 0)

    def forward(first_block, count):
        def step(i, carry):
            expert, here = lax.rem(i, 2), rows_at((first_block + i // 2) * ROWS, ROWS)
            mixed[expert, here, :] = dot(act[expert, here, :], wdown[expert]).astype(BF)
            return carry

        lax.fori_loop(0, 2 * count, step, 0)

    def sent_step(i, carry):
        hidden(i, 1 + i)
        gradient(i, 1 + i)
        return carry

    def kept_step(i, carry):
        hidden(i, 2 - i)
        gradient(i, 2 - i)
        return carry

    def far_step(i, carry):
        hidden(i, 3)
        return carry

    def far_back(i, carry):
        gradient(i, 3)
        return carry

    def deliver(src, places):
        for (expert, block), place in places:
            outs.append(links.local(src.at[expert, pl.ds(block * ROWS, ROWS)], place))

    def write(src, dst, first_block, count):
        piece = pl.ds(first_block * ROWS, count * ROWS)
        outs.append(links.local(src.at[:, piece], dst.at[:, piece]))

    for copy in weights:
        copy.wait()
    both(0, 1)
    forward(0, 1)
    relay(pending)
    write(gpre, gpre_out, 0, 1)
    deliver(back, (((0, 0), own_out.at[0]), ((1, 0), own_out.at[1])))
    deliver(mixed, (((0, 0), m_own_out.at[0]), ((1, 0), m_own_out.at[1])))
    lax.fori_loop(0, 2, sent_step, 0)
    back_near = [
        links.remote(back.at[1, pl.ds(2 * ROWS, ROWS)], near_below_out, up),
        links.remote(back.at[0, pl.ds(ROWS, ROWS)], near_above_out, down),
    ]
    lax.fori_loop(0, 2, kept_step, 0)
    write(rows, rows_out, 0, 3)
    write(grads, grads_out, 0, 3)
    write(gpre, gpre_out, 1, 2)
    deliver(back, (((0, 2), low_out), ((1, 1), high_out)))
    for copy in waits:
        copy.wait_recv()
    lax.fori_loop(0, 2, far_step, 0)
    write(rows, rows_out, 3, 1)
    write(act, act_out, 0, 4)
    forward(1, 3)
    deliver(
        mixed,
        (
            ((0, 2), m_low_out), ((1, 1), m_high_out), ((1, 2), m_go_up_out.at[1]), ((0, 1), m_go_down_out.at[1]),
            ((0, 3), m_go_up_out.at[0]), ((1, 3), m_go_down_out.at[0]),
        ),
    )
    for copy in g_far:
        copy.wait_recv()
    lax.fori_loop(0, 2, far_back, 0)
    write(grads, grads_out, 3, 1)
    write(gpre, gpre_out, 3, 1)
    deliver(back, (((0, 3), go_up_out), ((1, 3), go_down_out)))
    for copy in outs + back_near:
        copy.wait()
    for dz in order:
        for copy in sent[dz]:
            copy.wait_send()
    for copy in gather + relayed + wall_sends + wall_first + wall_second + wall_third + g_sends + head_sends + g_near + g_far + waits:
        copy.wait_send()


def front_call(block_input, gain1, bias1, gain2, bias2, ids, out_grad, w_qkv, w_out, w_in, w_down):
    rows, width = N_HID * ROWS, w_qkv.shape[2]
    flat = jax.ShapeDtypeStruct((rows, width), BF)
    pair = jax.ShapeDtypeStruct((2, ROWS, WIDTH), BF)
    shares = (N_HID, ROWS, WIDTH)
    held = pltpu.VMEM((rows, width), BF)
    slots = pltpu.VMEM((SLOTS, WIDTH), BF)
    block = pltpu.VMEM((ROWS, WIDTH), BF)
    one = jax.ShapeDtypeStruct((ROWS, WIDTH), BF)
    whole = jax.ShapeDtypeStruct((2, rows, WIDTH), BF)
    held_rows = pltpu.VMEM((2, rows, WIDTH), BF)
    weight = pltpu.VMEM(w_in.shape, BF)
    return pl.pallas_call(
        front_kernel,
        out_shape=(
            jax.ShapeDtypeStruct((rows, WIDTH), BF),
            flat, flat, flat,
            jax.ShapeDtypeStruct((N_HID, ROWS, width), BF),
            jax.ShapeDtypeStruct(shares, BF),
            jax.ShapeDtypeStruct((8, rows), F32),
            jax.ShapeDtypeStruct((ROWS, WIDTH), F32),
            jax.ShapeDtypeStruct((SLOTS, ROWS), BF),
            whole, whole, whole, whole,
            pair, one, one, one, one, one, one,
            pair, one, one, pair, pair,
        ),
        in_specs=[VMEM] * 6 + [ANY] * 5,
        out_specs=[ANY] * 6 + [VMEM] * 3 + [ANY] * 16,
        scratch_shapes=[
            block, pltpu.VMEM((rows, WIDTH), BF), block, pltpu.VMEM(w_qkv.shape, BF), block, pltpu.VMEM(shares, BF),
            held, held, held, held, pltpu.VMEM((N_HID, ROWS, width), BF),
            slots, slots, slots, slots, weight, weight, held_rows, held_rows, held_rows,
            pltpu.VMEM((2, ROWS, WIDTH), F32), held_rows, held_rows, held_rows,
        ]
        + sems(5 + 7 + 4 + 32 + 13 + 4 + 2 + 4 + 4 + 2 + 32 + 16 + 30),
        compiler_params=pltpu.CompilerParams(
            collective_id=1, has_side_effects=True, vmem_limit_bytes=62 * MIB
        ),
        cost_estimate=pl.CostEstimate(flops=20 * 10**9, bytes_accessed=100 * MIB, transcendentals=0),
        name="front",
    )(block_input, gain1, bias1, gain2, bias2, ids, out_grad, w_qkv, w_out, w_in, w_down)


def weights_kernel(rows_ref, gpre_ref, act_ref, grads_ref, dwin_ref, dwdown_ref):
    dwin_ref[0] = dot_tn(rows_ref[0], gpre_ref[0])
    dwdown_ref[0] = dot_tn(act_ref[0], grads_ref[0])


def weights_call(rows, grad_pre, act, grads):
    part = WIDTH // 2
    whole = pl.BlockSpec((1, WIDTH, WIDTH), lambda i, j: (i, 0, 0))
    columns = pl.BlockSpec((1, WIDTH, part), lambda i, j: (i, 0, j))
    result = jax.ShapeDtypeStruct(rows.shape, F32)
    return pl.pallas_call(
        weights_kernel,
        grid=(2, 2),
        out_shape=(result, result),
        in_specs=[whole, columns, columns, whole],
        out_specs=[columns, pl.BlockSpec((1, part, WIDTH), lambda i, j: (i, j, 0))],
        compiler_params=pltpu.CompilerParams(vmem_limit_bytes=60 * MIB),
        cost_estimate=pl.CostEstimate(flops=86 * 10**8, bytes_accessed=32 * MIB, transcendentals=0),
        name="weights",
    )(rows, grad_pre, act, grads)


RING = (1, 3, 2)


def put_vector(vec, index, value):
    half = WIDTH // 2
    for i in (0, 1):
        row = 2 * index + i
        vec[0, row : row + 1, :] = value[:, i * half : (i + 1) * half]


def back_kernel(
    up_pass_up, up_pass_down, up_below, up_above, near_below, near_above, gain1_ref, gain2_ref, logs_ref,
    up_own_hbm, pick_hbm, residual_hbm, grad_hbm, x_hbm, wall_hbm, wqkv_hbm, joined_hbm, q_hbm, k_hbm, v_hbm, hall_hbm,
    m_own_hbm, m_low_hbm, m_high_hbm, m_go_up, m_go_down,
    out_ref, ginput_ref, dwq_ref, dwo_ref, vecsum_ref,
    up_own, pick, residual, grad_in, x, wall, wqkv, joined, q, k, v, hall, m_own, m_pass_up, m_pass_down,
    pass_up, pass_down, got, outgoing, landed, gres, gas, gheads_out, gheads,
    dwo, dwo_got, dwo_half, dwo_got1, dwo_x, dwo_got2, dwo_sum, dwo_hid,
    m_far_up, m_far_down, m_near_up, m_near_down, m_got, m_outgoing, m_landed,
    gq, gk, gv, term, t_got, half_up, half_down, t_pass_up, t_pass_down,
    dwq, dwq_got, dwq_half, dwq_got1, dwq_mid, dwq_got2, vec, vec_got, send_sem, recv_sem,
):
    e, h = place()
    z, x_at, core = e // 8, lax.rem(e // 2, 4), lax.rem(e, 2)
    up, down, far = (e, hid_of(h, 1)), (e, hid_of(h, -1)), (e, hid_of(h, 2))
    twin = (exp_of(e, 0, 0, 1), h)
    plane = plane_peers(e, h)
    peers = [up, down, far] + plane
    peers += [(exp_of(e, dz, 0, 0), hid_of(h, dy)) for dz in (1, 2, 3) for dy in (1, 2, 3)]
    signal(peers)
    links = Links(send_sem, recv_sem)

    def along(axis, d):
        return (exp_of(e, 0, d, 0) if axis == "x" else exp_of(e, d, 0, 0), h)

    def position(axis):
        return x_at if axis == "x" else z

    def scatter(axis, piece_of, got_ref):
        return [
            links.remote(piece_of(lax.rem(position(axis) + d, 4)), got_ref.at[i], along(axis, d))
            for i, d in enumerate(RING)
        ]

    def share(axis, piece):
        return [links.remote(piece, piece, along(axis, d)) for d in RING]

    def arrived(copies):
        for copy in copies:
            copy.wait_recv()
        ended.extend(copies)

    def total(own_piece, got_ref):
        whole = own_piece.astype(F32)
        for i in range(len(RING)):
            whole = whole + got_ref[i].astype(F32)
        return whole.astype(BF)

    ended = []
    load = {}
    for name, src, dst in (
        ("own", up_own_hbm, up_own), ("pick", pick_hbm, pick), ("residual", residual_hbm, residual),
        ("grad", grad_hbm, grad_in), ("wall", wall_hbm, wall), ("hall", hall_hbm, hall), ("q", q_hbm, q), ("k", k_hbm, k),
        ("v", v_hbm, v), ("wqkv", wqkv_hbm, wqkv), ("joined", joined_hbm, joined), ("x", x_hbm, x),
        ("m", m_own_hbm, m_own), ("mu", m_low_hbm, m_pass_up), ("md", m_high_hbm, m_pass_down),
    ):
        load[name] = links.local(src, dst)
    await_signals(peers)
    order = (2, 1, 3, 0)
    passed = []
    for dz in order:
        at = lax.rem(z + dz, 4) * 64
        piece = rows_at(at, 64)
        pass_up[piece, :] = (up_pass_up[piece, :].astype(F32) + up_below[piece, :].astype(F32)).astype(BF)
        five = links.remote(pass_up.at[piece], got.at[0, piece], up)
        pass_down[piece, :] = (up_pass_down[piece, :].astype(F32) + up_above[piece, :].astype(F32)).astype(BF)
        six = links.remote(pass_down.at[piece], got.at[1, piece], down)
        passed.append((at, five, six))
        ended += [five, six]
    mine = landed.at[rows_at(e * 16, 16)]
    back = []
    load["own"].wait()
    for dz, (at, five, six) in zip(order, passed):
        five.wait_recv()
        six.wait_recv()
        piece = rows_at(at, 64)
        pair = [
            up_own[j, piece, :].astype(F32) + got[j, piece, :].astype(F32) + near[piece, :].astype(F32)
            for j, near in enumerate((near_above, near_below))
        ]
        outgoing[rows_at(at * 2, 128), :] = merge_experts(*pair)
        for step in plane_steps((dz,)):
            t = exp_of(e, *step)
            back.append(links.remote(outgoing.at[rows_at(t * 16, 16)], mine, (t, h)))
    m_far = [links.remote(m_go_up.at[0], m_far_up, up), links.remote(m_go_down.at[0], m_far_down, down)]
    ended += m_far
    kept = links.local(outgoing.at[rows_at(e * 16, 16)], mine)
    kept.wait()
    for name in ("pick", "residual", "grad", "wall"):
        load[name].wait()
    load["hall"].wait()
    for copy in back:
        copy.wait_recv()
    ended += back
    routed = dot_tn(pick[...], landed[...])
    hat, scale = norm_parts(residual[...])
    put_vector(vec, 2, jnp.sum(routed * hat, axis=0, keepdims=True))
    put_vector(vec, 3, jnp.sum(routed, axis=0, keepdims=True))
    whole = grad_in[...].astype(F32) + norm_back(routed, hat, scale, gain2_ref[...])
    gres[...] = whole
    gas[...] = whole.astype(BF)
    head_sends = []
    for i, peer in enumerate((far, up, down)):
        gheads_out[i] = dot_nt(gas[...], wall[peer[1]]).astype(BF)
        head_sends.append(links.remote(gheads_out.at[i], gheads.at[rows_at(h * ROWS, ROWS)], peer))
    ended += head_sends
    gheads[rows_at(h * ROWS, ROWS), :] = dot_nt(gas[...], wall[h]).astype(BF)
    m_near = [links.remote(m_go_up.at[1], m_near_up, up), links.remote(m_go_down.at[1], m_near_down, down)]
    ended += m_near
    for i in range(N_HID):
        dwo[i] = dot_tn(hall[i], gas[...]).astype(BF)
    other = pl.ds(pl.multiple_of((1 - core) * 512, 512), 512)
    own = pl.ds(pl.multiple_of(core * 512, 512), 512)
    dwo_swap = links.remote(dwo.at[:, :, other], dwo_got, twin)
    for name in ("q", "k", "v"):
        load[name].wait()
    for copy in head_sends:
        copy.wait_recv()
    gk[...] = jnp.zeros_like(gk)
    gv[...] = jnp.zeros_like(gv)

    def attention(block):
        attend_block_back(block, q, k, v, gheads, logs_ref, gq, gk, gv)

    attention(0)
    arrived([dwo_swap])
    for i in range(N_HID):
        dwo_half[i] = (dwo[i, :, own].astype(F32) + dwo_got[i].astype(F32)).astype(BF)
    dwo_first = scatter("x", lambda t: dwo_half.at[:, rows_at(t * 64, 64)], dwo_got1)
    attention(1)
    attention(2)
    load["mu"].wait()
    load["md"].wait()
    m_far[0].wait_recv()
    m_pass_up[...] = (m_pass_up[...].astype(F32) + m_far_up[...].astype(F32)).astype(BF)
    five = links.remote(m_pass_up, m_got.at[0], up)
    m_far[1].wait_recv()
    m_pass_down[...] = (m_pass_down[...].astype(F32) + m_far_down[...].astype(F32)).astype(BF)
    six = links.remote(m_pass_down, m_got.at[1], down)
    ended += [five, six]
    attention(3)
    load["wqkv"].wait()
    load["joined"].wait()
    parts = (gq[...], gk[...].astype(BF), gv[...].astype(BF))
    for i, part in enumerate(parts):
        dwq[pl.ds(i * WIDTH, WIDTH), :] = dot_tn(joined[...], part).astype(BF)
    count = dwq.shape[0] // 2
    dwq_swap = links.remote(dwq.at[rows_at((1 - core) * count, count)], dwq_got, twin)
    arrived(dwo_first)
    dwo_x[...] = total(dwo_half[:, rows_at(x_at * 64, 64), :], dwo_got1)
    dwo_second = scatter("z", lambda t: dwo_x.at[:, rows_at(t * 16, 16)], dwo_got2)
    term[...] = sum(dot_nt(part, wqkv[i]) for i, part in enumerate(parts)).astype(BF)
    begun = reduce_begin(links, term, t_got, half_up, half_down, e, h)
    arrived(dwo_second)
    dwo_sum[...] = total(dwo_x[:, rows_at(z * 16, 16), :], dwo_got2)
    dwo_cross = [
        links.remote(dwo_sum.at[peer[1]], dwo_hid.at[i], peer) for i, peer in enumerate((far, up, down))
    ]
    arrived([dwq_swap])
    dwq_half[...] = (dwq[rows_at(core * count, count), :].astype(F32) + dwq_got[...].astype(F32)).astype(BF)
    wide, narrow = count // 8, count // 32
    ways = (("z", "x", 0), ("x", "z", count // 2))
    dwq_first = [
        scatter(one, lambda t, base=base: dwq_half.at[rows_at(base + t * wide, wide)], dwq_got1.at[j])
        for j, (one, two, base) in enumerate(ways)
    ]
    load["m"].wait()
    for copy in m_near:
        copy.wait_recv()
    five.wait_recv()
    six.wait_recv()
    for i in range(4):
        piece = pl.ds(i * 64, 64)
        pair = [
            m_own[j, piece, :].astype(F32) + m_got[j, piece, :].astype(F32) + near[piece, :].astype(F32)
            for j, near in enumerate((m_near_down, m_near_up))
        ]
        m_outgoing[pl.ds(i * 128, 128), :] = merge_experts(*pair)
    mine = m_landed.at[rows_at(e * 16, 16)]
    m_back = []
    for step in plane_steps((2, 1, 3, 0)):
        t = exp_of(e, *step)
        m_back.append(links.remote(m_outgoing.at[rows_at(t * 16, 16)], mine, (t, h)))
    m_kept = links.local(m_outgoing.at[rows_at(e * 16, 16)], mine)
    dwq_second = []
    for j, (one, two, base) in enumerate(ways):
        arrived(dwq_first[j])
        dwq_mid[j] = total(dwq_half[rows_at(base + position(one) * wide, wide), :], dwq_got1.at[j])
        dwq_second.append(scatter(two, lambda t, j=j: dwq_mid.at[j, rows_at(t * narrow, narrow)], dwq_got2.at[j]))
    arrived(dwo_cross)
    dwo_at = rows_at(x_at * 64 + z * 16, 16)
    dwo_ref[dwo_at, own] = total(dwo_sum[h], dwo_hid)
    dwo_third = share("z", dwo_ref.at[dwo_at, own])
    reduced = reduce_middle(links, begun, term, t_got, half_up, half_down, t_pass_up, t_pass_down, e, h)
    ended += reduced
    dwq_third = []
    for j, (one, two, base) in enumerate(ways):
        arrived(dwq_second[j])
        at = rows_at(core * count + base + position(one) * wide + position(two) * narrow, narrow)
        dwq_ref[at, :] = total(dwq_mid[j, rows_at(position(two) * narrow, narrow), :], dwq_got2.at[j])
        dwq_third.append(share(two, dwq_ref.at[at]))
    arrived(dwo_third)
    dwo_fourth = share("x", dwo_ref.at[rows_at(x_at * 64, 64), own])
    dwq_fourth = []
    for j, (one, two, base) in enumerate(ways):
        arrived(dwq_third[j])
        dwq_fourth.append(share(one, dwq_ref.at[rows_at(core * count + base + position(one) * wide, wide)]))
    load["x"].wait()
    grad = reduce_end(reduced, term, t_got, h)
    hat, scale = norm_parts(x[...].astype(F32))
    ginput_ref[...] = gres[...] + norm_back(grad, hat, scale, gain1_ref[...])
    put_vector(vec, 0, jnp.sum(grad * hat, axis=0, keepdims=True))
    put_vector(vec, 1, jnp.sum(grad, axis=0, keepdims=True))
    rounds = (
        [(exp_of(e, dz, 0, 0), hid_of(h, dy)) for dz in range(4) for dy in range(4) if (dz, dy) != (0, 0)],
        [(exp_of(e, 0, dx, dc), h) for dx in range(4) for dc in (0, 1) if (dx, dc) != (0, 0)],
    )
    first_round = [links.remote(vec.at[0], vec_got.at[i], peer) for i, peer in enumerate(rounds[0])]
    for j in range(len(ways)):
        arrived(dwq_fourth[j])
    dwq_twin = dwq_ref.at[rows_at(core * count, count)]
    twins = [links.remote(dwq_twin, dwq_twin, twin)]
    arrived(dwo_fourth)
    dwo_twin = dwo_ref.at[:, own]
    twins.append(links.remote(dwo_twin, dwo_twin, twin))
    arrived(first_round)
    whole = vec[0]
    for i in range(len(rounds[0])):
        whole = whole + vec_got[i]
    vec[1] = whole
    second_round = [
        links.remote(vec.at[1], vec_got.at[len(rounds[0]) + i], peer) for i, peer in enumerate(rounds[1])
    ]
    m_kept.wait()
    arrived(m_back)
    out_ref[...] = (residual[...] + dot_tn(pick[...], m_landed[...])).astype(BF)
    arrived(second_round)
    whole = vec[1]
    for i in range(len(rounds[1])):
        whole = whole + vec_got[len(rounds[0]) + i]
    vecsum_ref[...] = whole
    arrived(twins)
    for copy in ended:
        copy.wait_send()


def back_call(up_parts, gain1, gain2, logs, pick, residual, out_grad, block_input, wall, w_qkv, joined, q, k, v, hall, down_parts):
    rows, width = q.shape
    block = pltpu.VMEM((ROWS, WIDTH), BF)
    half = pltpu.VMEM((ROWS // 2, WIDTH), BF)
    pair = pltpu.VMEM((2, ROWS, WIDTH), BF)
    slots = pltpu.VMEM((SLOTS, WIDTH), BF)
    held = pltpu.VMEM((rows, width), BF)
    wide = pltpu.VMEM((rows, WIDTH), BF)
    shares = pltpu.VMEM((N_HID, ROWS, WIDTH), BF)
    half_shares = pltpu.VMEM((N_HID, ROWS, WIDTH // 2), BF)
    quarter = pltpu.VMEM((3 * WIDTH // 2, width), BF)
    return pl.pallas_call(
        back_kernel,
        out_shape=(
            jax.ShapeDtypeStruct((ROWS, WIDTH), BF),
            jax.ShapeDtypeStruct((ROWS, WIDTH), F32),
            jax.ShapeDtypeStruct((3 * WIDTH, width), BF),
            jax.ShapeDtypeStruct((ROWS, WIDTH), BF),
            jax.ShapeDtypeStruct((8, WIDTH // 2), F32),
        ),
        in_specs=[VMEM] * 9 + [ANY] * 17,
        out_specs=[VMEM] * 5,
        scratch_shapes=[
            pair, pltpu.VMEM((SLOTS, ROWS), BF), pltpu.VMEM((ROWS, WIDTH), F32),
            block, block, shares, pltpu.VMEM(w_qkv.shape, BF), wide, held, held, held,
            pltpu.VMEM((N_HID, ROWS, width), BF), pair, block, block,
            block, block, pair, slots, slots, pltpu.VMEM((ROWS, WIDTH), F32), block,
            pltpu.VMEM((3, ROWS, width), BF), held,
            shares, half_shares, half_shares, pltpu.VMEM((3, N_HID, 64, WIDTH // 2), BF), pltpu.VMEM((N_HID, 64, WIDTH // 2), BF),
            pltpu.VMEM((3, N_HID, 16, WIDTH // 2), BF), pltpu.VMEM((N_HID, 16, WIDTH // 2), BF), pltpu.VMEM((3, 16, WIDTH // 2), BF),
            block, block, block, block, pair, slots, slots,
            held, pltpu.VMEM((rows, width), F32), pltpu.VMEM((rows, width), F32),
            wide, pair, half, half, half, half,
            pltpu.VMEM((3 * WIDTH, width), BF), quarter, quarter, pltpu.VMEM((2, 3, 192, width), BF),
            pltpu.VMEM((2, 192, width), BF), pltpu.VMEM((2, 3, 48, width), BF),
            pltpu.VMEM((2, 8, WIDTH // 2), F32), pltpu.VMEM((22, 8, WIDTH // 2), F32),
        ]
        + sems(15 + 8 + 32 + 3 + 4 + 2 + 1 + 15 + 6 + 1 + 24 + 32 + 22 + 2),
        compiler_params=pltpu.CompilerParams(
            collective_id=2, has_side_effects=True, vmem_limit_bytes=62 * MIB
        ),
        cost_estimate=pl.CostEstimate(flops=12 * 10**9, bytes_accessed=100 * MIB, transcendentals=0),
        name="back",
    )(*up_parts[1:], gain1, gain2, logs, up_parts[0], pick, residual, out_grad, block_input, wall, w_qkv, joined, q, k, v, hall, *down_parts)


def finish_kernel(out_ref, ginput_ref, dwq_ref, dwo_ref, vec_ref, out, ginput, dwq, dwo, *vectors):
    out[...] = out_ref[...]
    ginput[...] = ginput_ref[...]
    dwq[...] = dwq_ref[...].astype(F32)
    dwo[...] = dwo_ref[...].astype(F32)
    for i, ref in enumerate(vectors):
        ref[:, : WIDTH // 2] = vec_ref[2 * i : 2 * i + 1, :]
        ref[:, WIDTH // 2 :] = vec_ref[2 * i + 1 : 2 * i + 2, :]


def finish_call(out, ginput, dwq, dwo, vec):
    def rows_of(array, parts):
        return pl.BlockSpec((array.shape[0] // parts, array.shape[1]), lambda i: (i, 0))

    blocks = [rows_of(array, 4) for array in (out, ginput, dwq, dwo)]
    fixed = pl.BlockSpec((8, WIDTH // 2), lambda i: (0, 0))
    vector = pl.BlockSpec((1, WIDTH), lambda i: (0, 0))
    return pl.pallas_call(
        finish_kernel,
        grid=(4,),
        out_shape=(
            jax.ShapeDtypeStruct(out.shape, BF), jax.ShapeDtypeStruct(ginput.shape, F32),
            jax.ShapeDtypeStruct(dwq.shape, F32), jax.ShapeDtypeStruct(dwo.shape, F32),
        ) + (jax.ShapeDtypeStruct((1, WIDTH), F32),) * 4,
        in_specs=blocks + [fixed],
        out_specs=blocks + [vector] * 4,
        compiler_params=pltpu.CompilerParams(vmem_limit_bytes=60 * MIB),
        cost_estimate=pl.CostEstimate(flops=0, bytes_accessed=9 * MIB, transcendentals=0),
        name="results",
    )(out, ginput, dwq, dwo, vec)


def hid_shift(rows, step):
    return lax.ppermute(rows, "hid", [(i, (i + step) % N_HID) for i in range(N_HID)])


def after(arrays, *first):
    return lax.optimization_barrier((arrays, first))[0]


def on_device(
    block_input, norm1_gain, norm1_bias, w_qkv, w_out, norm2_gain, norm2_bias,
    w_in, w_down, expert_ids, out_grad,
):
    gain1, bias1, gain2, bias2 = (
        v.reshape(1, WIDTH) for v in (norm1_gain, norm1_bias, norm2_gain, norm2_bias)
    )
    (
        joined, q, k, v, hall, wall, logs, residual, pick,
        rows, grads, act, grad_pre, up_own, up_low, up_high, go_up, go_down, near_below, near_above, *down_parts,
    ) = front_call(
        block_input, gain1, bias1, gain2, bias2, expert_ids.reshape(1, ROWS), out_grad, w_qkv, w_out, w_in, w_down
    )
    below, above = hid_shift(go_up, 1), hid_shift(go_down, -1)
    d_w_in, d_w_down = weights_call(rows, grad_pre, act, grads)
    below, above = after((below, above), d_w_in, d_w_down)
    output, grad_input, dw_qkv, dw_out, vec_sum = back_call(
        (up_own, up_low, up_high, below, above, near_below, near_above), gain1, gain2, logs, pick, residual, out_grad, block_input,
        wall, w_qkv, joined, q, k, v, hall, down_parts,
    )
    output, grad_input, d_w_qkv, d_w_out, *vectors = finish_call(output, grad_input, dw_qkv, dw_out, vec_sum)
    d_gain1, d_bias1, d_gain2, d_bias2 = (v.reshape(WIDTH) for v in vectors)
    return (
        output, grad_input, d_gain1, d_bias1, d_w_qkv.reshape(w_qkv.shape), d_w_out,
        d_gain2, d_bias2, d_w_in, d_w_down,
    )


def solution(mesh):
    in_specs = (
        P(("exp", "hid"), None), P(), P(), P(None, None, "hid"), P("hid", None), P(), P(),
        P("exp", None, "hid"), P("exp", "hid", None), P(("exp", "hid"), None), P(("exp", "hid"), None),
    )
    out_specs = (
        P(("exp", "hid"), None), P(("exp", "hid"), None), P(), P(), P(None, None, "hid"), P("hid", None),
        P(), P(), P("exp", None, "hid"), P("exp", "hid", None),
    )
    return jax.shard_map(on_device, mesh=mesh, in_specs=in_specs, out_specs=out_specs, check_vma=False)
```

```python
import jax
import jax.numpy as jnp
from jax import lax
from jax.experimental import pallas as pl
from jax.experimental.pallas import tpu as pltpu
from jax.sharding import PartitionSpec as P

HD = 64
EPSILON = 1e-05
NEG_LARGE = -1e30
BF = jnp.bfloat16
F32 = jnp.float32
MESH = pl.DeviceIdType.MESH
ANY = pl.BlockSpec(memory_space=pl.ANY)
VMEM = pl.BlockSpec(memory_space=pltpu.VMEM)
N_HID = 4
N_EXP = 32
ROWS = 256
WIDTH = 1024
SLOTS = 512
MIB = 1 << 20


def dot(a, b):
    return jnp.dot(a, b, preferred_element_type=F32)


def dot_nt(a, b):
    return lax.dot_general(a, b, (((1,), (1,)), ((), ())), preferred_element_type=F32)


def dot_tn(a, b):
    return lax.dot_general(a, b, (((0,), (0,)), ((), ())), preferred_element_type=F32)


def place():
    return lax.axis_index("exp"), lax.axis_index("hid")


def hid_of(h, step):
    return lax.rem(h + step + N_HID, N_HID)


def exp_of(e, dz, dx, dc):
    z, x, c = e // 8, lax.rem(e // 2, 4), lax.rem(e, 2)
    return (lax.rem(z + dz, 4) * 4 + lax.rem(x + dx, 4)) * 2 + lax.rem(c + dc, 2)


def plane_steps(order):
    return [
        (dz, dx, dc)
        for dz in order
        for dx in (0, 1, 3, 2)
        for dc in (0, 1)
        if (dz, dx, dc) != (0, 0, 0)
    ]


def signal(peers):
    barrier = pltpu.get_barrier_semaphore()
    for peer in peers:
        pl.semaphore_signal(barrier, inc=1, device_id=peer, device_id_type=MESH)


def await_signals(peers):
    pl.semaphore_wait(pltpu.get_barrier_semaphore(), len(peers))


class Links:
    def __init__(self, send_sem, recv_sem):
        self.send_sem, self.recv_sem, self.used = send_sem, recv_sem, 0

    def remote(self, src, dst, peer):
        i = self.used
        self.used += 1
        copy = pltpu.make_async_remote_copy(
            src_ref=src,
            dst_ref=dst,
            send_sem=self.send_sem.at[i],
            recv_sem=self.recv_sem.at[i],
            device_id=peer,
            device_id_type=MESH,
        )
        copy.start()
        return copy

    def local(self, src, dst):
        i = self.used
        self.used += 1
        copy = pltpu.make_async_copy(src, dst, self.send_sem.at[i])
        copy.start()
        return copy


def rows_at(start, size, unit=16):
    return pl.ds(pl.multiple_of(start, unit), size)


def split_experts(block):
    n = block.shape[0] // 16
    wide = block.astype(F32).reshape(n, 2, 8, block.shape[1])
    return [wide[:, i].reshape(n * 8, block.shape[1]).astype(BF) for i in (0, 1)]


def merge_experts(first, second):
    n, width = first.shape[0] // 8, first.shape[1]
    pair = jnp.concatenate(
        [first.reshape(n, 1, 8, width), second.reshape(n, 1, 8, width)], axis=1
    )
    return pair.reshape(n * 16, width).astype(BF)


def norm_parts(rows):
    centered = rows - jnp.mean(rows, -1, keepdims=True)
    scale = lax.rsqrt(jnp.mean(centered * centered, -1, keepdims=True) + EPSILON)
    return centered * scale, scale


def norm_back(grad, hat, scale, gain):
    gh = grad * gain
    inner = jnp.mean(gh * hat, -1, keepdims=True)
    return scale * (gh - jnp.mean(gh, -1, keepdims=True) - hat * inner)


def slot_picks(ids):
    named = jnp.where(ids == lax.broadcasted_iota(jnp.int32, (128, ROWS), 0), 1.0, 0.0)
    earlier = jnp.where(
        lax.broadcasted_iota(jnp.int32, (ROWS, ROWS), 0)
        < lax.broadcasted_iota(jnp.int32, (ROWS, ROWS), 1),
        1.0,
        0.0,
    )
    running = dot(named.astype(BF), earlier.astype(BF))
    position = jnp.sum(running * named, axis=0, keepdims=True).astype(jnp.int32)
    slot = ids * 8 + position
    return jnp.where(slot == lax.broadcasted_iota(jnp.int32, (SLOTS, ROWS), 0), 1.0, 0.0).astype(BF)


def gather_begin(links, src, out, e, h):
    half = ROWS // 2
    copies = []
    for first, peer in ((0, (e, hid_of(h, 1))), (half, (e, hid_of(h, -1)))):
        for start in (first, half - first):
            piece = out.at[rows_at(h * ROWS + start, half)]
            copies.append(links.remote(src.at[pl.ds(start, half)], piece, peer))
    return copies, links.local(src, out.at[rows_at(h * ROWS, ROWS)])


def gather_relay(links, copies, out, e, h):
    half = ROWS // 2
    relayed = []
    for copy, block, start, peer in (
        (copies[0], hid_of(h, -1), 0, (e, hid_of(h, 1))),
        (copies[2], hid_of(h, 1), half, (e, hid_of(h, -1))),
    ):
        copy.wait_recv()
        piece = out.at[rows_at(block * ROWS + start, half)]
        relayed.append(links.remote(piece, piece, peer))
    return relayed


def reduce_begin(links, term, got, half_up, half_down, e, h):
    up, down = (e, hid_of(h, 1)), (e, hid_of(h, -1))
    half = ROWS // 2
    far, above, below = hid_of(h, 2) * ROWS, hid_of(h, 1) * ROWS, hid_of(h, -1) * ROWS
    one = links.remote(term.at[rows_at(far, half)], half_up, up)
    two = links.remote(term.at[rows_at(far + half, half)], half_down, down)
    three = links.remote(term.at[rows_at(above + half, half)], got.at[0, pl.ds(half, half)], up)
    four = links.remote(term.at[rows_at(below, half)], got.at[1, pl.ds(0, half)], down)
    return one, two, three, four


def reduce_middle(links, begun, term, got, half_up, half_down, pass_up, pass_down, e, h):
    up, down = (e, hid_of(h, 1)), (e, hid_of(h, -1))
    half = ROWS // 2
    above, below = hid_of(h, 1) * ROWS, hid_of(h, -1) * ROWS
    one, two, three, four = begun
    one.wait_recv()
    pass_up[...] = (
        term[rows_at(above, half), :].astype(F32) + half_up[...].astype(F32)
    ).astype(BF)
    five = links.remote(pass_up, got.at[0, pl.ds(0, half)], up)
    two.wait_recv()
    pass_down[...] = (
        term[rows_at(below + half, half), :].astype(F32) + half_down[...].astype(F32)
    ).astype(BF)
    six = links.remote(pass_down, got.at[1, pl.ds(half, half)], down)
    return one, two, three, four, five, six


def reduce_end(copies, term, got, h):
    for copy in copies[2:]:
        copy.wait_recv()
    return (
        term[rows_at(h * ROWS, ROWS), :].astype(F32)
        + got[0].astype(F32)
        + got[1].astype(F32)
    )


def reduce_scratch():
    half = ROWS // 2
    return [pltpu.VMEM((2, ROWS, WIDTH), BF)] + [pltpu.VMEM((half, WIDTH), BF)] * 4


def sems(count):
    return [pltpu.SemaphoreType.DMA((count,)), pltpu.SemaphoreType.DMA((count,))]


def hid_peers(e, h):
    return [(e, hid_of(h, 1)), (e, hid_of(h, -1))]


def plane_peers(e, h):
    return [(exp_of(e, *step), h) for step in plane_steps((0, 1, 3, 2))]


def head_lanes(shape, head):
    return lax.broadcasted_iota(jnp.int32, shape, 1) // HD == head


def causal_tail(scores_t):
    keys, queries = scores_t.shape
    tail = scores_t[keys - queries :]
    allowed = lax.broadcasted_iota(jnp.int32, tail.shape, 0) <= lax.broadcasted_iota(
        jnp.int32, tail.shape, 1
    )
    tail = jnp.where(allowed, tail, NEG_LARGE)
    if keys == queries:
        return tail
    return jnp.concatenate([scores_t[: keys - queries], tail], axis=0)


def by_head(rows):
    return [
        jnp.where(head_lanes(rows.shape, head), rows, jnp.zeros_like(rows))
        for head in range(rows.shape[1] // HD)
    ]


def own_lanes(parts):
    whole = parts[0]
    for head in range(1, len(parts)):
        whole = jnp.where(head_lanes(whole.shape, head), parts[head], whole)
    return whole


def attend_block(block, q, k, v, heads, logs):
    keys, here = pl.ds(0, (block + 1) * ROWS), pl.ds(block * ROWS, ROWS)
    parts = []
    for head, query in enumerate(by_head(q[here, :] * BF(HD**-0.5))):
        scores = causal_tail(dot_nt(k[keys, :], query))
        top = jnp.max(scores, axis=0, keepdims=True)
        exps = jnp.exp(scores - top)
        summed = jnp.sum(exps, axis=0, keepdims=True)
        logs[head : head + 1, here] = top + jnp.log(summed)
        parts.append(dot_tn((exps * (1.0 / summed)).astype(BF), v[keys, :]))
    heads[here, :] = own_lanes(parts).astype(BF)


def attend_block_back(block, q, k, v, gheads, logs, gq, gk, gv):
    keys, here = pl.ds(0, (block + 1) * ROWS), pl.ds(block * ROWS, ROWS)
    queries, grads = by_head(q[here, :] * BF(HD**-0.5)), by_head(gheads[here, :])
    keys_t = k[keys, :].T
    parts, sum_v, sum_k = [], 0.0, 0.0
    for head, (query, grad) in enumerate(zip(queries, grads)):
        scores = causal_tail(dot_nt(k[keys, :], query))
        probs = jnp.exp(scores - logs[head : head + 1, here])
        weighted = probs * dot_nt(v[keys, :], grad)
        inner = jnp.sum(weighted, axis=0, keepdims=True)
        grad_scores = (weighted - probs * inner).astype(BF)
        sum_v = sum_v + dot(probs.astype(BF), grad)
        sum_k = sum_k + dot(grad_scores, query)
        parts.append(dot(keys_t[head * HD : (head + 1) * HD], grad_scores))
    gq[here, :] = (jnp.concatenate(parts, axis=0).T * HD**-0.5).astype(BF)
    gv[keys, :] += sum_v
    gk[keys, :] += sum_k


def front_kernel(
    x_ref, gain1_ref, bias1_ref, gain2_ref, bias2_ref, ids_ref, grad_hbm, wqkv_hbm, wout_hbm, win_hbm, wdown_hbm,
    joined_out, q_out, k_out, v_out, hall_out, wall_out, logs_ref, residual_ref, pick_ref,
    rows_out, grads_out, act_out, gpre_out, own_out, low_out, high_out, go_up_out, go_down_out, near_below_out, near_above_out,
    m_own_out, m_low_out, m_high_out, m_go_up_out, m_go_down_out,
    normed, joined, grad, wqkv, wout, wall, q, k, v, heads, hall,
    outgoing_g, landed_g, outgoing, landed, win, wdown, rows, grads, act, slope, gpre, back, mixed, send_sem, recv_sem,
):
    e, h = place()
    z, x_at, core = e // 8, lax.rem(e // 2, 4), lax.rem(e, 2)
    up, down, far = (e, hid_of(h, 1)), (e, hid_of(h, -1)), (e, hid_of(h, 2))
    peers = [up, down, far] + plane_peers(e, h)
    signal(peers)
    links = Links(send_sem, recv_sem)
    loads = [links.local(wout_hbm, wout), links.local(grad_hbm, grad), links.local(wqkv_hbm, wqkv)]
    weights = [links.local(win_hbm, win), links.local(wdown_hbm, wdown)]
    hat, _ = norm_parts(x_ref[...].astype(F32))
    normed[...] = (hat * gain1_ref[...] + bias1_ref[...]).astype(BF)
    await_signals(peers)
    gather, gather_own = gather_begin(links, normed, joined, e, h)
    loads[0].wait()
    columns = pl.ds(pl.multiple_of(core * 512, 512), 512)
    along_z, along_x = x_at * 64 + z * 16, z * 64 + x_at * 16
    turned = h // 2
    wall_row = rows_at(along_z * (1 - turned) + along_x * turned, 16)
    share, share_place = wout.at[wall_row, columns], wall.at[h, wall_row, columns]
    wall_sends = [links.remote(share, share_place, peer) for peer in (up, down, far)]
    wall_kept = links.local(share, share_place)
    pick = slot_picks(ids_ref[...])
    pick_ref[...] = pick
    loads[1].wait()
    outgoing_g[...] = dot(pick, grad[...]).astype(BF)
    mine = landed_g.at[rows_at(e * 16, 16)]
    g_sends = []
    for step in plane_steps((0, 1, 3, 2)):
        t = exp_of(e, *step)
        g_sends.append(links.remote(outgoing_g.at[rows_at(t * 16, 16)], mine, (t, h)))
    g_kept = links.local(outgoing_g.at[rows_at(e * 16, 16)], mine)
    wall_kept.wait()
    for copy in wall_sends:
        copy.wait_recv()

    def to_ring(axis, piece):
        steps = [(0, d, 0) if axis == "x" else (d, 0, 0) for d in (1, 3, 2)]
        return [links.remote(piece, piece, (exp_of(e, *step), h)) for step in steps]

    low_half, high_half = pl.ds(0, 2), pl.ds(2, 2)
    wall_first = to_ring("z", wall.at[low_half, rows_at(along_z, 16), columns])
    wall_first += to_ring("x", wall.at[high_half, rows_at(along_x, 16), columns])

    def project(block):
        here = rows_at(block * ROWS, ROWS)
        block_rows = joined[here, :]
        for i, ref in enumerate((q, k, v)):
            ref[here, :] = dot(block_rows, wqkv[i]).astype(BF)

    gather_own.wait()
    loads[2].wait()
    project(h)
    relayed = gather_relay(links, gather, joined, e, h)
    for copy in wall_first:
        copy.wait_recv()
    wall_second = to_ring("x", wall.at[low_half, rows_at(x_at * 64, 64), columns])
    wall_second += to_ring("z", wall.at[high_half, rows_at(z * 64, 64), columns])
    gather[1].wait_recv()
    project(hid_of(h, -1))
    gather[3].wait_recv()
    project(hid_of(h, 1))
    g_kept.wait()
    for copy in g_sends:
        copy.wait_recv()
    for i in range(4):
        pair = split_experts(landed_g[pl.ds(i * 128, 128), :])
        for j in (0, 1):
            grads[j, pl.ds(i * 64, 64), :] = pair[j]

    def near(j):
        piece = grads.at[j, pl.ds(0, ROWS)]
        return [
            links.remote(piece, grads.at[j, pl.ds(ROWS, ROWS)], up),
            links.remote(piece, grads.at[j, pl.ds(2 * ROWS, ROWS)], down),
        ]

    g_near = near(0) + near(1)
    outs = []
    for copy in relayed:
        copy.wait_recv()
    project(hid_of(h, 2))
    outs += [links.local(src, dst) for src, dst in ((joined, joined_out), (q, q_out), (k, k_out), (v, v_out))]
    for copy in wall_second:
        copy.wait_recv()
    wall_core = wall.at[:, :, columns]
    wall_third = [links.remote(wall_core, wall_core, (exp_of(e, 0, 0, 1), h))]
    head_sends = []
    for peer in (far, up, down, (e, h)):
        for b in range(N_HID):

            @pl.when(peer[1] == b)
            def _(b=b):
                attend_block(b, q, k, v, heads, logs_ref)

        piece = heads.at[rows_at(peer[1] * ROWS, ROWS)]
        if peer[1] is h:
            head_own = links.local(piece, hall.at[h])
        else:
            head_sends.append(links.remote(piece, hall.at[h], peer))
    for copy in g_near:
        copy.wait_recv()
    g_far = [
        links.remote(grads.at[0, pl.ds(ROWS, ROWS)], grads.at[0, pl.ds(3 * ROWS, ROWS)], up),
        links.remote(grads.at[1, pl.ds(2 * ROWS, ROWS)], grads.at[1, pl.ds(3 * ROWS, ROWS)], down),
    ]
    for copy in wall_third:
        copy.wait_recv()
    outs.append(links.local(wall, wall_out))
    head_own.wait()
    for copy in head_sends:
        copy.wait_recv()
    outs.append(links.local(hall, hall_out))
    attn_sum = dot(hall[0], wall[0])
    for i in range(1, N_HID):
        attn_sum = attn_sum + dot(hall[i], wall[i])
    residual = x_ref[...].astype(F32) + attn_sum
    residual_ref[...] = residual
    hat, _ = norm_parts(residual)
    routed = (hat * gain2_ref[...] + bias2_ref[...]).astype(BF)
    outgoing[...] = dot(pick_ref[...], routed).astype(BF)
    mine = landed.at[rows_at(e * 16, 16)]
    order = (0, 1, 3, 2)
    sent = {}
    for dz in order:
        sent[dz] = []
        for step in plane_steps((dz,)):
            t = exp_of(e, *step)
            sent[dz].append(links.remote(outgoing.at[rows_at(t * 16, 16)], mine, (t, h)))
    kept = links.local(outgoing.at[rows_at(e * 16, 16)], mine)
    waits = []
    pending = None

    def relay(chunk):
        at, first, second = chunk
        first.wait_recv()
        third = links.remote(rows.at[0, rows_at(ROWS + at, 64)], rows.at[0, rows_at(3 * ROWS + at, 64)], up)
        second.wait_recv()
        fourth = links.remote(
            rows.at[1, rows_at(2 * ROWS + at, 64)], rows.at[1, rows_at(3 * ROWS + at, 64)], down
        )
        waits.extend((third, fourth))

    for dz in order:
        if dz == 0:
            kept.wait()
        for copy in sent[dz]:
            copy.wait_recv()
        from_z = lax.rem(z - dz + 4, 4)
        at = from_z * 64
        pair = split_experts(landed[rows_at(from_z * 128, 128), :])
        for j in (0, 1):
            rows[j, rows_at(at, 64), :] = pair[j]
        piece = rows.at[:, rows_at(at, 64)]
        first = links.remote(piece, rows.at[:, rows_at(ROWS + at, 64)], up)
        second = links.remote(piece, rows.at[:, rows_at(2 * ROWS + at, 64)], down)
        if pending is not None:
            relay(pending)
        pending = (at, first, second)
        sent[dz].extend((first, second))

    def hidden(expert, block):
        here = rows_at(block * ROWS, ROWS)
        pre = dot(rows[expert, here, :], win[expert])
        root = 0.7978845608028654
        square = pre * pre
        curve = jnp.tanh(pre * (root + (root * 0.044715) * square))
        half = 0.5 + 0.5 * curve
        active = pre * half
        act[expert, here, :] = active.astype(BF)
        slope[expert] = half + active * (1.0 - curve) * (root + (3 * 0.044715 * root) * square)

    def gradient(expert, block):
        here = rows_at(block * ROWS, ROWS)
        grad_act = dot_nt(grads[expert, here, :], wdown[expert])
        grad_pre = (grad_act * slope[expert]).astype(BF)
        gpre[expert, here, :] = grad_pre
        back[expert, here, :] = dot_nt(grad_pre, win[expert]).astype(BF)

    def both(first_block, count):
        def step(i, carry):
            expert, block = lax.rem(i, 2), first_block + i // 2
            hidden(expert, block)
            gradient(expert, block)
            return carry

        lax.fori_loop(0, 2 * count, step, 0)

    def forward(first_block, count):
        def step(i, carry):
            expert, here = lax.rem(i, 2), rows_at((first_block + i // 2) * ROWS, ROWS)
            mixed[expert, here, :] = dot(act[expert, here, :], wdown[expert]).astype(BF)
            return carry

        lax.fori_loop(0, 2 * count, step, 0)

    def sent_step(i, carry):
        hidden(i, 1 + i)
        gradient(i, 1 + i)
        return carry

    def kept_step(i, carry):
        hidden(i, 2 - i)
        gradient(i, 2 - i)
        return carry

    def far_step(i, carry):
        hidden(i, 3)
        return carry

    def far_back(i, carry):
        gradient(i, 3)
        return carry

    def deliver(src, places):
        for (expert, block), place in places:
            outs.append(links.local(src.at[expert, pl.ds(block * ROWS, ROWS)], place))

    def write(src, dst, first_block, count):
        piece = pl.ds(first_block * ROWS, count * ROWS)
        outs.append(links.local(src.at[:, piece], dst.at[:, piece]))

    for copy in weights:
        copy.wait()
    both(0, 1)
    forward(0, 1)
    relay(pending)
    write(gpre, gpre_out, 0, 1)
    deliver(back, (((0, 0), own_out.at[0]), ((1, 0), own_out.at[1])))
    deliver(mixed, (((0, 0), m_own_out.at[0]), ((1, 0), m_own_out.at[1])))
    lax.fori_loop(0, 2, sent_step, 0)
    back_near = [
        links.remote(back.at[1, pl.ds(2 * ROWS, ROWS)], near_below_out, up),
        links.remote(back.at[0, pl.ds(ROWS, ROWS)], near_above_out, down),
    ]
    lax.fori_loop(0, 2, kept_step, 0)
    write(rows, rows_out, 0, 3)
    write(grads, grads_out, 0, 3)
    write(gpre, gpre_out, 1, 2)
    deliver(back, (((0, 2), low_out), ((1, 1), high_out)))
    for copy in waits:
        copy.wait_recv()
    lax.fori_loop(0, 2, far_step, 0)
    write(rows, rows_out, 3, 1)
    write(act, act_out, 0, 4)
    forward(1, 3)
    deliver(
        mixed,
        (
            ((0, 2), m_low_out), ((1, 1), m_high_out), ((1, 2), m_go_up_out.at[1]), ((0, 1), m_go_down_out.at[1]),
            ((0, 3), m_go_up_out.at[0]), ((1, 3), m_go_down_out.at[0]),
        ),
    )
    for copy in g_far:
        copy.wait_recv()
    lax.fori_loop(0, 2, far_back, 0)
    write(grads, grads_out, 3, 1)
    write(gpre, gpre_out, 3, 1)
    deliver(back, (((0, 3), go_up_out), ((1, 3), go_down_out)))
    for copy in outs + back_near:
        copy.wait()
    for dz in order:
        for copy in sent[dz]:
            copy.wait_send()
    for copy in gather + relayed + wall_sends + wall_first + wall_second + wall_third + g_sends + head_sends + g_near + g_far + waits:
        copy.wait_send()


def front_call(block_input, gain1, bias1, gain2, bias2, ids, out_grad, w_qkv, w_out, w_in, w_down):
    rows, width = N_HID * ROWS, w_qkv.shape[2]
    flat = jax.ShapeDtypeStruct((rows, width), BF)
    pair = jax.ShapeDtypeStruct((2, ROWS, WIDTH), BF)
    shares = (N_HID, ROWS, WIDTH)
    held = pltpu.VMEM((rows, width), BF)
    slots = pltpu.VMEM((SLOTS, WIDTH), BF)
    block = pltpu.VMEM((ROWS, WIDTH), BF)
    one = jax.ShapeDtypeStruct((ROWS, WIDTH), BF)
    whole = jax.ShapeDtypeStruct((2, rows, WIDTH), BF)
    held_rows = pltpu.VMEM((2, rows, WIDTH), BF)
    weight = pltpu.VMEM(w_in.shape, BF)
    return pl.pallas_call(
        front_kernel,
        out_shape=(
            jax.ShapeDtypeStruct((rows, WIDTH), BF),
            flat, flat, flat,
            jax.ShapeDtypeStruct((N_HID, ROWS, width), BF),
            jax.ShapeDtypeStruct(shares, BF),
            jax.ShapeDtypeStruct((8, rows), F32),
            jax.ShapeDtypeStruct((ROWS, WIDTH), F32),
            jax.ShapeDtypeStruct((SLOTS, ROWS), BF),
            whole, whole, whole, whole,
            pair, one, one, one, one, one, one,
            pair, one, one, pair, pair,
        ),
        in_specs=[VMEM] * 6 + [ANY] * 5,
        out_specs=[ANY] * 6 + [VMEM] * 3 + [ANY] * 16,
        scratch_shapes=[
            block, pltpu.VMEM((rows, WIDTH), BF), block, pltpu.VMEM(w_qkv.shape, BF), block, pltpu.VMEM(shares, BF),
            held, held, held, held, pltpu.VMEM((N_HID, ROWS, width), BF),
            slots, slots, slots, slots, weight, weight, held_rows, held_rows, held_rows,
            pltpu.VMEM((2, ROWS, WIDTH), F32), held_rows, held_rows, held_rows,
        ]
        + sems(5 + 7 + 4 + 32 + 13 + 4 + 2 + 4 + 4 + 2 + 32 + 16 + 30),
        compiler_params=pltpu.CompilerParams(
            collective_id=1, has_side_effects=True, vmem_limit_bytes=62 * MIB
        ),
        cost_estimate=pl.CostEstimate(flops=20 * 10**9, bytes_accessed=100 * MIB, transcendentals=0),
        name="front",
    )(block_input, gain1, bias1, gain2, bias2, ids, out_grad, w_qkv, w_out, w_in, w_down)


def weights_kernel(rows_ref, gpre_ref, act_ref, grads_ref, dwin_ref, dwdown_ref):
    dwin_ref[0] = dot_tn(rows_ref[0], gpre_ref[0])
    dwdown_ref[0] = dot_tn(act_ref[0], grads_ref[0])


def weights_call(rows, grad_pre, act, grads):
    part = WIDTH // 2
    whole = pl.BlockSpec((1, WIDTH, WIDTH), lambda i, j: (i, 0, 0))
    columns = pl.BlockSpec((1, WIDTH, part), lambda i, j: (i, 0, j))
    result = jax.ShapeDtypeStruct(rows.shape, F32)
    return pl.pallas_call(
        weights_kernel,
        grid=(2, 2),
        out_shape=(result, result),
        in_specs=[whole, columns, columns, whole],
        out_specs=[columns, pl.BlockSpec((1, part, WIDTH), lambda i, j: (i, j, 0))],
        compiler_params=pltpu.CompilerParams(vmem_limit_bytes=60 * MIB),
        cost_estimate=pl.CostEstimate(flops=86 * 10**8, bytes_accessed=32 * MIB, transcendentals=0),
        name="weights",
    )(rows, grad_pre, act, grads)


RING = (1, 3, 2)


def put_vector(vec, index, value):
    half = WIDTH // 2
    for i in (0, 1):
        row = 2 * index + i
        vec[0, row : row + 1, :] = value[:, i * half : (i + 1) * half]


def back_kernel(
    up_pass_up, up_pass_down, up_below, up_above, gain1_ref, gain2_ref, logs_ref,
    near_below_hbm, near_above_hbm, up_own_hbm, pick_hbm, residual_hbm, grad_hbm, x_hbm, wall_hbm, wqkv_hbm, joined_hbm, q_hbm, k_hbm, v_hbm, hall_hbm,
    m_own_hbm, m_low_hbm, m_high_hbm, m_go_up, m_go_down,
    out_ref, ginput_ref, dwq_ref, dwo_ref, vecsum_ref,
    near_below, near_above, up_own, pick, residual, grad_in, x, wall, wqkv, joined, q, k, v, hall, m_own, m_pass_up, m_pass_down,
    pass_up, pass_down, got, outgoing, landed, gres, gas, gheads_out, gheads,
    dwo, dwo_got, dwo_half, dwo_got1, dwo_x, dwo_got2, dwo_sum, dwo_hid,
    m_far_up, m_far_down, m_near_up, m_near_down, m_got, m_outgoing, m_landed,
    gq, gk, gv, term, t_got, half_up, half_down, t_pass_up, t_pass_down,
    dwq, dwq_got, dwq_half, dwq_got1, dwq_mid, dwq_got2, vec, vec_got, send_sem, recv_sem,
):
    e, h = place()
    z, x_at, core = e // 8, lax.rem(e // 2, 4), lax.rem(e, 2)
    up, down, far = (e, hid_of(h, 1)), (e, hid_of(h, -1)), (e, hid_of(h, 2))
    twin = (exp_of(e, 0, 0, 1), h)
    plane = plane_peers(e, h)
    peers = [up, down, far] + plane
    peers += [(exp_of(e, dz, 0, 0), hid_of(h, dy)) for dz in (1, 2, 3) for dy in (1, 2, 3)]
    signal(peers)
    links = Links(send_sem, recv_sem)

    def along(axis, d):
        return (exp_of(e, 0, d, 0) if axis == "x" else exp_of(e, d, 0, 0), h)

    def position(axis):
        return x_at if axis == "x" else z

    def scatter(axis, piece_of, got_ref):
        return [
            links.remote(piece_of(lax.rem(position(axis) + d, 4)), got_ref.at[i], along(axis, d))
            for i, d in enumerate(RING)
        ]

    def share(axis, piece):
        return [links.remote(piece, piece, along(axis, d)) for d in RING]

    def arrived(copies):
        for copy in copies:
            copy.wait_recv()
        ended.extend(copies)

    def total(own_piece, got_ref):
        whole = own_piece.astype(F32)
        for i in range(len(RING)):
            whole = whole + got_ref[i].astype(F32)
        return whole.astype(BF)

    ended = []
    load = {}
    for name, src, dst in (
        ("below", near_below_hbm, near_below), ("above", near_above_hbm, near_above), ("own", up_own_hbm, up_own), ("pick", pick_hbm, pick), ("residual", residual_hbm, residual),
        ("grad", grad_hbm, grad_in), ("wall", wall_hbm, wall), ("hall", hall_hbm, hall), ("q", q_hbm, q), ("k", k_hbm, k),
        ("v", v_hbm, v), ("wqkv", wqkv_hbm, wqkv), ("joined", joined_hbm, joined), ("x", x_hbm, x),
        ("m", m_own_hbm, m_own), ("mu", m_low_hbm, m_pass_up), ("md", m_high_hbm, m_pass_down),
    ):
        load[name] = links.local(src, dst)
    await_signals(peers)
    order = (2, 1, 3, 0)
    passed = []
    for dz in order:
        at = lax.rem(z + dz, 4) * 64
        piece = rows_at(at, 64)
        pass_up[piece, :] = (up_pass_up[piece, :].astype(F32) + up_below[piece, :].astype(F32)).astype(BF)
        five = links.remote(pass_up.at[piece], got.at[0, piece], up)
        pass_down[piece, :] = (up_pass_down[piece, :].astype(F32) + up_above[piece, :].astype(F32)).astype(BF)
        six = links.remote(pass_down.at[piece], got.at[1, piece], down)
        passed.append((at, five, six))
        ended += [five, six]
    mine = landed.at[rows_at(e * 16, 16)]
    back = []
    for name in ("below", "above", "own"):
        load[name].wait()
    for dz, (at, five, six) in zip(order, passed):
        five.wait_recv()
        six.wait_recv()
        piece = rows_at(at, 64)
        pair = [
            up_own[j, piece, :].astype(F32) + got[j, piece, :].astype(F32) + near[piece, :].astype(F32)
            for j, near in enumerate((near_above, near_below))
        ]
        outgoing[rows_at(at * 2, 128), :] = merge_experts(*pair)
        for step in plane_steps((dz,)):
            t = exp_of(e, *step)
            back.append(links.remote(outgoing.at[rows_at(t * 16, 16)], mine, (t, h)))
    m_far = [links.remote(m_go_up.at[0], m_far_up, up), links.remote(m_go_down.at[0], m_far_down, down)]
    ended += m_far
    kept = links.local(outgoing.at[rows_at(e * 16, 16)], mine)
    kept.wait()
    for name in ("pick", "residual", "grad", "wall"):
        load[name].wait()
    load["hall"].wait()
    for copy in back:
        copy.wait_recv()
    ended += back
    routed = dot_tn(pick[...], landed[...])
    hat, scale = norm_parts(residual[...])
    put_vector(vec, 2, jnp.sum(routed * hat, axis=0, keepdims=True))
    put_vector(vec, 3, jnp.sum(routed, axis=0, keepdims=True))
    whole = grad_in[...].astype(F32) + norm_back(routed, hat, scale, gain2_ref[...])
    gres[...] = whole
    gas[...] = whole.astype(BF)
    head_sends = []
    for i, peer in enumerate((far, up, down)):
        gheads_out[i] = dot_nt(gas[...], wall[peer[1]]).astype(BF)
        head_sends.append(links.remote(gheads_out.at[i], gheads.at[rows_at(h * ROWS, ROWS)], peer))
    ended += head_sends
    gheads[rows_at(h * ROWS, ROWS), :] = dot_nt(gas[...], wall[h]).astype(BF)
    m_near = [links.remote(m_go_up.at[1], m_near_up, up), links.remote(m_go_down.at[1], m_near_down, down)]
    ended += m_near
    for i in range(N_HID):
        dwo[i] = dot_tn(hall[i], gas[...]).astype(BF)
    other = pl.ds(pl.multiple_of((1 - core) * 512, 512), 512)
    own = pl.ds(pl.multiple_of(core * 512, 512), 512)
    dwo_swap = links.remote(dwo.at[:, :, other], dwo_got, twin)
    for name in ("q", "k", "v"):
        load[name].wait()
    for copy in head_sends:
        copy.wait_recv()
    gk[...] = jnp.zeros_like(gk)
    gv[...] = jnp.zeros_like(gv)

    def attention(block):
        attend_block_back(block, q, k, v, gheads, logs_ref, gq, gk, gv)

    attention(0)
    arrived([dwo_swap])
    for i in range(N_HID):
        dwo_half[i] = (dwo[i, :, own].astype(F32) + dwo_got[i].astype(F32)).astype(BF)
    dwo_first = scatter("x", lambda t: dwo_half.at[:, rows_at(t * 64, 64)], dwo_got1)
    attention(1)
    attention(2)
    load["mu"].wait()
    load["md"].wait()
    m_far[0].wait_recv()
    m_pass_up[...] = (m_pass_up[...].astype(F32) + m_far_up[...].astype(F32)).astype(BF)
    five = links.remote(m_pass_up, m_got.at[0], up)
    m_far[1].wait_recv()
    m_pass_down[...] = (m_pass_down[...].astype(F32) + m_far_down[...].astype(F32)).astype(BF)
    six = links.remote(m_pass_down, m_got.at[1], down)
    ended += [five, six]
    attention(3)
    load["wqkv"].wait()
    load["joined"].wait()
    parts = (gq[...], gk[...].astype(BF), gv[...].astype(BF))
    for i, part in enumerate(parts):
        dwq[pl.ds(i * WIDTH, WIDTH), :] = dot_tn(joined[...], part).astype(BF)
    count = dwq.shape[0] // 2
    dwq_swap = links.remote(dwq.at[rows_at((1 - core) * count, count)], dwq_got, twin)
    arrived(dwo_first)
    dwo_x[...] = total(dwo_half[:, rows_at(x_at * 64, 64), :], dwo_got1)
    dwo_second = scatter("z", lambda t: dwo_x.at[:, rows_at(t * 16, 16)], dwo_got2)
    term[...] = sum(dot_nt(part, wqkv[i]) for i, part in enumerate(parts)).astype(BF)
    begun = reduce_begin(links, term, t_got, half_up, half_down, e, h)
    arrived(dwo_second)
    dwo_sum[...] = total(dwo_x[:, rows_at(z * 16, 16), :], dwo_got2)
    dwo_cross = [
        links.remote(dwo_sum.at[peer[1]], dwo_hid.at[i], peer) for i, peer in enumerate((far, up, down))
    ]
    arrived([dwq_swap])
    dwq_half[...] = (dwq[rows_at(core * count, count), :].astype(F32) + dwq_got[...].astype(F32)).astype(BF)
    wide, narrow = count // 8, count // 32
    ways = (("z", "x", 0), ("x", "z", count // 2))
    dwq_first = [
        scatter(one, lambda t, base=base: dwq_half.at[rows_at(base + t * wide, wide)], dwq_got1.at[j])
        for j, (one, two, base) in enumerate(ways)
    ]
    load["m"].wait()
    for copy in m_near:
        copy.wait_recv()
    five.wait_recv()
    six.wait_recv()
    for i in range(4):
        piece = pl.ds(i * 64, 64)
        pair = [
            m_own[j, piece, :].astype(F32) + m_got[j, piece, :].astype(F32) + near[piece, :].astype(F32)
            for j, near in enumerate((m_near_down, m_near_up))
        ]
        m_outgoing[pl.ds(i * 128, 128), :] = merge_experts(*pair)
    mine = m_landed.at[rows_at(e * 16, 16)]
    m_back = []
    for step in plane_steps((2, 1, 3, 0)):
        t = exp_of(e, *step)
        m_back.append(links.remote(m_outgoing.at[rows_at(t * 16, 16)], mine, (t, h)))
    m_kept = links.local(m_outgoing.at[rows_at(e * 16, 16)], mine)
    dwq_second = []
    for j, (one, two, base) in enumerate(ways):
        arrived(dwq_first[j])
        dwq_mid[j] = total(dwq_half[rows_at(base + position(one) * wide, wide), :], dwq_got1.at[j])
        dwq_second.append(scatter(two, lambda t, j=j: dwq_mid.at[j, rows_at(t * narrow, narrow)], dwq_got2.at[j]))
    arrived(dwo_cross)
    dwo_at = rows_at(x_at * 64 + z * 16, 16)
    dwo_ref[dwo_at, own] = total(dwo_sum[h], dwo_hid)
    dwo_third = share("z", dwo_ref.at[dwo_at, own])
    reduced = reduce_middle(links, begun, term, t_got, half_up, half_down, t_pass_up, t_pass_down, e, h)
    ended += reduced
    dwq_third = []
    for j, (one, two, base) in enumerate(ways):
        arrived(dwq_second[j])
        at = rows_at(core * count + base + position(one) * wide + position(two) * narrow, narrow)
        dwq_ref[at, :] = total(dwq_mid[j, rows_at(position(two) * narrow, narrow), :], dwq_got2.at[j])
        dwq_third.append(share(two, dwq_ref.at[at]))
    arrived(dwo_third)
    dwo_fourth = share("x", dwo_ref.at[rows_at(x_at * 64, 64), own])
    dwq_fourth = []
    for j, (one, two, base) in enumerate(ways):
        arrived(dwq_third[j])
        dwq_fourth.append(share(one, dwq_ref.at[rows_at(core * count + base + position(one) * wide, wide)]))
    load["x"].wait()
    grad = reduce_end(reduced, term, t_got, h)
    hat, scale = norm_parts(x[...].astype(F32))
    ginput_ref[...] = gres[...] + norm_back(grad, hat, scale, gain1_ref[...])
    put_vector(vec, 0, jnp.sum(grad * hat, axis=0, keepdims=True))
    put_vector(vec, 1, jnp.sum(grad, axis=0, keepdims=True))
    rounds = (
        [(exp_of(e, dz, 0, 0), hid_of(h, dy)) for dz in range(4) for dy in range(4) if (dz, dy) != (0, 0)],
        [(exp_of(e, 0, dx, dc), h) for dx in range(4) for dc in (0, 1) if (dx, dc) != (0, 0)],
    )
    first_round = [links.remote(vec.at[0], vec_got.at[i], peer) for i, peer in enumerate(rounds[0])]
    for j in range(len(ways)):
        arrived(dwq_fourth[j])
    dwq_twin = dwq_ref.at[rows_at(core * count, count)]
    twins = [links.remote(dwq_twin, dwq_twin, twin)]
    arrived(dwo_fourth)
    dwo_twin = dwo_ref.at[:, own]
    twins.append(links.remote(dwo_twin, dwo_twin, twin))
    arrived(first_round)
    whole = vec[0]
    for i in range(len(rounds[0])):
        whole = whole + vec_got[i]
    vec[1] = whole
    second_round = [
        links.remote(vec.at[1], vec_got.at[len(rounds[0]) + i], peer) for i, peer in enumerate(rounds[1])
    ]
    m_kept.wait()
    arrived(m_back)
    out_ref[...] = (residual[...] + dot_tn(pick[...], m_landed[...])).astype(BF)
    arrived(second_round)
    whole = vec[1]
    for i in range(len(rounds[1])):
        whole = whole + vec_got[len(rounds[0]) + i]
    vecsum_ref[...] = whole
    arrived(twins)
    for copy in ended:
        copy.wait_send()


def back_call(up_parts, gain1, gain2, logs, pick, residual, out_grad, block_input, wall, w_qkv, joined, q, k, v, hall, down_parts):
    rows, width = q.shape
    block = pltpu.VMEM((ROWS, WIDTH), BF)
    half = pltpu.VMEM((ROWS // 2, WIDTH), BF)
    pair = pltpu.VMEM((2, ROWS, WIDTH), BF)
    slots = pltpu.VMEM((SLOTS, WIDTH), BF)
    held = pltpu.VMEM((rows, width), BF)
    wide = pltpu.VMEM((rows, WIDTH), BF)
    shares = pltpu.VMEM((N_HID, ROWS, WIDTH), BF)
    half_shares = pltpu.VMEM((N_HID, ROWS, WIDTH // 2), BF)
    quarter = pltpu.VMEM((3 * WIDTH // 2, width), BF)
    return pl.pallas_call(
        back_kernel,
        out_shape=(
            jax.ShapeDtypeStruct((ROWS, WIDTH), BF),
            jax.ShapeDtypeStruct((ROWS, WIDTH), F32),
            jax.ShapeDtypeStruct((3 * WIDTH, width), BF),
            jax.ShapeDtypeStruct((ROWS, WIDTH), BF),
            jax.ShapeDtypeStruct((8, WIDTH // 2), F32),
        ),
        in_specs=[VMEM] * 7 + [ANY] * 19,
        out_specs=[VMEM] * 5,
        scratch_shapes=[
            block, block, pair, pltpu.VMEM((SLOTS, ROWS), BF), pltpu.VMEM((ROWS, WIDTH), F32),
            block, block, shares, pltpu.VMEM(w_qkv.shape, BF), wide, held, held, held,
            pltpu.VMEM((N_HID, ROWS, width), BF), pair, block, block,
            block, block, pair, slots, slots, pltpu.VMEM((ROWS, WIDTH), F32), block,
            pltpu.VMEM((3, ROWS, width), BF), held,
            shares, half_shares, half_shares, pltpu.VMEM((3, N_HID, 64, WIDTH // 2), BF), pltpu.VMEM((N_HID, 64, WIDTH // 2), BF),
            pltpu.VMEM((3, N_HID, 16, WIDTH // 2), BF), pltpu.VMEM((N_HID, 16, WIDTH // 2), BF), pltpu.VMEM((3, 16, WIDTH // 2), BF),
            block, block, block, block, pair, slots, slots,
            held, pltpu.VMEM((rows, width), F32), pltpu.VMEM((rows, width), F32),
            wide, pair, half, half, half, half,
            pltpu.VMEM((3 * WIDTH, width), BF), quarter, quarter, pltpu.VMEM((2, 3, 192, width), BF),
            pltpu.VMEM((2, 192, width), BF), pltpu.VMEM((2, 3, 48, width), BF),
            pltpu.VMEM((2, 8, WIDTH // 2), F32), pltpu.VMEM((22, 8, WIDTH // 2), F32),
        ]
        + sems(17 + 8 + 32 + 3 + 4 + 2 + 1 + 15 + 6 + 1 + 24 + 32 + 22 + 2),
        compiler_params=pltpu.CompilerParams(
            collective_id=2, has_side_effects=True, vmem_limit_bytes=62 * MIB
        ),
        cost_estimate=pl.CostEstimate(flops=12 * 10**9, bytes_accessed=100 * MIB, transcendentals=0),
        name="back",
    )(*up_parts[1:5], gain1, gain2, logs, *up_parts[5:], up_parts[0], pick, residual, out_grad, block_input, wall, w_qkv, joined, q, k, v, hall, *down_parts)


def finish_kernel(out_ref, ginput_ref, dwq_ref, dwo_ref, vec_ref, out, ginput, dwq, dwo, *vectors):
    out[...] = out_ref[...]
    ginput[...] = ginput_ref[...]
    dwq[...] = dwq_ref[...].astype(F32)
    dwo[...] = dwo_ref[...].astype(F32)
    for i, ref in enumerate(vectors):
        ref[:, : WIDTH // 2] = vec_ref[2 * i : 2 * i + 1, :]
        ref[:, WIDTH // 2 :] = vec_ref[2 * i + 1 : 2 * i + 2, :]


def finish_call(out, ginput, dwq, dwo, vec):
    def rows_of(array, parts):
        return pl.BlockSpec((array.shape[0] // parts, array.shape[1]), lambda i: (i, 0))

    blocks = [rows_of(array, 4) for array in (out, ginput, dwq, dwo)]
    fixed = pl.BlockSpec((8, WIDTH // 2), lambda i: (0, 0))
    vector = pl.BlockSpec((1, WIDTH), lambda i: (0, 0))
    return pl.pallas_call(
        finish_kernel,
        grid=(4,),
        out_shape=(
            jax.ShapeDtypeStruct(out.shape, BF), jax.ShapeDtypeStruct(ginput.shape, F32),
            jax.ShapeDtypeStruct(dwq.shape, F32), jax.ShapeDtypeStruct(dwo.shape, F32),
        ) + (jax.ShapeDtypeStruct((1, WIDTH), F32),) * 4,
        in_specs=blocks + [fixed],
        out_specs=blocks + [vector] * 4,
        compiler_params=pltpu.CompilerParams(vmem_limit_bytes=60 * MIB),
        cost_estimate=pl.CostEstimate(flops=0, bytes_accessed=9 * MIB, transcendentals=0),
        name="results",
    )(out, ginput, dwq, dwo, vec)


def hid_shift(rows, step):
    return lax.ppermute(rows, "hid", [(i, (i + step) % N_HID) for i in range(N_HID)])


def after(arrays, *first):
    return lax.optimization_barrier((arrays, first))[0]


def on_device(
    block_input, norm1_gain, norm1_bias, w_qkv, w_out, norm2_gain, norm2_bias,
    w_in, w_down, expert_ids, out_grad,
):
    gain1, bias1, gain2, bias2 = (
        v.reshape(1, WIDTH) for v in (norm1_gain, norm1_bias, norm2_gain, norm2_bias)
    )
    (
        joined, q, k, v, hall, wall, logs, residual, pick,
        rows, grads, act, grad_pre, up_own, up_low, up_high, go_up, go_down, near_below, near_above, *down_parts,
    ) = front_call(
        block_input, gain1, bias1, gain2, bias2, expert_ids.reshape(1, ROWS), out_grad, w_qkv, w_out, w_in, w_down
    )
    below, above = hid_shift(go_up, 1), hid_shift(go_down, -1)
    d_w_in, d_w_down = weights_call(rows, grad_pre, act, grads)
    below, above = after((below, above), d_w_in, d_w_down)
    output, grad_input, dw_qkv, dw_out, vec_sum = back_call(
        (up_own, up_low, up_high, below, above, near_below, near_above), gain1, gain2, logs, pick, residual, out_grad, block_input,
        wall, w_qkv, joined, q, k, v, hall, down_parts,
    )
    output, grad_input, d_w_qkv, d_w_out, *vectors = finish_call(output, grad_input, dw_qkv, dw_out, vec_sum)
    d_gain1, d_bias1, d_gain2, d_bias2 = (v.reshape(WIDTH) for v in vectors)
    return (
        output, grad_input, d_gain1, d_bias1, d_w_qkv.reshape(w_qkv.shape), d_w_out,
        d_gain2, d_bias2, d_w_in, d_w_down,
    )


def solution(mesh):
    in_specs = (
        P(("exp", "hid"), None), P(), P(), P(None, None, "hid"), P("hid", None), P(), P(),
        P("exp", None, "hid"), P("exp", "hid", None), P(("exp", "hid"), None), P(("exp", "hid"), None),
    )
    out_specs = (
        P(("exp", "hid"), None), P(("exp", "hid"), None), P(), P(), P(None, None, "hid"), P("hid", None),
        P(), P(), P("exp", None, "hid"), P("exp", "hid", None),
    )
    return jax.shard_map(on_device, mesh=mesh, in_specs=in_specs, out_specs=out_specs, check_vma=False)
```
